128 devices in a mesh: row: 16 (over x, y_hi, core), col: 8 (over z, y_lo).
Axes of the slice: x: 4, y: 4 (y_hi: 2, y_lo: 2; y = y_hi * 2 + y_lo), z: 4, core: 2. Of those that a mesh axis runs over, the one named last changes fastest.
Arguments:
- features: bfloat16 [131072, 128], P(('row', 'col')), may hold values from -6 to 6
- weight: bfloat16 [128, 128], replicated, may hold values from -0.5 to 0.5
- layer_bias: float32 [128], replicated, may hold values from -3 to 3
- cotangent: bfloat16 [131072, 128], P(('col', 'row')), may hold values from -6 to 6
- tile_out: int32 [16, 8, 128], P('row', 'col'), may hold values from 0 to 63
- tile_in: int32 [16, 8, 128], P('row', 'col'), may hold values from 0 to 31
- tile_vals: bfloat16 [16, 8, 128, 256, 256], P('row', 'col'), may hold values from -0.09375 to 0.09375
- tile_count: int32 [16, 8], P('row', 'col'), may hold values from 1 to 128, as said below
Outputs:
- hidden_out: bfloat16 [131072, 128], P(('col', 'row'))
- feature_grad: bfloat16 [131072, 128], P(('row', 'col'))
- weight_grad: float32 [128, 128], replicated
- bias_grad: float32 [128], replicated
The draws below stay inside these ranges and needn't reach their ends.
Inputs may be any that keep to these rules, and one draw needn't show every extreme that they name: `tile_count`: live slots of each grid block; some grid block has exactly 128 in every draw.
All inputs are finite; a program needn't handle non-finite values.
Results may differ from the reference program's by a relative error of at most 0.025.
Values may be sent and summed in bfloat16 or wider, within the bound.
No kernel may reach another device: no remote copies, remote signals or barrier semaphores. Data moves between devices by JAX's collectives and lax.ppermute only.
A program may use at most 192 MiB of HBM per device.

```python
import math
import jax
import jax.numpy as jnp
from jax import lax

F = 128
TILE = 256
NODE_DEV = 1024
TMAX = 128
OUT_TILES = 64
IN_TILES = 32
NODES = 131072
N_ROW = 16
N_COL = 8


def draw_tile_count(key, part):
    first_key = jax.random.fold_in(key, 11)
    second_key = jax.random.fold_in(key, 23)
    lowest = max(1, TMAX // 8)
    levels = jax.random.randint(first_key, (N_ROW, N_COL), 0, 64, dtype=jnp.int32)
    counts = lowest + (TMAX - lowest) * levels * levels // 3969
    position = jax.random.randint(second_key, (), 0, N_ROW * N_COL, dtype=jnp.int32)
    counts = counts.reshape(-1).at[position].set(TMAX)
    return counts.reshape(N_ROW, N_COL).astype(jnp.int32)


def set_ends(entries, rng, smallest, high):
    index_at = [jax.random.randint(jax.random.fold_in(rng, axis), (), 0, length) for axis, length in enumerate(entries.shape)]
    longest = entries.shape.index(max(entries.shape))
    next_to = index_at[:longest] + [(index_at[longest] + 1) % entries.shape[longest]] + index_at[longest + 1:]
    return entries.at[tuple(index_at)].set(smallest).at[tuple(next_to)].set(high)


def level_of(stream_key, dims, shards, low, high):
    def one(axis_at, blocks):
        heights = jax.random.uniform(jax.random.fold_in(jax.random.fold_in(stream_key, 6), axis_at), (blocks,), jnp.float32, low / len(shards), high / len(shards))
        return jnp.repeat(jnp.exp(heights), dims[axis_at] // blocks).reshape((-1,) + (1,) * (len(dims) - axis_at - 1))

    loudness = one(*shards[0])
    for cut in shards[1:]:
        loudness = loudness * one(*cut)
    return loudness


def noise(rng, dims, scale, most, shards=(), kind=jnp.bfloat16):
    array = jax.random.normal(rng, dims, jnp.float32) * scale
    if len(shards) > 0:
        array = level_of(rng, dims, shards, -0.22, 0.18) * array
    return jnp.clip(array, min=-most, max=most).astype(kind)


def setup_inputs(seed: int = 0) -> dict:
    streams_of = jax.random.split(jax.random.key(seed), 9)
    features = noise(streams_of[0], (NODES, F), 1.0, 6.0, ((0, 128),))
    weight = noise(streams_of[1], (F, F), F ** -0.5, 0.5)
    layer_bias = noise(streams_of[2], (F,), 0.5, 3.0, (), jnp.float32)
    cotangent = noise(streams_of[3], (NODES, F), 1.0, 6.0, ((0, 128),))
    tile_out = set_ends(jax.random.randint(streams_of[4], (N_ROW, N_COL, TMAX), 0, OUT_TILES), jax.random.fold_in(streams_of[4], 1), 0, OUT_TILES - 1).astype(jnp.int32)
    tile_in = set_ends(jax.random.randint(streams_of[5], (N_ROW, N_COL, TMAX), 0, IN_TILES), jax.random.fold_in(streams_of[5], 1), 0, IN_TILES - 1).astype(jnp.int32)
    tile_vals = noise(streams_of[6], (N_ROW, N_COL, TMAX, TILE, TILE), (TMAX * TILE * TILE // (2 * NODE_DEV)) ** -0.5, 0.09375, ((0, 16), (1, 8)))
    tile_count = draw_tile_count(jax.random.fold_in(streams_of[8], 71), 0)
    return dict(features=features, weight=weight, layer_bias=layer_bias, cotangent=cotangent, tile_out=tile_out, tile_in=tile_in, tile_vals=tile_vals, tile_count=tile_count)


gelu_coef = 0.7978845608
cube_coef = 0.044715

def gelu_tanh(inputs):
    inner = jnp.tanh(gelu_coef * (inputs + cube_coef * inputs * inputs * inputs))
    return 0.5 * inputs * (1.0 + inner)

def gelu_slope(inputs):
    inner = jnp.tanh(gelu_coef * (inputs + cube_coef * inputs * inputs * inputs))
    return 0.5 * (1.0 + inner) + 0.5 * inputs * (1.0 - inner * inner) * gelu_coef * (1.0 + 3.0 * cube_coef * inputs * inputs)

def rounded(values):
    return lax.optimization_barrier(values.astype(jnp.bfloat16)).astype(jnp.float32)

def reference(features, weight, layer_bias, cotangent, tile_out, tile_in, tile_vals, tile_count):
    slots = jnp.arange(TMAX, dtype=jnp.int32)

    def forward_part(row_idx, col_idx):
        live_mask = (slots < tile_count[row_idx, col_idx]).astype(jnp.float32)
        start = (row_idx * (N_COL * NODE_DEV)).astype(jnp.int32)
        source = lax.dynamic_slice_in_dim(features, start, N_COL * NODE_DEV, 0).astype(jnp.float32)
        source = source.reshape(IN_TILES, TILE, F)
        picked = source[tile_in[row_idx, col_idx]]
        products = jnp.einsum('tab,tbf->taf', tile_vals[row_idx, col_idx].astype(jnp.float32), picked)
        products = products * live_mask[:, None, None]
        target = jnp.zeros((OUT_TILES, TILE, F), jnp.float32).at[tile_out[row_idx, col_idx]].add(products)
        return rounded(target.reshape(OUT_TILES * TILE, F))

    def forward_block(col_idx):

        def step_row(carry, row_idx):
            return (carry + forward_part(row_idx, col_idx), None)
        total, unused = lax.scan(step_row, jnp.zeros((OUT_TILES * TILE, F), jnp.float32), jnp.arange(N_ROW, dtype=jnp.int32))
        return total
    aggregated = lax.map(forward_block, jnp.arange(N_COL, dtype=jnp.int32)).reshape(NODES, F).astype(jnp.bfloat16)
    preact = jnp.dot(aggregated, weight, preferred_element_type=jnp.float32) + layer_bias.astype(jnp.float32)
    hidden_out = gelu_tanh(preact).astype(jnp.bfloat16)
    grad_pre = (cotangent.astype(jnp.float32) * gelu_slope(preact)).astype(jnp.bfloat16)
    norm_scale = 1.0 / math.sqrt(NODES)
    weight_grad = lax.dot_general(aggregated, grad_pre, (((0,), (0,)), ((), ())), preferred_element_type=jnp.float32) * norm_scale
    bias_grad = lax.optimization_barrier(jnp.sum(grad_pre.astype(jnp.float32), axis=0)) * norm_scale
    grad_agg = jnp.dot(grad_pre, weight.T, preferred_element_type=jnp.float32).astype(jnp.bfloat16)

    def backward_part(row_idx, col_idx):
        live_mask = (slots < tile_count[row_idx, col_idx]).astype(jnp.float32)
        start = (col_idx * (N_ROW * NODE_DEV)).astype(jnp.int32)
        target = lax.dynamic_slice_in_dim(grad_agg, start, N_ROW * NODE_DEV, 0).astype(jnp.float32)
        target = target.reshape(OUT_TILES, TILE, F)
        picked = target[tile_out[row_idx, col_idx]]
        products = jnp.einsum('tab,taf->tbf', tile_vals[row_idx, col_idx].astype(jnp.float32), picked)
        products = products * live_mask[:, None, None]
        source = jnp.zeros((IN_TILES, TILE, F), jnp.float32).at[tile_in[row_idx, col_idx]].add(products)
        return rounded(source.reshape(IN_TILES * TILE, F))

    def backward_block(row_idx):

        def step_col(carry, col_idx):
            return (carry + backward_part(row_idx, col_idx), None)
        total, unused = lax.scan(step_col, jnp.zeros((IN_TILES * TILE, F), jnp.float32), jnp.arange(N_COL, dtype=jnp.int32))
        return total
    feature_grad = lax.map(backward_block, jnp.arange(N_ROW, dtype=jnp.int32)).reshape(NODES, F).astype(jnp.bfloat16)
    return (hidden_out, feature_grad, weight_grad, bias_grad)
```

```python
import functools
import math

import jax
import jax.numpy as jnp
from jax import lax
from jax.experimental import pallas as pl
from jax.experimental.pallas import tpu as pltpu
from jax.sharding import PartitionSpec as P

gelu_coef = 0.7978845608
cube_coef = 0.044715
TILE = 256
FEAT = 128
SLOTS = 128
NPEER = 8
LIST = 160
UNROLL = 4
DEPTH = 16
EXTRA = 32
FWD_DUMMY = 32
BWD_DUMMY = 16
f32, bf16 = jnp.float32, jnp.bfloat16
VMEM_LIMIT = 48 * 2**20


def params():
    return pltpu.CompilerParams(vmem_limit_bytes=VMEM_LIMIT)


def vmem():
    return pl.BlockSpec(memory_space=pltpu.VMEM)


def smem():
    return pl.BlockSpec(memory_space=pltpu.SMEM)


def hbm():
    return pl.BlockSpec(memory_space=pl.ANY)


def prep_kernel(where_ref, out_ref, in_ref, count_ref, lists_ref, sizes_ref):
    core, z, y = where_ref[0], where_ref[1], where_ref[2]

    def clear(i, carry):
        lists_ref[i] = FWD_DUMMY << 16
        lists_ref[LIST + i] = FWD_DUMMY << 16
        lists_ref[2 * LIST + i] = BWD_DUMMY << 16
        lists_ref[3 * LIST + i] = BWD_DUMMY << 16
        return carry

    lax.fori_loop(0, LIST, clear, 0)

    def place(k, carry):
        f0, f1, b0, b1 = carry
        t = out_ref[k]
        s = in_ref[k]
        dev_t = t >> 2
        rel = jnp.bitwise_xor(dev_t & 1, core)
        j_t = dev_t >> 1
        half_t, sub_t = (t >> 1) & 1, t & 1
        dev_s = s >> 2
        half_s, sub_s = (s >> 1) & 1, s & 1
        dz = (z - (dev_s >> 1)) & 3
        dy = (y - (dev_s & 1)) & 1
        src_f = (dz * 2 + dy) * 4 + (s & 3)
        dst_f = rel * 16 + j_t * 2 + sub_t
        src_b = ((half_t * 2 + rel) * NPEER + j_t) * 2 + sub_t
        dst_b = dev_s * 2 + sub_s
        at_f = jnp.where(half_t == 0, f0, LIST + f1)
        at_b = jnp.where(half_s == 0, 2 * LIST + b0, 3 * LIST + b1)
        lists_ref[at_f] = k | (src_f << 8) | (dst_f << 16)
        lists_ref[at_b] = k | (src_b << 8) | (dst_b << 16)
        return (
            f0 + 1 - half_t,
            f1 + half_t,
            b0 + 1 - half_s,
            b1 + half_s,
        )

    zero = jnp.int32(0)
    sizes = lax.fori_loop(0, count_ref[0], place, (zero, zero, zero, zero))
    for i in range(4):
        sizes_ref[i] = sizes[i]


def prep(where, out_index, in_index, count):
    return pl.pallas_call(
        prep_kernel,
        out_shape=(
            jax.ShapeDtypeStruct((4 * LIST,), jnp.int32),
            jax.ShapeDtypeStruct((4,), jnp.int32),
        ),
        in_specs=[smem()] * 4,
        out_specs=(smem(), smem()),
        name="slot_lists",
    )(where, out_index, in_index, count)


def tile_loop(which, lists_ref, sizes_ref, vals, buf, sems, ready, step):
    base = which * LIST
    groups = (sizes_ref[which] + (UNROLL - 1)) // UNROLL
    ahead = DEPTH // UNROLL

    def copy(g, u):
        slot = lists_ref[base + g * UNROLL + u] & 255
        at = lax.rem(g, ahead) * UNROLL + u
        return pltpu.make_async_copy(vals.at[slot], buf.at[at], sems.at[at])

    for g in range(ahead):

        @pl.when(g < groups)
        def _():
            for u in range(UNROLL):
                copy(g, u).start()

    ready()

    def body(g, carry):
        for u in range(UNROLL):
            copy(g, u).wait()
        todo = []
        for u in range(UNROLL):
            entry = lists_ref[base + g * UNROLL + u]
            at = lax.rem(g, ahead) * UNROLL + u
            todo.append(((entry >> 16), step((entry >> 8) & 255, at)))
        yield_to(todo)

        @pl.when(g + ahead < groups)
        def _():
            for u in range(UNROLL):
                copy(g + ahead, u).start()

        return carry

    acc = step.acc

    def yield_to(todo):
        for to, product in todo:
            acc[to] += product

    lax.fori_loop(0, groups, body, 0)


class Step:
    def __init__(self, acc, product):
        self.acc = acc
        self.product = product

    def __call__(self, source, at):
        return self.product(source, at)


def forward_kernel(half, lists_ref, sizes_ref, vals, *rest):
    blocks = rest[:NPEER]
    mine_ref, other_ref, x, buf, acc, sems, xsems = rest[NPEER:]

    def block_copy(k):
        return pltpu.make_async_copy(blocks[k], x.at[pl.ds(k * 4 * TILE, 4 * TILE)], xsems.at[k])

    def ready():
        for k in range(NPEER):
            block_copy(k).start()

        def clear(i, carry):
            acc[i] = jnp.zeros((TILE, FEAT), f32)
            return carry

        lax.fori_loop(0, FWD_DUMMY + 1, clear, 0)
        for k in range(NPEER):
            block_copy(k).wait()

    def product(source, at):
        rows = x[pl.ds(pl.multiple_of(source * TILE, TILE), TILE), :]
        return jnp.dot(buf[at], rows, preferred_element_type=f32)

    tile_loop(half, lists_ref, sizes_ref, vals, buf, sems, ready, Step(acc, product))

    def put(i, carry):
        peer, sub = i // 2, i % 2
        rows = pl.ds(pl.multiple_of(sub * TILE, TILE), TILE)
        mine_ref[peer, rows, :] = acc[i].astype(bf16)
        other_ref[peer, rows, :] = acc[16 + i].astype(bf16)
        return carry

    lax.fori_loop(0, 16, put, 0)


def forward(half, lists, sizes, values, blocks):
    shape = jax.ShapeDtypeStruct((NPEER, 2 * TILE, FEAT), bf16)
    return pl.pallas_call(
        functools.partial(forward_kernel, half),
        out_shape=(shape, shape),
        in_specs=[smem(), smem()] + [hbm()] * (1 + NPEER),
        out_specs=(vmem(), vmem()),
        scratch_shapes=[
            pltpu.VMEM((NPEER * 4 * TILE, FEAT), bf16),
            pltpu.VMEM((DEPTH, TILE, TILE), bf16),
            pltpu.VMEM((FWD_DUMMY + 1, TILE, FEAT), f32),
            pltpu.SemaphoreType.DMA((DEPTH,)),
            pltpu.SemaphoreType.DMA((NPEER,)),
        ],
        compiler_params=params(),
        cost_estimate=pl.CostEstimate(
            flops=2 * 64 * TILE * TILE * FEAT, bytes_accessed=14 * 2**20, transcendentals=0
        ),
        name="forward_tiles",
    )(lists, sizes, values, *blocks)


def split_lanes(value):
    high = value.astype(bf16)
    low = (value - high.astype(f32)).astype(bf16)
    return jnp.concatenate([high, low], axis=1)


def backward_kernel(half, lists_ref, sizes_ref, vals, *rest):
    parts = rest[:4]
    out_ref, g, buf, acc, sems, gsems = rest[4:10]
    per = 2 * NPEER

    def part_copy(p, peer):
        return pltpu.make_async_copy(
            parts[p].at[peer, pl.ds(0, 2 * FEAT)],
            g.at[pl.ds((p * per + peer * 2) * FEAT, 2 * FEAT)],
            gsems.at[p],
        )

    if half == 0:
        extra, esem = rest[10:12]

        def extra_copy(p):
            return pltpu.make_async_copy(
                parts[2 + p].at[:, pl.ds(2 * FEAT, EXTRA)], extra.at[p], esem.at[p]
            )

    def ready():
        for p in range(4):
            for peer in range(NPEER):
                part_copy(p, peer).start()
        if half == 0:
            extra_copy(0).start()
            extra_copy(1).start()

        def clear(i, carry):
            acc[i] = jnp.zeros((FEAT, TILE), f32)
            return carry

        lax.fori_loop(0, BWD_DUMMY + 1, clear, 0)
        for p in range(4):
            pltpu.make_async_copy(
                g.at[pl.ds(p * per * FEAT, per * FEAT)],
                g.at[pl.ds(p * per * FEAT, per * FEAT)],
                gsems.at[p],
            ).wait()

    def product(source, at):
        rows = g[pl.ds(pl.multiple_of(source * FEAT, FEAT), FEAT), :]
        return jnp.dot(rows, buf[at], preferred_element_type=f32)

    tile_loop(2 + half, lists_ref, sizes_ref, vals, buf, sems, ready, Step(acc, product))

    def put(i, carry):
        peer, sub = i // 2, i % 2
        rows = pl.ds(pl.multiple_of(sub * FEAT, FEAT), FEAT)
        out_ref[peer, rows, :] = acc[i].astype(bf16)
        return carry

    lax.fori_loop(0, 16, put, 0)
    if half == 0:
        extra_copy(0).wait()
        extra_copy(1).wait()
        sums = []
        for p in range(2):
            total = jnp.zeros((EXTRA, FEAT), f32)
            for peer in range(NPEER):
                pair = extra[p, peer].astype(f32)
                total += pair[:, :FEAT] + pair[:, FEAT:]
            sums.append(total)
        packed = split_lanes(sums[0] + sums[1])
        for peer in range(NPEER):
            out_ref[peer, pl.ds(2 * FEAT, EXTRA), :] = packed


def backward(half, lists, sizes, values, parts):
    rows = 2 * FEAT + (EXTRA if half == 0 else 0)
    scratch = [
        pltpu.VMEM((4 * 2 * NPEER * FEAT, TILE), bf16),
        pltpu.VMEM((DEPTH, TILE, TILE), bf16),
        pltpu.VMEM((BWD_DUMMY + 1, FEAT, TILE), f32),
        pltpu.SemaphoreType.DMA((DEPTH,)),
        pltpu.SemaphoreType.DMA((4,)),
    ]
    if half == 0:
        scratch += [
            pltpu.VMEM((2, NPEER, EXTRA, TILE), bf16),
            pltpu.SemaphoreType.DMA((2,)),
        ]
    return pl.pallas_call(
        functools.partial(backward_kernel, half),
        out_shape=jax.ShapeDtypeStruct((NPEER, rows, TILE), bf16),
        in_specs=[smem(), smem()] + [hbm()] * 5,
        out_specs=vmem(),
        scratch_shapes=scratch,
        compiler_params=params(),
        cost_estimate=pl.CostEstimate(
            flops=2 * 64 * TILE * TILE * FEAT, bytes_accessed=14 * 2**20, transcendentals=0
        ),
        name="backward_tiles",
    )(lists, sizes, values, *parts)


def dense_kernel(half, recv_ref, weight_ref, bias_ref, cot_ref, *rest):
    if half == 0:
        hidden_ref, grad_ref, wsum_ref = rest
    else:
        before_ref, unused, hidden_ref, grad_ref = rest
    total = recv_ref[0].astype(f32)
    for peer in range(1, NPEER):
        total += recv_ref[peer].astype(f32)
    agg = total.astype(bf16)
    weight = weight_ref[...]
    v = jnp.dot(agg, weight, preferred_element_type=f32) + bias_ref[...]
    s = jnp.tanh(gelu_coef * (v + cube_coef * v * v * v))
    hidden_ref[...] = (0.5 * v * (1.0 + s)).astype(bf16)
    slope = 0.5 * (1.0 + s) + 0.5 * v * (1.0 - s * s) * gelu_coef * (1.0 + 3.0 * cube_coef * v * v)
    grad = (cot_ref[...].astype(f32) * slope).astype(bf16)
    wsum = lax.dot_general(agg, grad, (((0,), (0,)), ((), ())), preferred_element_type=f32)
    bsum = jnp.dot(jnp.ones((16, 2 * TILE), bf16), grad, preferred_element_type=f32)
    back = lax.dot_general(weight, grad, (((1,), (1,)), ((), ())), preferred_element_type=f32)
    back = back.astype(bf16)
    for peer in range(NPEER):
        for sub in range(2):
            grad_ref[peer, pl.ds(sub * FEAT, FEAT), :] = back[:, sub * TILE : (sub + 1) * TILE]
    if half == 0:
        wsum_ref[pl.ds(0, FEAT), :] = wsum
        wsum_ref[pl.ds(FEAT, 16), :] = bsum
    else:
        wpack = split_lanes(wsum + before_ref[pl.ds(0, FEAT), :])
        bpack = split_lanes(bsum + before_ref[pl.ds(FEAT, 16), :])
        for peer in range(NPEER):
            grad_ref[peer, pl.ds(2 * FEAT, 16), :] = wpack[peer * 16 : peer * 16 + 16]
            grad_ref[peer, pl.ds(2 * FEAT + 16, 16), :] = bpack


def dense(half, recv, weight, bias, cotangent, before=None, hidden=None):
    rows = 2 * FEAT + (EXTRA if half == 1 else 0)
    hidden_shape = jax.ShapeDtypeStruct((4 * TILE, FEAT), bf16)
    half_rows = pl.BlockSpec((2 * TILE, FEAT), lambda i: (half, 0))
    grad_shape = jax.ShapeDtypeStruct((NPEER, rows, TILE), bf16)
    whole3 = pl.BlockSpec((NPEER, rows, TILE), lambda i: (0, 0, 0))
    wsum_shape = jax.ShapeDtypeStruct((FEAT + 16, FEAT), f32)

    def whole(*shape):
        return pl.BlockSpec(shape, lambda i: (0,) * len(shape))

    in_specs = [whole(NPEER, 2 * TILE, FEAT), whole(FEAT, FEAT), whole(1, FEAT), half_rows]
    operands = [recv, weight, bias, cotangent]
    aliases = {}
    if half == 0:
        out_shape = (hidden_shape, grad_shape, wsum_shape)
        out_specs = (half_rows, whole3, whole(FEAT + 16, FEAT))
    else:
        out_shape = (hidden_shape, grad_shape)
        out_specs = (half_rows, whole3)
        in_specs += [whole(FEAT + 16, FEAT), hbm()]
        operands += [before, hidden]
        aliases = {5: 0}
    return pl.pallas_call(
        functools.partial(dense_kernel, half),
        grid=(1,),
        out_shape=out_shape,
        in_specs=in_specs,
        out_specs=out_specs,
        input_output_aliases=aliases,
        compiler_params=params(),
        cost_estimate=pl.CostEstimate(
            flops=6 * 512 * FEAT * FEAT, bytes_accessed=3 * 2**20, transcendentals=512 * FEAT
        ),
        name="dense_layer",
    )(*operands)


def last_kernel(half, scale, recv_ref, *rest):
    if half == 0:
        grad_ref, slice_ref = rest
    else:
        unused, grad_ref = rest
    for sub in range(2):
        rows = pl.ds(sub * FEAT, FEAT)
        total = recv_ref[0, rows, :].astype(f32)
        for peer in range(1, NPEER):
            total += recv_ref[peer, rows, :].astype(f32)
        grad_ref[pl.ds(sub * TILE, TILE), :] = total.T.astype(bf16)
    if half == 0:
        total = jnp.zeros((EXTRA, FEAT), f32)
        for peer in range(NPEER):
            pair = recv_ref[peer, pl.ds(2 * FEAT, EXTRA), :].astype(f32)
            total += pair[:, :FEAT] + pair[:, FEAT:]
        total = total * scale
        for peer in range(NPEER):
            slice_ref[peer] = total


def last(half, scale, recv, grad=None):
    rows = recv.shape[1]
    half_rows = pl.BlockSpec((2 * TILE, FEAT), lambda i: (half, 0))
    grad_shape = jax.ShapeDtypeStruct((4 * TILE, FEAT), bf16)
    in_specs = [pl.BlockSpec((NPEER, rows, TILE), lambda i: (0, 0, 0))]
    operands = [recv]
    aliases = {}
    if half == 0:
        out_shape = (grad_shape, jax.ShapeDtypeStruct((NPEER, EXTRA, FEAT), f32))
        out_specs = (half_rows, pl.BlockSpec((NPEER, EXTRA, FEAT), lambda i: (0, 0, 0)))
    else:
        out_shape = grad_shape
        out_specs = half_rows
        in_specs += [hbm()]
        operands += [grad]
        aliases = {1: 0}
    return pl.pallas_call(
        functools.partial(last_kernel, half, scale),
        grid=(1,),
        out_shape=out_shape,
        in_specs=in_specs,
        out_specs=out_specs,
        input_output_aliases=aliases,
        compiler_params=params(),
        cost_estimate=pl.CostEstimate(flops=2**20, bytes_accessed=2 * 2**20, transcendentals=0),
        name="last_sum",
    )(*operands)


SAME_CORE = [[2 * j + core for j in range(NPEER)] for core in range(2)]
OTHER_CORE = [(r, r ^ 1) for r in range(16)]


def to_other_core(value):
    return lax.ppermute(value, "row", OTHER_CORE)


def row_exchange(value):
    return lax.all_to_all(value, "row", 0, 0, axis_index_groups=SAME_CORE)


def col_exchange(value):
    return lax.all_to_all(value, "col", 0, 0)


def col_shift(value, dz, dy):
    pairs = []
    for c in range(8):
        z, y = c // 2, c % 2
        pairs.append((c, ((z + dz) % 4) * 2 + (y + dy) % 2))
    return lax.ppermute(value, "col", pairs)


def local(features, weight, layer_bias, cotangent, tile_out, tile_in, tile_vals, tile_count):
    values = tile_vals[0, 0]
    row, col = lax.axis_index("row"), lax.axis_index("col")
    where = jnp.stack([row % 2, col // 2, col % 2]).astype(jnp.int32)
    lists, sizes = prep(where, tile_out[0, 0], tile_in[0, 0], tile_count[0])
    bias = layer_bias.reshape(1, FEAT)

    blocks = [features]
    for k in range(1, NPEER):
        blocks.append(col_shift(features, k // 2, k % 2))

    received = []
    for half in range(2):
        mine, other = forward(half, lists, sizes, values, blocks)
        both = mine + to_other_core(other)
        received.append(row_exchange(both))

    hidden, grad0, wsum = dense(0, received[0], weight, bias, cotangent)
    grads0 = row_exchange(grad0)
    hidden, grad1 = dense(1, received[1], weight, bias, cotangent, wsum, hidden)
    grads1 = row_exchange(grad1)
    parts = [grads0, to_other_core(grads0), grads1, to_other_core(grads1)]

    back0 = col_exchange(backward(0, lists, sizes, values, parts))
    back1 = col_exchange(backward(1, lists, sizes, values, parts))
    scale = 1.0 / math.sqrt(4 * TILE * 128)
    feature_grad, wslice = last(0, scale, back0)
    slices = row_exchange(wslice)
    feature_grad = last(1, scale, back1, feature_grad)
    weight_grad = slices[:, :16].reshape(FEAT, FEAT)
    bias_grad = slices[0, 16]
    return (hidden, feature_grad, weight_grad, bias_grad)


def solution(mesh):
    in_specs = (
        P(("row", "col"), None),
        P(),
        P(),
        P(("col", "row"), None),
        P("row", "col", None),
        P("row", "col", None),
        P("row", "col", None, None, None),
        P("row", "col"),
    )
    out_specs = (P(("col", "row"), None), P(("row", "col"), None), P(), P())
    return jax.shard_map(local, mesh=mesh, in_specs=in_specs, out_specs=out_specs, check_vma=False)
```

```python
import functools
import math

import jax
import jax.numpy as jnp
from jax import lax
from jax.experimental import pallas as pl
from jax.experimental.pallas import tpu as pltpu
from jax.sharding import PartitionSpec as P

gelu_coef = 0.7978845608
cube_coef = 0.044715
TILE = 256
FEAT = 128
SLOTS = 128
NPEER = 8
LIST = 160
UNROLL = 8
DEPTH = 32
EXTRA = 32
FWD_DUMMY = 32
BWD_DUMMY = 16
f32, bf16 = jnp.float32, jnp.bfloat16
VMEM_LIMIT = 28 * 2**20


def params():
    return pltpu.CompilerParams(vmem_limit_bytes=VMEM_LIMIT)


def vmem():
    return pl.BlockSpec(memory_space=pltpu.VMEM)


def smem():
    return pl.BlockSpec(memory_space=pltpu.SMEM)


def hbm():
    return pl.BlockSpec(memory_space=pl.ANY)


def prep_kernel(where_ref, out_ref, in_ref, count_ref, lists_ref, sizes_ref):
    x, yh, core, z, y = (where_ref[i] for i in range(5))

    def clear(i, carry):
        lists_ref[i] = FWD_DUMMY << 16
        lists_ref[LIST + i] = FWD_DUMMY << 16
        lists_ref[2 * LIST + i] = BWD_DUMMY << 16
        lists_ref[3 * LIST + i] = BWD_DUMMY << 16
        return carry

    lax.fori_loop(0, LIST, clear, 0)

    def place(k, carry):
        f0, f1, b0, b1 = carry
        t = out_ref[k]
        s = in_ref[k]
        rel = jnp.bitwise_xor((t >> 2) & 1, core)
        yh_t, x_t = (t >> 3) & 1, t >> 4
        half_t, sub_t = (t >> 1) & 1, t & 1
        y_s, z_s = (s >> 2) & 1, s >> 3
        half_s, sub_s = (s >> 1) & 1, s & 1
        dy_row = (yh_t + yh) & 1
        dy_col = (y_s + y) & 1
        j_t = t >> 3
        src_f = ((((z - z_s) & 3) * 2 + dy_col) << 2) + (s & 3)
        to_t = jnp.where(half_t == 0, j_t, ((x_t - x) & 3) * 2 + dy_row)
        from_t = jnp.where(half_t == 0, ((x - x_t) & 3) * 2 + dy_row, j_t)
        dst_f = rel * 16 + to_t * 2 + sub_t
        src_b = ((half_t * 2 + rel) * NPEER + from_t) * 2 + sub_t
        to_s = jnp.where(half_s == 0, s >> 2, ((z_s - z) & 3) * 2 + dy_col)
        dst_b = to_s * 2 + sub_s
        at_f = jnp.where(half_t == 0, f0, LIST + f1)
        at_b = jnp.where(half_s == 0, 2 * LIST + b0, 3 * LIST + b1)
        lists_ref[at_f] = k | (src_f << 8) | (dst_f << 16)
        lists_ref[at_b] = k | (src_b << 8) | (dst_b << 16)
        return (
            f0 + 1 - half_t,
            f1 + half_t,
            b0 + 1 - half_s,
            b1 + half_s,
        )

    zero = jnp.int32(0)
    sizes = lax.fori_loop(0, count_ref[0], place, (zero, zero, zero, zero))
    for i in range(4):
        sizes_ref[i] = sizes[i]


def prep(where, out_index, in_index, count):
    return pl.pallas_call(
        prep_kernel,
        out_shape=(
            jax.ShapeDtypeStruct((4 * LIST,), jnp.int32),
            jax.ShapeDtypeStruct((4,), jnp.int32),
        ),
        in_specs=[smem()] * 4,
        out_specs=(smem(), smem()),
        name="slot_lists",
    )(where, out_index, in_index, count)


def tile_loop(which, lists_ref, sizes_ref, vals, buf, sems, acc, ready, product):
    base = which * LIST
    groups = (sizes_ref[which] + (UNROLL - 1)) // UNROLL
    ahead = DEPTH // UNROLL

    def copy(g, u):
        slot = lists_ref[base + g * UNROLL + u] & 255
        at = lax.rem(g, ahead) * UNROLL + u
        return pltpu.make_async_copy(vals.at[slot], buf.at[at], sems.at[at])

    for g in range(ahead):

        @pl.when(g < groups)
        def _():
            for u in range(UNROLL):
                copy(g, u).start()

    ready()

    def body(g, carry):
        for u in range(UNROLL):
            copy(g, u).wait()
        todo = []
        for u in range(UNROLL):
            entry = lists_ref[base + g * UNROLL + u]
            at = lax.rem(g, ahead) * UNROLL + u
            todo.append((entry >> 16, product(buf[at], (entry >> 8) & 255)))
        for to, value in todo:
            acc[to] += value

        @pl.when(g + ahead < groups)
        def _():
            for u in range(UNROLL):
                copy(g + ahead, u).start()

        return carry

    lax.fori_loop(0, groups, body, 0)


def in_hbm(array):
    return pltpu.with_memory_space_constraint(array, pltpu.HBM)


TILES_COST = pl.CostEstimate(
    flops=2 * 64 * TILE * TILE * FEAT, bytes_accessed=20 * 2**20, transcendentals=0
)


def forward_kernel(half, lists_ref, sizes_ref, vals, *rest):
    blocks = rest[:NPEER]
    mine_ref, *others = rest[NPEER : NPEER + 3]
    x, buf, acc, sems = rest[NPEER + 3 :]

    def ready():
        def clear(i, carry):
            acc[i] = jnp.zeros((TILE, FEAT), f32)
            return carry

        lax.fori_loop(0, FWD_DUMMY, clear, 0)
        for k in range(NPEER):
            x[pl.ds(k * 4 * TILE, 4 * TILE), :] = blocks[k][...]

    def product(tile, source):
        rows = x[pl.ds(pl.multiple_of(source * TILE, TILE), TILE), :]
        return jnp.dot(tile, rows, preferred_element_type=f32)

    tile_loop(half, lists_ref, sizes_ref, vals, buf, sems, acc, ready, product)

    for i in range(2 * NPEER):
        peer, rows = i // 2, pl.ds((i % 2) * TILE, TILE)
        mine_ref[peer, rows, :] = acc[i].astype(bf16)
        others[peer // 4][peer % 4, rows, :] = acc[16 + i].astype(bf16)


def forward(half, lists, sizes, values, blocks):
    shape = jax.ShapeDtypeStruct((NPEER, 2 * TILE, FEAT), bf16)
    piece = jax.ShapeDtypeStruct((NPEER // 2, 2 * TILE, FEAT), bf16)
    return pl.pallas_call(
        functools.partial(forward_kernel, half),
        out_shape=(shape, piece, piece),
        in_specs=[smem(), smem(), hbm()] + [vmem()] * NPEER,
        out_specs=(vmem(), vmem(), vmem()),
        scratch_shapes=[
            pltpu.VMEM((NPEER * 4 * TILE, FEAT), bf16),
            pltpu.VMEM((DEPTH, TILE, TILE), bf16),
            pltpu.VMEM((FWD_DUMMY + 1, TILE, FEAT), f32),
            pltpu.SemaphoreType.DMA((DEPTH,)),
        ],
        compiler_params=params(),
        cost_estimate=TILES_COST,
        name="forward_tiles",
    )(lists, sizes, in_hbm(values), *blocks)


def pair_sum_kernel(half, mine_ref, low_ref, high_ref, *outs):
    others = [low_ref, high_ref]
    for k in range(NPEER):
        other = others[k // 4][k % 4].astype(f32)
        both = (mine_ref[k].astype(f32) + other).astype(bf16)
        if half == 0:
            outs[0][k] = both
        else:
            outs[k][...] = both


def pair_sum(half, mine, low, high):
    if half == 0:
        out_shape, out_specs = jax.ShapeDtypeStruct(mine.shape, bf16), vmem()
    else:
        out_shape = (jax.ShapeDtypeStruct(mine.shape[1:], bf16),) * NPEER
        out_specs = (vmem(),) * NPEER
    return pl.pallas_call(
        functools.partial(pair_sum_kernel, half),
        out_shape=out_shape,
        in_specs=[vmem()] * 3,
        out_specs=out_specs,
        compiler_params=params(),
        cost_estimate=pl.CostEstimate(flops=2**20, bytes_accessed=3 * 2**20, transcendentals=0),
        name="pair_sum",
    )(mine, low, high)


def split_lanes(value):
    high = value.astype(bf16)
    low = (value - high.astype(f32)).astype(bf16)
    return jnp.concatenate([high, low], axis=1)


def backward_kernel(half, lists_ref, sizes_ref, vals, *rest):
    rows2 = 2 * FEAT
    if half == 0:
        shifted, swapped = rest[: 2 * NPEER], rest[2 * NPEER : 2 * NPEER + 2]
        out_ref, g, buf, acc, sems = rest[2 * NPEER + 2 :]
    else:
        g, *outs = rest[: 1 + NPEER]
        buf, acc, sems = rest[1 + NPEER :]

    def ready():
        def clear(i, carry):
            acc[i] = jnp.zeros((FEAT, TILE), f32)
            return carry

        lax.fori_loop(0, BWD_DUMMY, clear, 0)
        if half == 0:
            for i in range(2 * NPEER):
                g[pl.ds(i * rows2, rows2), :] = shifted[i][...]
            for p in range(2):
                for peer in range(NPEER):
                    i = (2 + p) * NPEER + peer
                    g[pl.ds(i * rows2, rows2), :] = swapped[p][peer, pl.ds(0, rows2), :]

    def product(tile, source):
        rows = g[pl.ds(pl.multiple_of(source * FEAT, FEAT), FEAT), :]
        return jnp.dot(rows, tile, preferred_element_type=f32)

    tile_loop(2 + half, lists_ref, sizes_ref, vals, buf, sems, acc, ready, product)

    for i in range(2 * NPEER):
        rows = pl.ds((i % 2) * FEAT, FEAT)
        if half == 0:
            out_ref[i // 2, rows, :] = acc[i].astype(bf16)
        else:
            outs[i // 2][rows, :] = acc[i].astype(bf16)
    if half == 0:
        sums = []
        for p in range(2):
            total = jnp.zeros((EXTRA, FEAT), f32)
            for peer in range(NPEER):
                pair = swapped[p][peer, pl.ds(rows2, EXTRA), :].astype(f32)
                total += pair[:, :FEAT] + pair[:, FEAT:]
            sums.append(total)
        packed = split_lanes(sums[0] + sums[1])
        for peer in range(NPEER):
            out_ref[peer, pl.ds(rows2, EXTRA), :] = packed


def backward(half, lists, sizes, values, grads):
    if half == 0:
        out_shape = (
            jax.ShapeDtypeStruct((NPEER, 2 * FEAT + EXTRA, TILE), bf16),
            jax.ShapeDtypeStruct((4 * 2 * NPEER * FEAT, TILE), bf16),
        )
    else:
        out_shape = (jax.ShapeDtypeStruct((2 * FEAT, TILE), bf16),) * NPEER
    return pl.pallas_call(
        functools.partial(backward_kernel, half),
        out_shape=out_shape,
        in_specs=[smem(), smem(), hbm()] + [vmem()] * len(grads),
        out_specs=(vmem(),) * len(out_shape),
        scratch_shapes=[
            pltpu.VMEM((DEPTH, TILE, TILE), bf16),
            pltpu.VMEM((BWD_DUMMY + 1, FEAT, TILE), f32),
            pltpu.SemaphoreType.DMA((DEPTH,)),
        ],
        compiler_params=params(),
        cost_estimate=TILES_COST,
        name="backward_tiles",
    )(lists, sizes, in_hbm(values), *grads)


def dense_kernel(half, weight_ref, bias_ref, cot_ref, *rest):
    if half == 0:
        recv_ref, hidden_ref, grad_ref, wsum_ref = rest
        parts = [recv_ref.at[peer] for peer in range(NPEER)]
    else:
        before_ref, unused = rest[:2]
        parts = rest[2 : 2 + NPEER]
        hidden_ref, grad_ref = rest[2 + NPEER :]
    total = parts[0][...].astype(f32)
    for peer in range(1, NPEER):
        total += parts[peer][...].astype(f32)
    agg = total.astype(bf16)
    weight = weight_ref[...]
    v = jnp.dot(agg, weight, preferred_element_type=f32) + bias_ref[...]
    s = jnp.tanh(gelu_coef * (v + cube_coef * v * v * v))
    hidden_ref[...] = (0.5 * v * (1.0 + s)).astype(bf16)
    slope = 0.5 * (1.0 + s) + 0.5 * v * (1.0 - s * s) * gelu_coef * (1.0 + 3.0 * cube_coef * v * v)
    grad = (cot_ref[...].astype(f32) * slope).astype(bf16)
    wsum = lax.dot_general(agg, grad, (((0,), (0,)), ((), ())), preferred_element_type=f32)
    bsum = jnp.dot(jnp.ones((16, 2 * TILE), bf16), grad, preferred_element_type=f32)
    back = lax.dot_general(weight, grad, (((1,), (1,)), ((), ())), preferred_element_type=f32)
    back = back.astype(bf16)
    for sub in range(2):
        rows = pl.ds(sub * FEAT, FEAT)
        if half == 0:
            grad_ref[rows, :] = back[:, sub * TILE : (sub + 1) * TILE]
        else:
            for peer in range(NPEER):
                grad_ref[peer, rows, :] = back[:, sub * TILE : (sub + 1) * TILE]
    if half == 0:
        wsum_ref[pl.ds(0, FEAT), :] = wsum
        wsum_ref[pl.ds(FEAT, 16), :] = bsum
    else:
        wpack = split_lanes(wsum + before_ref[pl.ds(0, FEAT), :])
        bpack = split_lanes(bsum + before_ref[pl.ds(FEAT, 16), :])
        for peer in range(NPEER):
            grad_ref[peer, pl.ds(2 * FEAT, 16), :] = wpack[peer * 16 : peer * 16 + 16]
            grad_ref[peer, pl.ds(2 * FEAT + 16, 16), :] = bpack


def dense(half, recv, weight, bias, cotangent, before=None, hidden=None):
    hidden_shape = jax.ShapeDtypeStruct((4 * TILE, FEAT), bf16)
    half_rows = pl.BlockSpec((2 * TILE, FEAT), lambda i: (half, 0))
    wsum_shape = jax.ShapeDtypeStruct((FEAT + 16, FEAT), f32)

    def whole(*shape):
        return pl.BlockSpec(shape, lambda i: (0,) * len(shape))

    in_specs = [whole(FEAT, FEAT), whole(1, FEAT), half_rows]
    operands = [weight, bias, cotangent]
    aliases = {}
    if half == 0:
        grad = (2 * FEAT, TILE)
        in_specs += [whole(NPEER, 2 * TILE, FEAT)]
        operands += [recv]
        out_shape = (hidden_shape, jax.ShapeDtypeStruct(grad, bf16), wsum_shape)
        out_specs = (half_rows, whole(*grad), whole(FEAT + 16, FEAT))
    else:
        grad = (NPEER, 2 * FEAT + EXTRA, TILE)
        in_specs += [whole(FEAT + 16, FEAT), hbm()] + [whole(2 * TILE, FEAT)] * NPEER
        operands += [before, hidden, *recv]
        out_shape = (hidden_shape, jax.ShapeDtypeStruct(grad, bf16))
        out_specs = (half_rows, whole(*grad))
        aliases = {4: 0}
    return pl.pallas_call(
        functools.partial(dense_kernel, half),
        grid=(1,),
        out_shape=out_shape,
        in_specs=in_specs,
        out_specs=out_specs,
        input_output_aliases=aliases,
        compiler_params=params(),
        cost_estimate=pl.CostEstimate(
            flops=6 * 512 * FEAT * FEAT, bytes_accessed=3 * 2**20, transcendentals=512 * FEAT
        ),
        name="dense_layer",
    )(*operands)


def last_kernel(half, scale, *rest):
    if half == 0:
        recv_ref, grad_ref, slice_ref = rest
        parts = [recv_ref.at[peer] for peer in range(NPEER)]
    else:
        parts = rest[1 : 1 + NPEER]
        grad_ref = rest[1 + NPEER]
    for sub in range(2):
        rows = pl.ds(sub * FEAT, FEAT)
        total = parts[0][rows, :].astype(f32)
        for peer in range(1, NPEER):
            total += parts[peer][rows, :].astype(f32)
        grad_ref[pl.ds(sub * TILE, TILE), :] = total.T.astype(bf16)
    if half == 0:
        total = jnp.zeros((EXTRA, FEAT), f32)
        for peer in range(NPEER):
            pair = recv_ref[peer, pl.ds(2 * FEAT, EXTRA), :].astype(f32)
            total += pair[:, :FEAT] + pair[:, FEAT:]
        total = total * scale
        for peer in range(NPEER):
            slice_ref[peer] = total


def last(half, scale, recv, grad=None):
    half_rows = pl.BlockSpec((2 * TILE, FEAT), lambda i: (half, 0))
    grad_shape = jax.ShapeDtypeStruct((4 * TILE, FEAT), bf16)
    aliases = {}
    if half == 0:
        in_specs = [pl.BlockSpec(recv.shape, lambda i: (0, 0, 0))]
        operands = [recv]
        out_shape = (grad_shape, jax.ShapeDtypeStruct((NPEER, EXTRA, FEAT), f32))
        out_specs = (half_rows, pl.BlockSpec((NPEER, EXTRA, FEAT), lambda i: (0, 0, 0)))
    else:
        in_specs = [hbm()] + [pl.BlockSpec((2 * FEAT, TILE), lambda i: (0, 0))] * NPEER
        operands = [grad, *recv]
        out_shape = grad_shape
        out_specs = half_rows
        aliases = {0: 0}
    return pl.pallas_call(
        functools.partial(last_kernel, half, scale),
        grid=(1,),
        out_shape=out_shape,
        in_specs=in_specs,
        out_specs=out_specs,
        input_output_aliases=aliases,
        compiler_params=params(),
        cost_estimate=pl.CostEstimate(flops=2**20, bytes_accessed=2 * 2**20, transcendentals=0),
        name="last_sum",
    )(*operands)


SAME_CORE = [[2 * j + core for j in range(NPEER)] for core in range(2)]
OTHER_CORE = [(r, r ^ 1) for r in range(16)]


def to_other_core(value):
    return lax.ppermute(value, "row", OTHER_CORE)


def row_exchange(value):
    return lax.all_to_all(value, "row", 0, 0, axis_index_groups=SAME_CORE)


def col_exchange(value):
    return lax.all_to_all(value, "col", 0, 0)


def col_shift(value, k):
    pairs = []
    for c in range(8):
        z, y = c // 2, c % 2
        pairs.append((c, ((z + k // 2) % 4) * 2 + (y + k) % 2))
    return lax.ppermute(value, "col", pairs)


def row_shift(value, k):
    pairs = []
    for r in range(16):
        x, y, core = r // 4, (r // 2) % 2, r % 2
        pairs.append((r, ((x + k // 2) % 4) * 4 + ((y + k) % 2) * 2 + core))
    return lax.ppermute(value, "row", pairs)


def local(features, weight, layer_bias, cotangent, tile_out, tile_in, tile_vals, tile_count):
    values = tile_vals[0, 0]
    row, col = lax.axis_index("row"), lax.axis_index("col")
    where = jnp.stack([row >> 2, (row >> 1) & 1, row & 1, col >> 1, col & 1]).astype(jnp.int32)
    lists, sizes = prep(where, tile_out[0, 0], tile_in[0, 0], tile_count[0])
    bias = layer_bias.reshape(1, FEAT)
    order = lax.optimization_barrier

    blocks = [features] + [col_shift(features, k) for k in range(1, NPEER)]

    mine, low, high = forward(0, lists, sizes, values, blocks)
    both = pair_sum(0, mine, to_other_core(low), to_other_core(high))
    both, lists = order((both, lists))
    swapped = row_exchange(both)
    mine, low, high = forward(1, lists, sizes, values, blocks)
    chunks = pair_sum(1, mine, to_other_core(low), to_other_core(high))
    shifted = [chunks[0]] + [row_shift(chunks[k], k) for k in range(1, NPEER)]

    swapped = order((swapped, *chunks))[0]
    hidden, grad, wsum = dense(0, swapped, weight, bias, cotangent)
    grads = [grad] + [row_shift(grad, k) for k in range(1, NPEER)]
    hidden, grad = dense(1, shifted, weight, bias, cotangent, wsum, hidden)
    grad, *grads = order((grad, *grads))
    swapped = row_exchange(grad)
    grads += [to_other_core(g) for g in grads]
    swapped, *grads = order((swapped, *grads))
    grads += [swapped, to_other_core(swapped)]

    back, grads = backward(0, lists, sizes, values, grads)
    back0 = col_exchange(back)
    chunks = backward(1, lists, sizes, values, [grads])
    back1 = [chunks[0]] + [col_shift(chunks[k], k) for k in range(1, NPEER)]
    scale = 1.0 / math.sqrt(4 * TILE * 128)
    feature_grad, wslice = last(0, scale, back0)
    slices = row_exchange(wslice)
    feature_grad = last(1, scale, back1, feature_grad)
    weight_grad = slices[:, :16].reshape(FEAT, FEAT)
    bias_grad = slices[0, 16]
    return (hidden, feature_grad, weight_grad, bias_grad)


def solution(mesh):
    in_specs = (
        P(("row", "col"), None),
        P(),
        P(),
        P(("col", "row"), None),
        P("row", "col", None),
        P("row", "col", None),
        P("row", "col", None, None, None),
        P("row", "col"),
    )
    out_specs = (P(("col", "row"), None), P(("row", "col"), None), P(), P())
    return jax.shard_map(local, mesh=mesh, in_specs=in_specs, out_specs=out_specs, check_vma=False)
```

```python
import functools
import math

import jax
import jax.numpy as jnp
from jax import lax
from jax.experimental import pallas as pl
from jax.experimental.pallas import tpu as pltpu
from jax.sharding import PartitionSpec as P

gelu_coef = 0.7978845608
cube_coef = 0.044715
TILE = 256
FEAT = 128
SLOTS = 128
NPEER = 8
LIST = 160
UNROLL = 8
DEPTH = 32
EXTRA = 144
FWD_DUMMY = 32
BWD_DUMMY = 16
f32, bf16 = jnp.float32, jnp.bfloat16
VMEM_LIMIT = 28 * 2**20


def params():
    return pltpu.CompilerParams(vmem_limit_bytes=VMEM_LIMIT)


def vmem():
    return pl.BlockSpec(memory_space=pltpu.VMEM)


def smem():
    return pl.BlockSpec(memory_space=pltpu.SMEM)


def hbm():
    return pl.BlockSpec(memory_space=pl.ANY)


def prep_kernel(where_ref, out_ref, in_ref, count_ref, lists_ref):
    x, yh, core, z, y = (where_ref[i] for i in range(5))

    def clear(i, carry):
        lists_ref[i] = FWD_DUMMY << 16
        lists_ref[LIST + i] = FWD_DUMMY << 16
        lists_ref[2 * LIST + i] = BWD_DUMMY << 16
        lists_ref[3 * LIST + i] = BWD_DUMMY << 16
        return carry

    lax.fori_loop(0, LIST, clear, 0)

    def place(k, carry):
        f0, f1, b0, b1 = carry
        t = out_ref[k]
        s = in_ref[k]
        rel = jnp.bitwise_xor((t >> 2) & 1, core)
        yh_t, x_t = (t >> 3) & 1, t >> 4
        half_t, sub_t = (t >> 1) & 1, t & 1
        y_s, z_s = (s >> 2) & 1, s >> 3
        half_s, sub_s = (s >> 1) & 1, s & 1
        dy_row = (yh_t + yh) & 1
        dy_col = (y_s + y) & 1
        j_t = t >> 3
        src_f = ((((z - z_s) & 3) * 2 + dy_col) << 2) + (s & 3)
        to_t = jnp.where(half_t == 0, j_t, ((x_t - x) & 3) * 2 + dy_row)
        from_t = jnp.where(half_t == 0, j_t, ((x - x_t) & 3) * 2 + dy_row)
        dst_f = rel * 16 + to_t * 2 + sub_t
        src_b = ((half_t * 2 + rel) * NPEER + from_t) * 2 + sub_t
        to_s = jnp.where(half_s == 0, s >> 2, ((z_s - z) & 3) * 2 + dy_col)
        dst_b = to_s * 2 + sub_s
        at_f = jnp.where(half_t == 0, f0, LIST + f1)
        at_b = jnp.where(half_s == 0, 2 * LIST + b0, 3 * LIST + b1)
        lists_ref[at_f] = k | (src_f << 8) | (dst_f << 16)
        lists_ref[at_b] = k | (src_b << 8) | (dst_b << 16)
        return (
            f0 + 1 - half_t,
            f1 + half_t,
            b0 + 1 - half_s,
            b1 + half_s,
        )

    zero = jnp.int32(0)
    sizes = lax.fori_loop(0, count_ref[0], place, (zero, zero, zero, zero))
    for i in range(4):
        lists_ref[4 * LIST + i] = sizes[i]


def prep(where, out_index, in_index, count):
    return pl.pallas_call(
        prep_kernel,
        out_shape=jax.ShapeDtypeStruct((1024,), jnp.int32),
        in_specs=[smem()] * 4,
        out_specs=smem(),
        name="slot_lists",
    )(where, out_index, in_index, count)


def tile_loop(which, lists_ref, vals, buf, sems, acc, ready, product):
    base = which * LIST
    groups = (lists_ref[4 * LIST + which] + (UNROLL - 1)) // UNROLL
    ahead = DEPTH // UNROLL

    def copy(g, u):
        slot = lists_ref[base + g * UNROLL + u] & 255
        at = lax.rem(g, ahead) * UNROLL + u
        return pltpu.make_async_copy(vals.at[slot], buf.at[at], sems.at[at])

    for g in range(ahead):

        @pl.when(g < groups)
        def _():
            for u in range(UNROLL):
                copy(g, u).start()

    ready()

    def body(g, carry):
        for u in range(UNROLL):
            copy(g, u).wait()
        todo = []
        for u in range(UNROLL):
            entry = lists_ref[base + g * UNROLL + u]
            at = lax.rem(g, ahead) * UNROLL + u
            todo.append((entry >> 16, product(buf[at], (entry >> 8) & 255)))
        for to, value in todo:
            acc[to] += value

        @pl.when(g + ahead < groups)
        def _():
            for u in range(UNROLL):
                copy(g + ahead, u).start()

        return carry

    lax.fori_loop(0, groups, body, 0)


def in_hbm(array):
    return pltpu.with_memory_space_constraint(array, pltpu.HBM)


TILES_COST = pl.CostEstimate(
    flops=2 * 64 * TILE * TILE * FEAT, bytes_accessed=20 * 2**20, transcendentals=0
)


def forward_kernel(half, lists_ref, vals, *rest):
    blocks = rest[:NPEER]
    mine_ref, *others = rest[NPEER : NPEER + 3]
    x, buf, acc, sems, own_sem = rest[NPEER + 3 :]
    own = pltpu.make_async_copy(blocks[0], x.at[pl.ds(0, 4 * TILE)], own_sem)
    own.start()

    def ready():
        def clear(i, carry):
            acc[i] = jnp.zeros((TILE, FEAT), f32)
            return carry

        lax.fori_loop(0, FWD_DUMMY, clear, 0)
        for k in range(1, NPEER):
            x[pl.ds(k * 4 * TILE, 4 * TILE), :] = blocks[k][...]
        own.wait()

    def product(tile, source):
        rows = x[pl.ds(pl.multiple_of(source * TILE, TILE), TILE), :]
        return jnp.dot(tile, rows, preferred_element_type=f32)

    tile_loop(half, lists_ref, vals, buf, sems, acc, ready, product)

    for i in range(2 * NPEER):
        peer, rows = i // 2, pl.ds((i % 2) * TILE, TILE)
        mine_ref[peer, rows, :] = acc[i].astype(bf16)
        others[peer // 4][peer % 4, rows, :] = acc[16 + i].astype(bf16)


def forward(half, lists, values, blocks):
    shape = jax.ShapeDtypeStruct((NPEER, 2 * TILE, FEAT), bf16)
    piece = jax.ShapeDtypeStruct((NPEER // 2, 2 * TILE, FEAT), bf16)
    return pl.pallas_call(
        functools.partial(forward_kernel, half),
        out_shape=(shape, piece, piece),
        in_specs=[smem(), hbm(), hbm()] + [vmem()] * (NPEER - 1),
        out_specs=(vmem(), vmem(), vmem()),
        scratch_shapes=[
            pltpu.VMEM((NPEER * 4 * TILE, FEAT), bf16),
            pltpu.VMEM((DEPTH, TILE, TILE), bf16),
            pltpu.VMEM((FWD_DUMMY + 1, TILE, FEAT), f32),
            pltpu.SemaphoreType.DMA((DEPTH,)),
            pltpu.SemaphoreType.DMA,
        ],
        compiler_params=params(),
        cost_estimate=TILES_COST,
        name="forward_tiles",
    )(in_hbm(lists), in_hbm(values), in_hbm(blocks[0]), *blocks[1:])


def pair_sum_kernel(half, mine_ref, low_ref, high_ref, *outs):
    others = [low_ref, high_ref]
    for k in range(NPEER):
        other = others[k // 4][k % 4].astype(f32)
        both = (mine_ref[k].astype(f32) + other).astype(bf16)
        if half == 0:
            outs[0][k] = both
        else:
            outs[k][...] = both


def pair_sum(half, mine, low, high):
    if half == 0:
        out_shape, out_specs = jax.ShapeDtypeStruct(mine.shape, bf16), vmem()
    else:
        out_shape = (jax.ShapeDtypeStruct(mine.shape[1:], bf16),) * NPEER
        out_specs = (vmem(),) * NPEER
    return pl.pallas_call(
        functools.partial(pair_sum_kernel, half),
        out_shape=out_shape,
        in_specs=[vmem()] * 3,
        out_specs=out_specs,
        compiler_params=params(),
        cost_estimate=pl.CostEstimate(flops=2**20, bytes_accessed=3 * 2**20, transcendentals=0),
        name="pair_sum",
    )(mine, low, high)


def split_lanes(value):
    high = value.astype(bf16)
    low = (value - high.astype(f32)).astype(bf16)
    return jnp.concatenate([high, low], axis=1)


def backward_kernel(half, lists_ref, vals, *rest):
    rows2 = 2 * FEAT
    if half == 0:
        swapped, shifted = rest[:2], rest[2 : 2 + 2 * NPEER]
        out_ref, kept, g, buf, acc, sems, g_sem = rest[2 + 2 * NPEER :]
        keep = pltpu.make_async_copy(g, kept, g_sem)
    else:
        kept, *outs = rest[: 1 + NPEER]
        g, buf, acc, sems, g_sem = rest[1 + NPEER :]
        keep = pltpu.make_async_copy(kept, g, g_sem)
        keep.start()

    def ready():
        def clear(i, carry):
            acc[i] = jnp.zeros((FEAT, TILE), f32)
            return carry

        lax.fori_loop(0, BWD_DUMMY, clear, 0)
        if half == 0:
            for p in range(2):
                for peer in range(NPEER):
                    i = p * NPEER + peer
                    g[pl.ds(i * rows2, rows2), :] = swapped[p][peer]
            for i in range(2 * NPEER):
                g[pl.ds((2 * NPEER + i) * rows2, rows2), :] = shifted[i][pl.ds(0, rows2), :]
            keep.start()
        else:
            keep.wait()

    def product(tile, source):
        rows = g[pl.ds(pl.multiple_of(source * FEAT, FEAT), FEAT), :]
        return jnp.dot(rows, tile, preferred_element_type=f32)

    tile_loop(2 + half, lists_ref, vals, buf, sems, acc, ready, product)

    for i in range(2 * NPEER):
        rows = pl.ds((i % 2) * FEAT, FEAT)
        if half == 0:
            out_ref[i // 2, rows, :] = acc[i].astype(bf16)
        else:
            outs[i // 2][rows, :] = acc[i].astype(bf16)
    if half == 0:
        total = None
        for k in range(NPEER):
            pair = [
                shifted[i][pl.ds(rows2, EXTRA), :].astype(f32) for i in (k, NPEER + k)
            ]
            pair = [v[:, :FEAT] + v[:, FEAT:] for v in pair]
            total = pair[0] + pair[1] if total is None else total + (pair[0] + pair[1])
        packed = split_lanes(total)
        for peer in range(NPEER):
            out_ref[peer, pl.ds(rows2, EXTRA), :] = packed
        keep.wait()


def backward(half, lists, values, grads):
    blocks = pltpu.HBM((4 * 2 * NPEER * FEAT, TILE), bf16)
    if half == 0:
        out_shape = (
            jax.ShapeDtypeStruct((NPEER, 2 * FEAT + EXTRA, TILE), bf16),
            blocks,
        )
        out_specs = (vmem(), pl.BlockSpec(memory_space=pltpu.HBM))
        in_specs = [vmem()] * len(grads)
    else:
        out_shape = (jax.ShapeDtypeStruct((2 * FEAT, TILE), bf16),) * NPEER
        out_specs = (vmem(),) * NPEER
        in_specs = [hbm()]
        grads = [in_hbm(g) for g in grads]
    return pl.pallas_call(
        functools.partial(backward_kernel, half),
        out_shape=out_shape,
        in_specs=[smem(), hbm()] + in_specs,
        out_specs=out_specs,
        scratch_shapes=[
            pltpu.VMEM(blocks.shape, bf16),
            pltpu.VMEM((DEPTH, TILE, TILE), bf16),
            pltpu.VMEM((BWD_DUMMY + 1, FEAT, TILE), f32),
            pltpu.SemaphoreType.DMA((DEPTH,)),
            pltpu.SemaphoreType.DMA,
        ],
        compiler_params=params(),
        cost_estimate=TILES_COST,
        name="backward_tiles",
    )(in_hbm(lists), in_hbm(values), *grads)


def dense_kernel(half, weight_ref, bias_ref, cot_ref, *rest):
    if half == 0:
        recv_ref, hidden_ref, grad_ref, wsum_ref = rest
        parts = [recv_ref.at[peer] for peer in range(NPEER)]
    else:
        before_ref, unused = rest[:2]
        parts = rest[2 : 2 + NPEER]
        hidden_ref, grad_ref = rest[2 + NPEER :]
    total = parts[0][...].astype(f32)
    for peer in range(1, NPEER):
        total += parts[peer][...].astype(f32)
    agg = total.astype(bf16)
    weight = weight_ref[...]
    v = jnp.dot(agg, weight, preferred_element_type=f32) + bias_ref[...]
    s = jnp.tanh(gelu_coef * (v + cube_coef * v * v * v))
    hidden_ref[...] = (0.5 * v * (1.0 + s)).astype(bf16)
    slope = 0.5 * (1.0 + s) + 0.5 * v * (1.0 - s * s) * gelu_coef * (1.0 + 3.0 * cube_coef * v * v)
    grad = (cot_ref[...].astype(f32) * slope).astype(bf16)
    wsum = lax.dot_general(agg, grad, (((0,), (0,)), ((), ())), preferred_element_type=f32)
    bsum = jnp.dot(jnp.ones((16, 2 * TILE), bf16), grad, preferred_element_type=f32)
    back = lax.dot_general(weight, grad, (((1,), (1,)), ((), ())), preferred_element_type=f32)
    back = back.astype(bf16)
    for sub in range(2):
        rows = pl.ds(sub * FEAT, FEAT)
        if half == 0:
            for peer in range(NPEER):
                grad_ref[peer, rows, :] = back[:, sub * TILE : (sub + 1) * TILE]
        else:
            grad_ref[rows, :] = back[:, sub * TILE : (sub + 1) * TILE]
    if half == 0:
        wsum_ref[pl.ds(0, FEAT), :] = wsum
        wsum_ref[pl.ds(FEAT, 16), :] = bsum
    else:
        grad_ref[pl.ds(2 * FEAT, FEAT), :] = split_lanes(wsum + before_ref[pl.ds(0, FEAT), :])
        grad_ref[pl.ds(3 * FEAT, 16), :] = split_lanes(bsum + before_ref[pl.ds(FEAT, 16), :])


def dense(half, recv, weight, bias, cotangent, before=None, hidden=None):
    hidden_shape = jax.ShapeDtypeStruct((4 * TILE, FEAT), bf16)
    half_rows = pl.BlockSpec((2 * TILE, FEAT), lambda i: (half, 0))
    wsum_shape = jax.ShapeDtypeStruct((FEAT + 16, FEAT), f32)

    def whole(*shape):
        return pl.BlockSpec(shape, lambda i: (0,) * len(shape))

    in_specs = [whole(FEAT, FEAT), whole(1, FEAT), half_rows]
    operands = [weight, bias, cotangent]
    aliases = {}
    if half == 0:
        grad = (NPEER, 2 * FEAT, TILE)
        in_specs += [whole(NPEER, 2 * TILE, FEAT)]
        operands += [recv]
        out_shape = (hidden_shape, jax.ShapeDtypeStruct(grad, bf16), wsum_shape)
        out_specs = (half_rows, whole(*grad), whole(FEAT + 16, FEAT))
    else:
        grad = (2 * FEAT + EXTRA, TILE)
        in_specs += [whole(FEAT + 16, FEAT), hbm()] + [whole(2 * TILE, FEAT)] * NPEER
        operands += [before, hidden, *recv]
        out_shape = (hidden_shape, jax.ShapeDtypeStruct(grad, bf16))
        out_specs = (half_rows, whole(*grad))
        aliases = {4: 0}
    return pl.pallas_call(
        functools.partial(dense_kernel, half),
        grid=(1,),
        out_shape=out_shape,
        in_specs=in_specs,
        out_specs=out_specs,
        input_output_aliases=aliases,
        compiler_params=params(),
        cost_estimate=pl.CostEstimate(
            flops=6 * 512 * FEAT * FEAT, bytes_accessed=3 * 2**20, transcendentals=512 * FEAT
        ),
        name="dense_layer",
    )(*operands)


def last_kernel(half, scale, *rest):
    if half == 0:
        recv_ref, grad_ref, weight_ref, bias_ref = rest
        parts = [recv_ref.at[peer] for peer in range(NPEER)]
    else:
        parts = rest[1 : 1 + NPEER]
        grad_ref = rest[1 + NPEER]
    for sub in range(2):
        rows = pl.ds(sub * FEAT, FEAT)
        total = parts[0][rows, :].astype(f32)
        for peer in range(1, NPEER):
            total += parts[peer][rows, :].astype(f32)
        grad_ref[pl.ds(sub * TILE, TILE), :] = total.T.astype(bf16)
    if half == 0:
        total = jnp.zeros((EXTRA, FEAT), f32)
        for peer in range(NPEER):
            pair = recv_ref[peer, pl.ds(2 * FEAT, EXTRA), :].astype(f32)
            total += pair[:, :FEAT] + pair[:, FEAT:]
        total = total * scale
        weight_ref[...] = total[:FEAT]
        bias_ref[...] = total[FEAT : FEAT + 1]


def last(half, scale, recv, grad=None):
    half_rows = pl.BlockSpec((2 * TILE, FEAT), lambda i: (half, 0))
    grad_shape = jax.ShapeDtypeStruct((4 * TILE, FEAT), bf16)
    aliases = {}
    if half == 0:
        in_specs = [pl.BlockSpec(recv.shape, lambda i: (0, 0, 0))]
        operands = [recv]
        sums = [(FEAT, FEAT), (1, FEAT)]
        out_shape = (grad_shape, *[jax.ShapeDtypeStruct(s, f32) for s in sums])
        out_specs = (half_rows, *[pl.BlockSpec(s, lambda i: (0, 0)) for s in sums])
    else:
        in_specs = [hbm()] + [pl.BlockSpec((2 * FEAT, TILE), lambda i: (0, 0))] * NPEER
        operands = [grad, *recv]
        out_shape = grad_shape
        out_specs = half_rows
        aliases = {0: 0}
    return pl.pallas_call(
        functools.partial(last_kernel, half, scale),
        grid=(1,),
        out_shape=out_shape,
        in_specs=in_specs,
        out_specs=out_specs,
        input_output_aliases=aliases,
        compiler_params=params(),
        cost_estimate=pl.CostEstimate(flops=2**20, bytes_accessed=2 * 2**20, transcendentals=0),
        name="last_sum",
    )(*operands)


SAME_CORE = [[2 * j + core for j in range(NPEER)] for core in range(2)]
OTHER_CORE = [(r, r ^ 1) for r in range(16)]


def to_other_core(value):
    return lax.ppermute(value, "row", OTHER_CORE)


def row_exchange(value):
    return lax.all_to_all(value, "row", 0, 0, axis_index_groups=SAME_CORE)


def col_exchange(value):
    return lax.all_to_all(value, "col", 0, 0)


def col_shift(value, k):
    pairs = []
    for c in range(8):
        z, y = c // 2, c % 2
        pairs.append((c, ((z + k // 2) % 4) * 2 + (y + k) % 2))
    return lax.ppermute(value, "col", pairs)


def row_shift(value, k):
    pairs = []
    for r in range(16):
        x, y, core = r // 4, (r // 2) % 2, r % 2
        pairs.append((r, ((x + k // 2) % 4) * 4 + ((y + k) % 2) * 2 + core))
    return lax.ppermute(value, "row", pairs)


def local(features, weight, layer_bias, cotangent, tile_out, tile_in, tile_vals, tile_count):
    values = tile_vals[0, 0]
    row, col = lax.axis_index("row"), lax.axis_index("col")
    where = jnp.stack([row >> 2, (row >> 1) & 1, row & 1, col >> 1, col & 1]).astype(jnp.int32)
    lists = prep(where, tile_out[0, 0], tile_in[0, 0], tile_count[0])
    bias = layer_bias.reshape(1, FEAT)
    order = lax.optimization_barrier

    blocks = [features] + [col_shift(features, k) for k in range(1, NPEER)]

    mine, low, high = forward(0, lists, values, blocks)
    both = pair_sum(0, mine, to_other_core(low), to_other_core(high))
    both, lists = order((both, lists))
    swapped = row_exchange(both)
    mine, low, high = forward(1, lists, values, blocks)
    chunks = pair_sum(1, mine, to_other_core(low), to_other_core(high))
    shifted = [chunks[0]] + [row_shift(chunks[k], k) for k in range(1, NPEER)]

    swapped, *shifted[1:4] = order((swapped, *shifted[1:4]))
    hidden, grad, wsum = dense(0, swapped, weight, bias, cotangent)
    swapped = row_exchange(grad)
    hidden, grad = dense(1, shifted, weight, bias, cotangent, wsum, hidden)
    grads = [grad] + [row_shift(grad, k) for k in range(1, NPEER)]
    swapped, *grads[1:6] = order((swapped, *grads[1:6]))
    grads = [swapped, to_other_core(swapped)] + grads + [to_other_core(g) for g in grads]

    back, grads = backward(0, lists, values, grads)
    back0 = col_exchange(back)
    chunks = backward(1, lists, values, [grads])
    back1 = [chunks[0]] + [col_shift(chunks[k], k) for k in range(1, NPEER)]
    scale = 1.0 / math.sqrt(4 * TILE * 128)
    feature_grad, weight_grad, bias_grad = last(0, scale, back0)
    feature_grad = last(1, scale, back1, feature_grad)
    bias_grad = bias_grad.reshape(FEAT)
    return (hidden, feature_grad, weight_grad, bias_grad)


def solution(mesh):
    in_specs = (
        P(("row", "col"), None),
        P(),
        P(),
        P(("col", "row"), None),
        P("row", "col", None),
        P("row", "col", None),
        P("row", "col", None, None, None),
        P("row", "col"),
    )
    out_specs = (P(("col", "row"), None), P(("row", "col"), None), P(), P())
    return jax.shard_map(local, mesh=mesh, in_specs=in_specs, out_specs=out_specs, check_vma=False)
```

```python
import functools
import math

import jax
import jax.numpy as jnp
from jax import lax
from jax.experimental import pallas as pl
from jax.experimental.pallas import tpu as pltpu
from jax.sharding import PartitionSpec as P

gelu_coef = 0.7978845608
cube_coef = 0.044715
TILE = 256
FEAT = 128
SLOTS = 128
NPEER = 8
LIST = 160
UNROLL = 8
DEPTH = 32
FWD_DUMMY = 32
BWD_DUMMY = 32
f32, bf16 = jnp.float32, jnp.bfloat16
VMEM_LIMIT = 28 * 2**20


def params():
    return pltpu.CompilerParams(vmem_limit_bytes=VMEM_LIMIT)


def vmem():
    return pl.BlockSpec(memory_space=pltpu.VMEM)


def smem():
    return pl.BlockSpec(memory_space=pltpu.SMEM)


def hbm():
    return pl.BlockSpec(memory_space=pl.ANY)


def prep_kernel(where_ref, out_ref, in_ref, count_ref, lists_ref):
    core, z, y = (where_ref[i] for i in range(3))

    def clear(i, carry):
        lists_ref[i] = FWD_DUMMY << 16
        lists_ref[LIST + i] = FWD_DUMMY << 16
        lists_ref[2 * LIST + i] = BWD_DUMMY << 16
        return carry

    lax.fori_loop(0, LIST, clear, 0)

    def place(k, carry):
        f0, f1 = carry
        t = out_ref[k]
        s = in_ref[k]
        rel = jnp.bitwise_xor((t >> 2) & 1, core)
        to_t = ((t >> 3) << 2) | (t & 3)
        dy, dz = ((s >> 2) + y) & 1, (z - (s >> 3)) & 3
        src_f = (((dz << 1) | dy) << 2) | (s & 3)
        at_f = jnp.where(rel == 0, f0, LIST + f1)
        lists_ref[at_f] = k | (src_f << 8) | (to_t << 16)
        lists_ref[2 * LIST + k] = k | ((rel * 32 + to_t) << 8) | (s << 16)
        return (f0 + 1 - rel, f1 + rel)

    zero = jnp.int32(0)
    count = count_ref[0]
    sizes = lax.fori_loop(0, count, place, (zero, zero))
    lists_ref[3 * LIST] = sizes[0]
    lists_ref[3 * LIST + 1] = sizes[1]
    lists_ref[3 * LIST + 2] = count


def prep(where, out_index, in_index, count):
    return pl.pallas_call(
        prep_kernel,
        out_shape=jax.ShapeDtypeStruct((1024,), jnp.int32),
        in_specs=[smem()] * 4,
        out_specs=smem(),
        name="slot_lists",
    )(where, out_index, in_index, count)


def tile_loop(which, lists_ref, vals, buf, sems, acc, ready, product):
    base = which * LIST
    groups = (lists_ref[3 * LIST + which] + (UNROLL - 1)) // UNROLL
    ahead = DEPTH // UNROLL

    def copy(g, u):
        slot = lists_ref[base + g * UNROLL + u] & 255
        at = lax.rem(g, ahead) * UNROLL + u
        return pltpu.make_async_copy(vals.at[slot], buf.at[at], sems.at[at])

    for g in range(ahead):

        @pl.when(g < groups)
        def _():
            for u in range(UNROLL):
                copy(g, u).start()

    ready()

    def body(g, carry):
        for u in range(UNROLL):
            copy(g, u).wait()
        todo = []
        for u in range(UNROLL):
            entry = lists_ref[base + g * UNROLL + u]
            at = lax.rem(g, ahead) * UNROLL + u
            todo.append((entry >> 16, product(buf[at], (entry >> 8) & 255)))
        for to, value in todo:
            acc[to] += value

        @pl.when(g + ahead < groups)
        def _():
            for u in range(UNROLL):
                copy(g + ahead, u).start()

        return carry

    lax.fori_loop(0, groups, body, 0)


def in_hbm(array):
    return pltpu.with_memory_space_constraint(array, pltpu.HBM)


TILES_COST = pl.CostEstimate(
    flops=2 * 64 * TILE * TILE * FEAT, bytes_accessed=16 * 2**20, transcendentals=0
)


def forward_kernel(which, lists_ref, vals, *rest):
    blocks = rest[:NPEER]
    out_ref, x, buf, acc, sems, own_sem = rest[NPEER:]
    own = pltpu.make_async_copy(blocks[0], x.at[pl.ds(0, 4 * TILE)], own_sem)
    own.start()

    def ready():
        def clear(i, carry):
            acc[i] = jnp.zeros((TILE, FEAT), f32)
            return carry

        lax.fori_loop(0, FWD_DUMMY, clear, 0)
        for k in range(1, NPEER):
            x[pl.ds(k * 4 * TILE, 4 * TILE), :] = blocks[k][...]
        own.wait()

    def product(tile, source):
        rows = x[pl.ds(pl.multiple_of(source * TILE, TILE), TILE), :]
        return jnp.dot(tile, rows, preferred_element_type=f32)

    tile_loop(which, lists_ref, vals, buf, sems, acc, ready, product)

    for i in range(4 * NPEER):
        out_ref[i // 4, pl.ds((i % 4) * TILE, TILE), :] = acc[i].astype(bf16)


def forward(which, lists, values, blocks):
    return pl.pallas_call(
        functools.partial(forward_kernel, which),
        out_shape=jax.ShapeDtypeStruct((NPEER, 4 * TILE, FEAT), bf16),
        in_specs=[smem(), hbm(), hbm()] + [vmem()] * (NPEER - 1),
        out_specs=vmem(),
        scratch_shapes=[
            pltpu.VMEM((NPEER * 4 * TILE, FEAT), bf16),
            pltpu.VMEM((DEPTH, TILE, TILE), bf16),
            pltpu.VMEM((FWD_DUMMY + 1, TILE, FEAT), f32),
            pltpu.SemaphoreType.DMA((DEPTH,)),
            pltpu.SemaphoreType.DMA,
        ],
        compiler_params=params(),
        cost_estimate=TILES_COST,
        name="forward_tiles",
    )(in_hbm(lists), in_hbm(values), in_hbm(blocks[0]), *blocks[1:])


def pair_sum_kernel(mine_ref, other_ref, out_ref):
    for k in range(NPEER):
        out_ref[k] = (mine_ref[k].astype(f32) + other_ref[k].astype(f32)).astype(bf16)


def pair_sum(mine, other):
    return pl.pallas_call(
        pair_sum_kernel,
        out_shape=jax.ShapeDtypeStruct(mine.shape, bf16),
        in_specs=[vmem()] * 2,
        out_specs=vmem(),
        compiler_params=params(),
        cost_estimate=pl.CostEstimate(flops=2**21, bytes_accessed=6 * 2**20, transcendentals=0),
        name="pair_sum",
    )(mine, other)


def backward_kernel(
    lists_ref, vals, mine_ref, other_ref, out_ref, g, out, buf, acc, sems, out_sems
):
    rows4 = 4 * FEAT

    def ready():
        def clear(i, carry):
            acc[i] = jnp.zeros((FEAT, TILE), f32)
            return carry

        lax.fori_loop(0, BWD_DUMMY, clear, 0)
        for p, ref in enumerate((mine_ref, other_ref)):
            for peer in range(NPEER):
                g[pl.ds((p * NPEER + peer) * rows4, rows4), :] = ref[peer]

    def product(tile, source):
        rows = g[pl.ds(pl.multiple_of(source * FEAT, FEAT), FEAT), :]
        return jnp.dot(rows, tile, preferred_element_type=f32)

    tile_loop(2, lists_ref, vals, buf, sems, acc, ready, product)

    copies = []
    for i in range(4 * NPEER):
        out[i // 4, pl.ds((i % 4) * FEAT, FEAT), :] = acc[i].astype(bf16)
        if i % 4 == 3:
            peer = i // 4
            copies.append(
                pltpu.make_async_copy(out.at[peer], out_ref.at[peer], out_sems.at[peer])
            )
            copies[-1].start()
    for copy in copies:
        copy.wait()


def backward(lists, values, mine, other):
    return pl.pallas_call(
        backward_kernel,
        out_shape=pltpu.HBM((NPEER, 4 * FEAT, TILE), bf16),
        in_specs=[smem(), hbm(), vmem(), vmem()],
        out_specs=hbm(),
        scratch_shapes=[
            pltpu.VMEM((2 * NPEER * 4 * FEAT, TILE), bf16),
            pltpu.VMEM((NPEER, 4 * FEAT, TILE), bf16),
            pltpu.VMEM((DEPTH, TILE, TILE), bf16),
            pltpu.VMEM((BWD_DUMMY + 1, FEAT, TILE), f32),
            pltpu.SemaphoreType.DMA((DEPTH,)),
            pltpu.SemaphoreType.DMA((NPEER,)),
        ],
        compiler_params=params(),
        cost_estimate=TILES_COST,
        name="backward_tiles",
    )(in_hbm(lists), in_hbm(values), mine, other)


def dense_kernel(
    recv_ref, weight_ref, bias_ref, cot_ref, hidden_ref, grad_ref, wsum_ref, one, sems
):
    copies = []
    weight = weight_ref[...]
    for part in range(2):
        here = pl.ds(part * 2 * TILE, 2 * TILE)
        total = recv_ref[0, here, :].astype(f32)
        for peer in range(1, NPEER):
            total += recv_ref[peer, here, :].astype(f32)
        agg = total.astype(bf16)
        v = jnp.dot(agg, weight, preferred_element_type=f32) + bias_ref[...]
        s = jnp.tanh(gelu_coef * (v + cube_coef * v * v * v))
        hidden_ref[here, :] = (0.5 * v * (1.0 + s)).astype(bf16)
        slope = 0.5 * (1.0 + s) + 0.5 * v * (1.0 - s * s) * gelu_coef * (
            1.0 + 3.0 * cube_coef * v * v
        )
        grad = (cot_ref[here, :].astype(f32) * slope).astype(bf16)
        wsum = lax.dot_general(agg, grad, (((0,), (0,)), ((), ())), preferred_element_type=f32)
        bsum = jnp.dot(jnp.ones((16, 2 * TILE), bf16), grad, preferred_element_type=f32)[:8]
        back = lax.dot_general(weight, grad, (((1,), (1,)), ((), ())), preferred_element_type=f32)
        back = back.astype(bf16)
        for sub in range(2):
            rows = pl.ds((part * 2 + sub) * FEAT, FEAT)
            one[rows, :] = back[:, sub * TILE : (sub + 1) * TILE]
        rows = pl.ds(part * 2 * FEAT, 2 * FEAT)
        for peer in range(NPEER):
            copies.append(
                pltpu.make_async_copy(
                    one.at[rows], grad_ref.at[peer, rows], sems.at[part * NPEER + peer]
                )
            )
            copies[-1].start()
        if part == 0:
            wsum_ref[pl.ds(0, FEAT), :] = wsum
            wsum_ref[pl.ds(FEAT, 8), :] = bsum
        else:
            wsum_ref[pl.ds(0, FEAT), :] += wsum
            wsum_ref[pl.ds(FEAT, 8), :] += bsum
    for copy in copies:
        copy.wait()


def dense(recv, weight, bias, cotangent):
    return pl.pallas_call(
        dense_kernel,
        out_shape=(
            jax.ShapeDtypeStruct((4 * TILE, FEAT), bf16),
            pltpu.HBM((NPEER, 4 * FEAT, TILE), bf16),
            jax.ShapeDtypeStruct((FEAT + 8, FEAT), f32),
        ),
        in_specs=[vmem()] * 4,
        out_specs=(vmem(), hbm(), vmem()),
        scratch_shapes=[
            pltpu.VMEM((4 * FEAT, TILE), bf16),
            pltpu.SemaphoreType.DMA((2 * NPEER,)),
        ],
        compiler_params=params(),
        cost_estimate=pl.CostEstimate(
            flops=6 * 1024 * FEAT * FEAT, bytes_accessed=5 * 2**20, transcendentals=1024 * FEAT
        ),
        name="dense_layer",
    )(recv, weight, bias, cotangent)


def last_kernel(recv_ref, grad_ref):
    for sub in range(4):
        rows = pl.ds(sub * FEAT, FEAT)
        total = recv_ref[0, rows, :].astype(f32)
        for peer in range(1, NPEER):
            total += recv_ref[peer, rows, :].astype(f32)
        grad_ref[pl.ds(sub * TILE, TILE), :] = total.T.astype(bf16)


def last(recv):
    return pl.pallas_call(
        last_kernel,
        out_shape=jax.ShapeDtypeStruct((4 * TILE, FEAT), bf16),
        in_specs=[vmem()],
        out_specs=vmem(),
        compiler_params=params(),
        cost_estimate=pl.CostEstimate(flops=2**20, bytes_accessed=3 * 2**20, transcendentals=0),
        name="last_sum",
    )(recv)


SAME_CORE = [[2 * j + core for j in range(NPEER)] for core in range(2)]
OTHER_CORE = [(r, r ^ 1) for r in range(16)]


def to_other_core(value):
    return lax.ppermute(value, "row", OTHER_CORE)


def row_exchange(value):
    return lax.all_to_all(value, "row", 0, 0, axis_index_groups=SAME_CORE)


def col_exchange(value):
    return lax.all_to_all(value, "col", 0, 0)


def col_shift(value, k):
    pairs = []
    for c in range(8):
        z, y = c // 2, c % 2
        pairs.append((c, ((z + k // 2) % 4) * 2 + (y + k) % 2))
    return lax.ppermute(value, "col", pairs)


def butterfly(value, axis, size, bits):
    for bit in bits:
        value = value + lax.ppermute(value, axis, [(i, i ^ bit) for i in range(size)])
    return value


def local(features, weight, layer_bias, cotangent, tile_out, tile_in, tile_vals, tile_count):
    values = tile_vals[0, 0]
    row, col = lax.axis_index("row"), lax.axis_index("col")
    where = jnp.stack([row & 1, col >> 1, col & 1]).astype(jnp.int32)
    lists = prep(where, tile_out[0, 0], tile_in[0, 0], tile_count[0])
    bias = layer_bias.reshape(1, FEAT)
    order = lax.optimization_barrier

    blocks = [features] + [col_shift(features, k) for k in range(1, NPEER)]

    other = forward(1, lists, values, blocks)
    other, lists = order((other, lists))
    mine = forward(0, lists, values, blocks)
    recv = row_exchange(pair_sum(mine, to_other_core(other)))
    hidden, grad, wsum = dense(recv, weight, bias, cotangent)
    grads = row_exchange(grad)
    wsum = butterfly(wsum, "row", 16, (1, 2, 4, 8))
    grads, wsum = order((grads, wsum))
    back = backward(lists, values, grads, to_other_core(grads))
    back = col_exchange(back)
    wsum = butterfly(wsum, "col", 8, (1, 2, 4))
    scale = 1.0 / math.sqrt(4 * TILE * 128)
    weight_grad = wsum[:FEAT] * scale
    bias_grad = wsum[FEAT] * scale
    back, weight_grad, bias_grad = order((back, weight_grad, bias_grad))
    feature_grad = last(back)
    return (hidden, feature_grad, weight_grad, bias_grad)


def solution(mesh):
    in_specs = (
        P(("row", "col"), None),
        P(),
        P(),
        P(("col", "row"), None),
        P("row", "col", None),
        P("row", "col", None),
        P("row", "col", None, None, None),
        P("row", "col"),
    )
    out_specs = (P(("col", "row"), None), P(("row", "col"), None), P(), P())
    return jax.shard_map(local, mesh=mesh, in_specs=in_specs, out_specs=out_specs, check_vma=False)
```

```python
import functools
import math

import jax
import jax.numpy as jnp
from jax import lax
from jax.experimental import pallas as pl
from jax.experimental.pallas import tpu as pltpu
from jax.sharding import PartitionSpec as P

gelu_coef = 0.7978845608
cube_coef = 0.044715
TILE = 256
FEAT = 128
SLOTS = 128
NPEER = 8
LIST = 160
UNROLL = 8
DEPTH = 32
FWD_DUMMY = 32
BWD_DUMMY = 32
f32, bf16 = jnp.float32, jnp.bfloat16
VMEM_LIMIT = 28 * 2**20


def params():
    return pltpu.CompilerParams(vmem_limit_bytes=VMEM_LIMIT)


def vmem():
    return pl.BlockSpec(memory_space=pltpu.VMEM)


def smem():
    return pl.BlockSpec(memory_space=pltpu.SMEM)


def hbm():
    return pl.BlockSpec(memory_space=pl.ANY)


def prep_kernel(where_ref, out_ref, in_ref, count_ref, lists_ref):
    core = where_ref[0]

    def clear(i, carry):
        lists_ref[i] = FWD_DUMMY << 16
        lists_ref[LIST + i] = FWD_DUMMY << 16
        lists_ref[2 * LIST + i] = BWD_DUMMY << 16
        return carry

    lax.fori_loop(0, LIST, clear, 0)

    def place(k, carry):
        f0, f1 = carry
        t = out_ref[k]
        s = in_ref[k]
        rel = jnp.bitwise_xor((t >> 2) & 1, core)
        to_t = ((t >> 3) << 2) | (t & 3)
        at_f = jnp.where(rel == 0, f0, LIST + f1)
        lists_ref[at_f] = k | (s << 8) | (to_t << 16)
        lists_ref[2 * LIST + k] = k | ((rel * 32 + to_t) << 8) | (s << 16)
        return (f0 + 1 - rel, f1 + rel)

    zero = jnp.int32(0)
    count = count_ref[0]
    sizes = lax.fori_loop(0, count, place, (zero, zero))
    lists_ref[3 * LIST] = sizes[0]
    lists_ref[3 * LIST + 1] = sizes[1]
    lists_ref[3 * LIST + 2] = count


def prep(where, out_index, in_index, count):
    return pl.pallas_call(
        prep_kernel,
        out_shape=jax.ShapeDtypeStruct((1024,), jnp.int32),
        in_specs=[smem()] * 4,
        out_specs=smem(),
        name="slot_lists",
    )(where, out_index, in_index, count)


def tile_loop(which, lists_ref, vals, buf, sems, acc, ready, product):
    base = which * LIST
    groups = (lists_ref[3 * LIST + which] + (UNROLL - 1)) // UNROLL
    ahead = DEPTH // UNROLL

    def copy(g, u):
        slot = lists_ref[base + g * UNROLL + u] & 255
        at = lax.rem(g, ahead) * UNROLL + u
        return pltpu.make_async_copy(vals.at[slot], buf.at[at], sems.at[at])

    for g in range(ahead):

        @pl.when(g < groups)
        def _():
            for u in range(UNROLL):
                copy(g, u).start()

    ready()

    def body(g, carry):
        for u in range(UNROLL):
            copy(g, u).wait()
        todo = []
        for u in range(UNROLL):
            entry = lists_ref[base + g * UNROLL + u]
            at = lax.rem(g, ahead) * UNROLL + u
            todo.append((entry >> 16, product(buf[at], (entry >> 8) & 255)))
        for to, value in todo:
            acc[to] += value

        @pl.when(g + ahead < groups)
        def _():
            for u in range(UNROLL):
                copy(g + ahead, u).start()

        return carry

    lax.fori_loop(0, groups, body, 0)


def in_hbm(array):
    return pltpu.with_memory_space_constraint(array, pltpu.HBM)


TILES_COST = pl.CostEstimate(
    flops=2 * 64 * TILE * TILE * FEAT, bytes_accessed=16 * 2**20, transcendentals=0
)


def forward_kernel(which, lists_ref, vals, x, out_ref, buf, acc, sems):
    def ready():
        def clear(i, carry):
            acc[i] = jnp.zeros((TILE, FEAT), f32)
            return carry

        lax.fori_loop(0, FWD_DUMMY, clear, 0)

    def product(tile, source):
        rows = pl.ds(pl.multiple_of((source & 3) * TILE, TILE), TILE)
        return jnp.dot(tile, x[source >> 2, rows, :], preferred_element_type=f32)

    tile_loop(which, lists_ref, vals, buf, sems, acc, ready, product)

    for i in range(4 * NPEER):
        out_ref[i // 4, pl.ds((i % 4) * TILE, TILE), :] = acc[i].astype(bf16)


def forward(which, lists, values, sources):
    return pl.pallas_call(
        functools.partial(forward_kernel, which),
        out_shape=jax.ShapeDtypeStruct((NPEER, 4 * TILE, FEAT), bf16),
        in_specs=[smem(), hbm(), vmem()],
        out_specs=vmem(),
        scratch_shapes=[
            pltpu.VMEM((DEPTH, TILE, TILE), bf16),
            pltpu.VMEM((FWD_DUMMY + 1, TILE, FEAT), f32),
            pltpu.SemaphoreType.DMA((DEPTH,)),
        ],
        compiler_params=params(),
        cost_estimate=TILES_COST,
        name="forward_tiles",
    )(in_hbm(lists), in_hbm(values), sources)


def pair_sum_kernel(mine_ref, other_ref, out_ref):
    for k in range(NPEER):
        out_ref[k] = (mine_ref[k].astype(f32) + other_ref[k].astype(f32)).astype(bf16)


def pair_sum(mine, other):
    return pl.pallas_call(
        pair_sum_kernel,
        out_shape=jax.ShapeDtypeStruct(mine.shape, bf16),
        in_specs=[vmem()] * 2,
        out_specs=vmem(),
        compiler_params=params(),
        cost_estimate=pl.CostEstimate(flops=2**21, bytes_accessed=6 * 2**20, transcendentals=0),
        name="pair_sum",
    )(mine, other)


def backward_kernel(
    lists_ref, vals, mine_ref, other_ref, out_ref, g, out, buf, acc, sems, out_sems
):
    rows4 = 4 * FEAT

    def ready():
        def clear(i, carry):
            acc[i] = jnp.zeros((FEAT, TILE), f32)
            return carry

        lax.fori_loop(0, BWD_DUMMY, clear, 0)
        for p, ref in enumerate((mine_ref, other_ref)):
            for peer in range(NPEER):
                g[pl.ds((p * NPEER + peer) * rows4, rows4), :] = ref[peer]

    def product(tile, source):
        rows = g[pl.ds(pl.multiple_of(source * FEAT, FEAT), FEAT), :]
        return jnp.dot(rows, tile, preferred_element_type=f32)

    tile_loop(2, lists_ref, vals, buf, sems, acc, ready, product)

    copies = []
    for i in range(4 * NPEER):
        out[i // 4, pl.ds((i % 4) * FEAT, FEAT), :] = acc[i].astype(bf16)
        if i % 4 == 3:
            peer = i // 4
            copies.append(
                pltpu.make_async_copy(out.at[peer], out_ref.at[peer], out_sems.at[peer])
            )
            copies[-1].start()
    for copy in copies:
        copy.wait()


def backward(lists, values, mine, other):
    return pl.pallas_call(
        backward_kernel,
        out_shape=pltpu.HBM((NPEER, 4 * FEAT, TILE), bf16),
        in_specs=[smem(), hbm(), vmem(), vmem()],
        out_specs=hbm(),
        scratch_shapes=[
            pltpu.VMEM((2 * NPEER * 4 * FEAT, TILE), bf16),
            pltpu.VMEM((NPEER, 4 * FEAT, TILE), bf16),
            pltpu.VMEM((DEPTH, TILE, TILE), bf16),
            pltpu.VMEM((BWD_DUMMY + 1, FEAT, TILE), f32),
            pltpu.SemaphoreType.DMA((DEPTH,)),
            pltpu.SemaphoreType.DMA((NPEER,)),
        ],
        compiler_params=params(),
        cost_estimate=TILES_COST,
        name="backward_tiles",
    )(in_hbm(lists), in_hbm(values), mine, other)


def dense_kernel(
    recv_ref, weight_ref, bias_ref, cot_ref, hidden_ref, grad_ref, wsum_ref, one, sems
):
    copies = []
    weight = weight_ref[...]
    for part in range(2):
        here = pl.ds(part * 2 * TILE, 2 * TILE)
        total = recv_ref[0, here, :].astype(f32)
        for peer in range(1, NPEER):
            total += recv_ref[peer, here, :].astype(f32)
        agg = total.astype(bf16)
        v = jnp.dot(agg, weight, preferred_element_type=f32) + bias_ref[...]
        s = jnp.tanh(gelu_coef * (v + cube_coef * v * v * v))
        hidden_ref[here, :] = (0.5 * v * (1.0 + s)).astype(bf16)
        slope = 0.5 * (1.0 + s) + 0.5 * v * (1.0 - s * s) * gelu_coef * (
            1.0 + 3.0 * cube_coef * v * v
        )
        grad = (cot_ref[here, :].astype(f32) * slope).astype(bf16)
        wsum = lax.dot_general(agg, grad, (((0,), (0,)), ((), ())), preferred_element_type=f32)
        bsum = jnp.dot(jnp.ones((16, 2 * TILE), bf16), grad, preferred_element_type=f32)[:8]
        back = lax.dot_general(weight, grad, (((1,), (1,)), ((), ())), preferred_element_type=f32)
        back = back.astype(bf16)
        for sub in range(2):
            rows = pl.ds((part * 2 + sub) * FEAT, FEAT)
            one[rows, :] = back[:, sub * TILE : (sub + 1) * TILE]
        rows = pl.ds(part * 2 * FEAT, 2 * FEAT)
        for peer in range(NPEER):
            copies.append(
                pltpu.make_async_copy(
                    one.at[rows], grad_ref.at[peer, rows], sems.at[part * NPEER + peer]
                )
            )
            copies[-1].start()
        if part == 0:
            wsum_ref[pl.ds(0, FEAT), :] = wsum
            wsum_ref[pl.ds(FEAT, 8), :] = bsum
        else:
            wsum_ref[pl.ds(0, FEAT), :] += wsum
            wsum_ref[pl.ds(FEAT, 8), :] += bsum
    for copy in copies:
        copy.wait()


def dense(recv, weight, bias, cotangent):
    return pl.pallas_call(
        dense_kernel,
        out_shape=(
            jax.ShapeDtypeStruct((4 * TILE, FEAT), bf16),
            pltpu.HBM((NPEER, 4 * FEAT, TILE), bf16),
            jax.ShapeDtypeStruct((FEAT + 8, FEAT), f32),
        ),
        in_specs=[vmem()] * 4,
        out_specs=(vmem(), hbm(), vmem()),
        scratch_shapes=[
            pltpu.VMEM((4 * FEAT, TILE), bf16),
            pltpu.SemaphoreType.DMA((2 * NPEER,)),
        ],
        compiler_params=params(),
        cost_estimate=pl.CostEstimate(
            flops=6 * 1024 * FEAT * FEAT, bytes_accessed=5 * 2**20, transcendentals=1024 * FEAT
        ),
        name="dense_layer",
    )(recv, weight, bias, cotangent)


def last_kernel(recv_ref, grad_ref):
    for sub in range(4):
        rows = pl.ds(sub * FEAT, FEAT)
        total = recv_ref[0, rows, :].astype(f32)
        for peer in range(1, NPEER):
            total += recv_ref[peer, rows, :].astype(f32)
        grad_ref[pl.ds(sub * TILE, TILE), :] = total.T.astype(bf16)


def last(recv):
    return pl.pallas_call(
        last_kernel,
        out_shape=jax.ShapeDtypeStruct((4 * TILE, FEAT), bf16),
        in_specs=[vmem()],
        out_specs=vmem(),
        compiler_params=params(),
        cost_estimate=pl.CostEstimate(flops=2**20, bytes_accessed=3 * 2**20, transcendentals=0),
        name="last_sum",
    )(recv)


SAME_CORE = [[2 * j + core for j in range(NPEER)] for core in range(2)]
OTHER_CORE = [(r, r ^ 1) for r in range(16)]


def to_other_core(value):
    return lax.ppermute(value, "row", OTHER_CORE)


def row_exchange(value):
    return lax.all_to_all(value, "row", 0, 0, axis_index_groups=SAME_CORE)


def col_exchange(value):
    return lax.all_to_all(value, "col", 0, 0)


def partner(value, axis, size, bit):
    return lax.ppermute(value, axis, [(i, i ^ bit) for i in range(size)])


def local(features, weight, layer_bias, cotangent, tile_out, tile_in, tile_vals, tile_count):
    values = tile_vals[0, 0]
    where = (lax.axis_index("row") & 1).astype(jnp.int32).reshape(1)
    lists = prep(where, tile_out[0, 0], tile_in[0, 0], tile_count[0])
    bias = layer_bias.reshape(1, FEAT)
    order = lax.optimization_barrier

    sources = col_exchange(jnp.broadcast_to(features, (NPEER, 4 * TILE, FEAT)))
    other = forward(1, lists, values, sources)
    other, lists = order((other, lists))
    mine = forward(0, lists, values, sources)
    recv = row_exchange(pair_sum(mine, to_other_core(other)))
    hidden, grad, total = dense(recv, weight, bias, cotangent)

    grads = row_exchange(grad)
    for bit in (2, 4):
        total = total + partner(total, "col", 8, bit)
    total = total + partner(total, "row", 16, 1)
    grads, total = order((grads, total))
    other = to_other_core(grads)
    total = total + partner(total, "col", 8, 1)
    other, total = order((other, total))
    second = partner(total, "row", 16, 2)
    back = backward(lists, values, grads, other)
    back, second = order((back, second))
    total = total + second
    back = col_exchange(back)
    for bit in (4, 8):
        total = total + partner(total, "row", 16, bit)
    scale = 1.0 / math.sqrt(4 * TILE * 128)
    weight_grad = total[:FEAT] * scale
    bias_grad = total[FEAT] * scale
    back, weight_grad, bias_grad = order((back, weight_grad, bias_grad))
    feature_grad = last(back)
    return (hidden, feature_grad, weight_grad, bias_grad)


def solution(mesh):
    in_specs = (
        P(("row", "col"), None),
        P(),
        P(),
        P(("col", "row"), None),
        P("row", "col", None),
        P("row", "col", None),
        P("row", "col", None, None, None),
        P("row", "col"),
    )
    out_specs = (P(("col", "row"), None), P(("row", "col"), None), P(), P())
    return jax.shard_map(local, mesh=mesh, in_specs=in_specs, out_specs=out_specs, check_vma=False)
```

```python
import functools
import math

import jax
import jax.numpy as jnp
from jax import lax
from jax.experimental import pallas as pl
from jax.experimental.pallas import tpu as pltpu
from jax.sharding import PartitionSpec as P

gelu_coef = 0.7978845608
cube_coef = 0.044715
TILE = 256
FEAT = 128
SLOTS = 128
NPEER = 8
LIST = 160
UNROLL = 8
DEPTH = 32
FWD_DUMMY = 32
BWD_DUMMY = 32
f32, bf16 = jnp.float32, jnp.bfloat16
VMEM_LIMIT = 28 * 2**20


def params():
    return pltpu.CompilerParams(vmem_limit_bytes=VMEM_LIMIT)


def vmem():
    return pl.BlockSpec(memory_space=pltpu.VMEM)


def smem():
    return pl.BlockSpec(memory_space=pltpu.SMEM)


def hbm():
    return pl.BlockSpec(memory_space=pl.ANY)


def prep_kernel(where_ref, out_ref, in_ref, count_ref, lists_ref):
    core = where_ref[0]

    def clear(i, carry):
        lists_ref[i] = FWD_DUMMY << 16
        lists_ref[LIST + i] = FWD_DUMMY << 16
        lists_ref[2 * LIST + i] = BWD_DUMMY << 16
        return carry

    lax.fori_loop(0, LIST, clear, 0)

    def place(k, carry):
        f0, f1 = carry
        t = out_ref[k]
        s = in_ref[k]
        rel = jnp.bitwise_xor((t >> 2) & 1, core)
        to_t = ((t >> 3) << 2) | (t & 3)
        at_f = jnp.where(rel == 0, f0, LIST + f1)
        lists_ref[at_f] = k | (s << 8) | (to_t << 16)
        lists_ref[2 * LIST + k] = k | ((rel * 32 + to_t) << 8) | (s << 16)
        return (f0 + 1 - rel, f1 + rel)

    zero = jnp.int32(0)
    count = count_ref[0]
    sizes = lax.fori_loop(0, count, place, (zero, zero))
    lists_ref[3 * LIST] = sizes[0]
    lists_ref[3 * LIST + 1] = sizes[1]
    lists_ref[3 * LIST + 2] = count


def prep(where, out_index, in_index, count):
    return pl.pallas_call(
        prep_kernel,
        out_shape=jax.ShapeDtypeStruct((1024,), jnp.int32),
        in_specs=[smem()] * 4,
        out_specs=smem(),
        compiler_params=params(),
        name="slot_lists",
    )(where, out_index, in_index, count)


def copies_kernel(value_ref, out_ref, sems):
    copies = [
        pltpu.make_async_copy(value_ref, out_ref.at[peer], sems.at[peer]) for peer in range(NPEER)
    ]
    for copy in copies:
        copy.start()
    for copy in copies:
        copy.wait()


def copies_of(value):
    return pl.pallas_call(
        copies_kernel,
        out_shape=pltpu.HBM((NPEER, *value.shape), value.dtype),
        in_specs=[vmem()],
        out_specs=hbm(),
        scratch_shapes=[pltpu.SemaphoreType.DMA((NPEER,))],
        compiler_params=params(),
        name="copies",
    )(value)


def tile_loop(which, lists_ref, vals, buf, sems, acc, ready, product):
    base = which * LIST
    groups = (lists_ref[3 * LIST + which] + (UNROLL - 1)) // UNROLL
    ahead = DEPTH // UNROLL

    def copy(g, u):
        slot = lists_ref[base + g * UNROLL + u] & 255
        at = lax.rem(g, ahead) * UNROLL + u
        return pltpu.make_async_copy(vals.at[slot], buf.at[at], sems.at[at])

    for g in range(ahead):

        @pl.when(g < groups)
        def _():
            for u in range(UNROLL):
                copy(g, u).start()

    ready()

    def body(g, carry):
        for u in range(UNROLL):
            copy(g, u).wait()
        todo = []
        for u in range(UNROLL):
            entry = lists_ref[base + g * UNROLL + u]
            at = lax.rem(g, ahead) * UNROLL + u
            todo.append((entry >> 16, product(buf[at], (entry >> 8) & 255)))
        for to, value in todo:
            acc[to] += value

        @pl.when(g + ahead < groups)
        def _():
            for u in range(UNROLL):
                copy(g + ahead, u).start()

        return carry

    lax.fori_loop(0, groups, body, 0)


def in_hbm(array):
    return pltpu.with_memory_space_constraint(array, pltpu.HBM)


TILES_COST = pl.CostEstimate(
    flops=2 * 64 * TILE * TILE * FEAT, bytes_accessed=16 * 2**20, transcendentals=0
)


def forward_kernel(which, lists_ref, vals, x, out_ref, buf, acc, sems):
    def ready():
        def clear(i, carry):
            acc[i] = jnp.zeros((TILE, FEAT), f32)
            return carry

        lax.fori_loop(0, FWD_DUMMY, clear, 0)

    def product(tile, source):
        rows = pl.ds(pl.multiple_of((source & 3) * TILE, TILE), TILE)
        return jnp.dot(tile, x[source >> 2, rows, :], preferred_element_type=f32)

    tile_loop(which, lists_ref, vals, buf, sems, acc, ready, product)

    for i in range(4 * NPEER):
        out_ref[i // 4, pl.ds((i % 4) * TILE, TILE), :] = acc[i].astype(bf16)


def forward(which, lists, values, sources):
    return pl.pallas_call(
        functools.partial(forward_kernel, which),
        out_shape=jax.ShapeDtypeStruct((NPEER, 4 * TILE, FEAT), bf16),
        in_specs=[smem(), hbm(), vmem()],
        out_specs=vmem(),
        scratch_shapes=[
            pltpu.VMEM((DEPTH, TILE, TILE), bf16),
            pltpu.VMEM((FWD_DUMMY + 1, TILE, FEAT), f32),
            pltpu.SemaphoreType.DMA((DEPTH,)),
        ],
        compiler_params=params(),
        cost_estimate=TILES_COST,
        name="forward_tiles",
    )(in_hbm(lists), in_hbm(values), sources)


def pair_sum_kernel(mine_ref, other_ref, out_ref):
    for k in range(NPEER):
        out_ref[k] = (mine_ref[k].astype(f32) + other_ref[k].astype(f32)).astype(bf16)


def pair_sum(mine, other):
    return pl.pallas_call(
        pair_sum_kernel,
        out_shape=jax.ShapeDtypeStruct(mine.shape, bf16),
        in_specs=[vmem()] * 2,
        out_specs=vmem(),
        compiler_params=params(),
        cost_estimate=pl.CostEstimate(flops=2**21, bytes_accessed=6 * 2**20, transcendentals=0),
        name="pair_sum",
    )(mine, other)


def backward_kernel(
    lists_ref, vals, mine_ref, other_ref, out_ref, g, out, buf, acc, sems, out_sems
):
    rows4 = 4 * FEAT

    def ready():
        def clear(i, carry):
            acc[i] = jnp.zeros((FEAT, TILE), f32)
            return carry

        lax.fori_loop(0, BWD_DUMMY, clear, 0)
        for p, ref in enumerate((mine_ref, other_ref)):
            for peer in range(NPEER):
                g[pl.ds((p * NPEER + peer) * rows4, rows4), :] = ref[peer]

    def product(tile, source):
        rows = g[pl.ds(pl.multiple_of(source * FEAT, FEAT), FEAT), :]
        return jnp.dot(rows, tile, preferred_element_type=f32)

    tile_loop(2, lists_ref, vals, buf, sems, acc, ready, product)

    copies = []
    for i in range(4 * NPEER):
        out[i // 4, pl.ds((i % 4) * FEAT, FEAT), :] = acc[i].astype(bf16)
        if i % 4 == 3:
            peer = i // 4
            copies.append(
                pltpu.make_async_copy(out.at[peer], out_ref.at[peer], out_sems.at[peer])
            )
            copies[-1].start()
    for copy in copies:
        copy.wait()


def backward(lists, values, mine, other):
    return pl.pallas_call(
        backward_kernel,
        out_shape=pltpu.HBM((NPEER, 4 * FEAT, TILE), bf16),
        in_specs=[smem(), hbm(), vmem(), vmem()],
        out_specs=hbm(),
        scratch_shapes=[
            pltpu.VMEM((2 * NPEER * 4 * FEAT, TILE), bf16),
            pltpu.VMEM((NPEER, 4 * FEAT, TILE), bf16),
            pltpu.VMEM((DEPTH, TILE, TILE), bf16),
            pltpu.VMEM((BWD_DUMMY + 1, FEAT, TILE), f32),
            pltpu.SemaphoreType.DMA((DEPTH,)),
            pltpu.SemaphoreType.DMA((NPEER,)),
        ],
        compiler_params=params(),
        cost_estimate=TILES_COST,
        name="backward_tiles",
    )(in_hbm(lists), in_hbm(values), mine, other)


def dense_kernel(
    recv_ref, weight_ref, bias_ref, cot_ref, hidden_ref, grad_ref, wsum_ref, one, sems
):
    copies = []
    weight = weight_ref[...]
    for part in range(2):
        here = pl.ds(part * 2 * TILE, 2 * TILE)
        total = recv_ref[0, here, :].astype(f32)
        for peer in range(1, NPEER):
            total += recv_ref[peer, here, :].astype(f32)
        agg = total.astype(bf16)
        v = jnp.dot(agg, weight, preferred_element_type=f32) + bias_ref[...]
        s = jnp.tanh(gelu_coef * (v + cube_coef * v * v * v))
        hidden_ref[here, :] = (0.5 * v * (1.0 + s)).astype(bf16)
        slope = 0.5 * (1.0 + s) + 0.5 * v * (1.0 - s * s) * gelu_coef * (
            1.0 + 3.0 * cube_coef * v * v
        )
        grad = (cot_ref[here, :].astype(f32) * slope).astype(bf16)
        wsum = lax.dot_general(agg, grad, (((0,), (0,)), ((), ())), preferred_element_type=f32)
        bsum = jnp.dot(jnp.ones((16, 2 * TILE), bf16), grad, preferred_element_type=f32)[:8]
        back = lax.dot_general(weight, grad, (((1,), (1,)), ((), ())), preferred_element_type=f32)
        back = back.astype(bf16)
        for sub in range(2):
            rows = pl.ds((part * 2 + sub) * FEAT, FEAT)
            one[rows, :] = back[:, sub * TILE : (sub + 1) * TILE]
        rows = pl.ds(part * 2 * FEAT, 2 * FEAT)
        for peer in range(NPEER):
            copies.append(
                pltpu.make_async_copy(
                    one.at[rows], grad_ref.at[peer, rows], sems.at[part * NPEER + peer]
                )
            )
            copies[-1].start()
        if part == 0:
            wsum_ref[pl.ds(0, FEAT), :] = wsum
            wsum_ref[pl.ds(FEAT, 8), :] = bsum
        else:
            wsum_ref[pl.ds(0, FEAT), :] += wsum
            wsum_ref[pl.ds(FEAT, 8), :] += bsum
    for copy in copies:
        copy.wait()


def dense(recv, weight, bias, cotangent):
    return pl.pallas_call(
        dense_kernel,
        out_shape=(
            jax.ShapeDtypeStruct((4 * TILE, FEAT), bf16),
            pltpu.HBM((NPEER, 4 * FEAT, TILE), bf16),
            jax.ShapeDtypeStruct((FEAT + 8, FEAT), f32),
        ),
        in_specs=[vmem()] * 4,
        out_specs=(vmem(), hbm(), vmem()),
        scratch_shapes=[
            pltpu.VMEM((4 * FEAT, TILE), bf16),
            pltpu.SemaphoreType.DMA((2 * NPEER,)),
        ],
        compiler_params=params(),
        cost_estimate=pl.CostEstimate(
            flops=6 * 1024 * FEAT * FEAT, bytes_accessed=5 * 2**20, transcendentals=1024 * FEAT
        ),
        name="dense_layer",
    )(recv, weight, bias, cotangent)


def last_kernel(recv_ref, grad_ref):
    for sub in range(4):
        rows = pl.ds(sub * FEAT, FEAT)
        total = recv_ref[0, rows, :].astype(f32)
        for peer in range(1, NPEER):
            total += recv_ref[peer, rows, :].astype(f32)
        grad_ref[pl.ds(sub * TILE, TILE), :] = total.T.astype(bf16)


def last(recv):
    return pl.pallas_call(
        last_kernel,
        out_shape=jax.ShapeDtypeStruct((4 * TILE, FEAT), bf16),
        in_specs=[vmem()],
        out_specs=vmem(),
        compiler_params=params(),
        cost_estimate=pl.CostEstimate(flops=2**20, bytes_accessed=3 * 2**20, transcendentals=0),
        name="last_sum",
    )(recv)


SAME_CORE = [[2 * j + core for j in range(NPEER)] for core in range(2)]
OTHER_CORE = [(r, r ^ 1) for r in range(16)]


def to_other_core(value):
    return lax.ppermute(value, "row", OTHER_CORE)


def row_exchange(value):
    return lax.all_to_all(value, "row", 0, 0, axis_index_groups=SAME_CORE)


def col_exchange(value):
    return lax.all_to_all(value, "col", 0, 0)


def partner(value, axis, size, bit):
    return lax.ppermute(value, axis, [(i, i ^ bit) for i in range(size)])


def local(features, weight, layer_bias, cotangent, tile_out, tile_in, tile_vals, tile_count):
    values = tile_vals[0, 0]
    where = (lax.axis_index("row") & 1).astype(jnp.int32).reshape(1)
    lists = prep(where, tile_out[0, 0], tile_in[0, 0], tile_count[0])
    bias = layer_bias.reshape(1, FEAT)
    order = lax.optimization_barrier

    sources = col_exchange(copies_of(features))
    other = forward(1, lists, values, sources)
    other, lists = order((other, lists))
    mine = forward(0, lists, values, sources)
    recv = row_exchange(pair_sum(mine, to_other_core(other)))
    hidden, grad, total = dense(recv, weight, bias, cotangent)

    grads = row_exchange(grad)
    for bit in (2, 4):
        total = total + partner(total, "col", 8, bit)
    total = total + partner(total, "row", 16, 1)
    total = total + partner(total, "col", 8, 1)
    grads, total = order((grads, total))
    other = to_other_core(grads)
    second = partner(total, "row", 16, 2)
    back = backward(lists, values, grads, other)
    back, second = order((back, second))
    total = total + second
    back = col_exchange(back)
    for bit in (4, 8):
        total = total + partner(total, "row", 16, bit)
    scale = 1.0 / math.sqrt(4 * TILE * 128)
    weight_grad = total[:FEAT] * scale
    bias_grad = total[FEAT] * scale
    back, weight_grad, bias_grad = order((back, weight_grad, bias_grad))
    feature_grad = last(back)
    return (hidden, feature_grad, weight_grad, bias_grad)


def solution(mesh):
    in_specs = (
        P(("row", "col"), None),
        P(),
        P(),
        P(("col", "row"), None),
        P("row", "col", None),
        P("row", "col", None),
        P("row", "col", None, None, None),
        P("row", "col"),
    )
    out_specs = (P(("col", "row"), None), P(("row", "col"), None), P(), P())
    return jax.shard_map(local, mesh=mesh, in_specs=in_specs, out_specs=out_specs, check_vma=False)
```

```python
import functools
import math

import jax
import jax.numpy as jnp
from jax import lax
from jax.experimental import pallas as pl
from jax.experimental.pallas import tpu as pltpu
from jax.sharding import PartitionSpec as P

gelu_coef = 0.7978845608
cube_coef = 0.044715
TILE = 256
FEAT = 128
SLOTS = 128
NPEER = 8
LIST = 160
UNROLL = 8
DEPTH = 32
FWD_DUMMY = 32
BWD_DUMMY = 32
f32, bf16 = jnp.float32, jnp.bfloat16
VMEM_LIMIT = 28 * 2**20


def params():
    return pltpu.CompilerParams(vmem_limit_bytes=VMEM_LIMIT)


def vmem():
    return pl.BlockSpec(memory_space=pltpu.VMEM)


def smem():
    return pl.BlockSpec(memory_space=pltpu.SMEM)


def hbm():
    return pl.BlockSpec(memory_space=pl.ANY)


def prep_kernel(where_ref, out_ref, in_ref, count_ref, lists_ref):
    core = where_ref[0]

    def clear(i, carry):
        lists_ref[i] = FWD_DUMMY << 16
        lists_ref[LIST + i] = FWD_DUMMY << 16
        lists_ref[2 * LIST + i] = BWD_DUMMY << 16
        lists_ref[3 * LIST + i] = BWD_DUMMY << 16
        return carry

    lax.fori_loop(0, LIST, clear, 0)

    def place(k, carry):
        f0, f1 = carry
        t = out_ref[k]
        s = in_ref[k]
        rel = jnp.bitwise_xor((t >> 2) & 1, core)
        to_t = ((t >> 3) << 2) | (t & 3)
        at_f = jnp.where(rel == 0, f0, LIST + f1)
        lists_ref[at_f] = k | (s << 8) | (to_t << 16)
        lists_ref[2 * LIST + at_f] = k | (to_t << 8) | (s << 16)
        return (f0 + 1 - rel, f1 + rel)

    zero = jnp.int32(0)
    sizes = lax.fori_loop(0, count_ref[0], place, (zero, zero))
    lists_ref[4 * LIST] = sizes[0]
    lists_ref[4 * LIST + 1] = sizes[1]


def prep(where, out_index, in_index, count):
    return pl.pallas_call(
        prep_kernel,
        out_shape=jax.ShapeDtypeStruct((1024,), jnp.int32),
        in_specs=[smem()] * 4,
        out_specs=smem(),
        compiler_params=params(),
        name="slot_lists",
    )(where, out_index, in_index, count)


def copies_kernel(value_ref, out_ref, sems):
    copies = [
        pltpu.make_async_copy(value_ref, out_ref.at[peer], sems.at[peer]) for peer in range(NPEER)
    ]
    for copy in copies:
        copy.start()
    for copy in copies:
        copy.wait()


def copies_of(value):
    return pl.pallas_call(
        copies_kernel,
        out_shape=pltpu.HBM((NPEER, *value.shape), value.dtype),
        in_specs=[hbm()],
        out_specs=hbm(),
        scratch_shapes=[pltpu.SemaphoreType.DMA((NPEER,))],
        compiler_params=params(),
        name="copies",
    )(in_hbm(value))


def tile_loop(which, lists_ref, vals, buf, sems, acc, ready, product):
    base = which * LIST
    groups = (lists_ref[4 * LIST + (which & 1)] + (UNROLL - 1)) // UNROLL
    ahead = DEPTH // UNROLL

    def copy(g, u):
        slot = lists_ref[base + g * UNROLL + u] & 255
        at = lax.rem(g, ahead) * UNROLL + u
        return pltpu.make_async_copy(vals.at[slot], buf.at[at], sems.at[at])

    for g in range(ahead):

        @pl.when(g < groups)
        def _():
            for u in range(UNROLL):
                copy(g, u).start()

    ready()

    def body(g, carry):
        for u in range(UNROLL):
            copy(g, u).wait()
        todo = []
        for u in range(UNROLL):
            entry = lists_ref[base + g * UNROLL + u]
            at = lax.rem(g, ahead) * UNROLL + u
            todo.append((entry >> 16, product(buf[at], (entry >> 8) & 255)))
        for to, value in todo:
            acc[to] += value

        @pl.when(g + ahead < groups)
        def _():
            for u in range(UNROLL):
                copy(g + ahead, u).start()

        return carry

    lax.fori_loop(0, groups, body, 0)


def in_hbm(array):
    return pltpu.with_memory_space_constraint(array, pltpu.HBM)


TILES_COST = pl.CostEstimate(
    flops=2 * 64 * TILE * TILE * FEAT, bytes_accessed=16 * 2**20, transcendentals=0
)


def forward_kernel(which, lists_ref, vals, x, out_ref, buf, acc, sems):
    def ready():
        def clear(i, carry):
            acc[i] = jnp.zeros((TILE, FEAT), f32)
            return carry

        lax.fori_loop(0, FWD_DUMMY, clear, 0)

    def product(tile, source):
        rows = pl.ds(pl.multiple_of((source & 3) * TILE, TILE), TILE)
        return jnp.dot(tile, x[source >> 2, rows, :], preferred_element_type=f32)

    tile_loop(which, lists_ref, vals, buf, sems, acc, ready, product)

    for i in range(4 * NPEER):
        out_ref[i // 4, pl.ds((i % 4) * TILE, TILE), :] = acc[i].astype(bf16)


def forward(which, lists, values, sources):
    return pl.pallas_call(
        functools.partial(forward_kernel, which),
        out_shape=jax.ShapeDtypeStruct((NPEER, 4 * TILE, FEAT), bf16),
        in_specs=[smem(), hbm(), vmem()],
        out_specs=vmem(),
        scratch_shapes=[
            pltpu.VMEM((DEPTH, TILE, TILE), bf16),
            pltpu.VMEM((FWD_DUMMY + 1, TILE, FEAT), f32),
            pltpu.SemaphoreType.DMA((DEPTH,)),
        ],
        compiler_params=params(),
        cost_estimate=TILES_COST,
        name="forward_tiles",
    )(in_hbm(lists), in_hbm(values), sources)


def pair_sum_kernel(mine_ref, other_ref, out_ref):
    for k in range(NPEER):
        out_ref[k] = (mine_ref[k].astype(f32) + other_ref[k].astype(f32)).astype(bf16)


def pair_sum(mine, other):
    return pl.pallas_call(
        pair_sum_kernel,
        out_shape=jax.ShapeDtypeStruct(mine.shape, bf16),
        in_specs=[vmem()] * 2,
        out_specs=vmem(),
        compiler_params=params(),
        cost_estimate=pl.CostEstimate(flops=2**21, bytes_accessed=6 * 2**20, transcendentals=0),
        name="pair_sum",
    )(mine, other)


def backward_kernel(which, lists_ref, vals, g, *rest):
    if which == 2:
        out, buf, acc, sems = rest
    else:
        before, out_ref, buf, acc, sems, out, out_sems = rest

    def ready():
        def clear(i, carry):
            acc[i] = jnp.zeros((FEAT, TILE), f32)
            return carry

        lax.fori_loop(0, BWD_DUMMY, clear, 0)

    def product(tile, source):
        rows = pl.ds(pl.multiple_of((source & 3) * FEAT, FEAT), FEAT)
        return jnp.dot(g[source >> 2, rows, :], tile, preferred_element_type=f32)

    tile_loop(which, lists_ref, vals, buf, sems, acc, ready, product)

    copies = []
    for i in range(4 * NPEER):
        peer, rows = i // 4, pl.ds((i % 4) * FEAT, FEAT)
        if which == 2:
            out[peer, rows, :] = acc[i].astype(bf16)
        else:
            out[peer, rows, :] = (acc[i] + before[peer, rows, :].astype(f32)).astype(bf16)
            if i % 4 == 3:
                copies.append(
                    pltpu.make_async_copy(out.at[peer], out_ref.at[peer], out_sems.at[peer])
                )
                copies[-1].start()
    for copy in copies:
        copy.wait()


def backward(which, lists, values, *blocks):
    shape = (NPEER, 4 * FEAT, TILE)
    scratch = [
        pltpu.VMEM((DEPTH, TILE, TILE), bf16),
        pltpu.VMEM((BWD_DUMMY + 1, FEAT, TILE), f32),
        pltpu.SemaphoreType.DMA((DEPTH,)),
    ]
    if which == 3:
        scratch += [pltpu.VMEM(shape, bf16), pltpu.SemaphoreType.DMA((NPEER,))]
    return pl.pallas_call(
        functools.partial(backward_kernel, which),
        out_shape=jax.ShapeDtypeStruct(shape, bf16) if which == 2 else pltpu.HBM(shape, bf16),
        in_specs=[smem(), hbm()] + [vmem()] * len(blocks),
        out_specs=vmem() if which == 2 else hbm(),
        scratch_shapes=scratch,
        compiler_params=params(),
        cost_estimate=TILES_COST,
        name="backward_tiles",
    )(in_hbm(lists), in_hbm(values), *blocks)


def dense_kernel(
    recv_ref, weight_ref, bias_ref, cot_ref, hidden_ref, grad_ref, wsum_ref, one, sems
):
    copies = []
    weight = weight_ref[...]
    for part in range(2):
        here = pl.ds(part * 2 * TILE, 2 * TILE)
        total = recv_ref[0, here, :].astype(f32)
        for peer in range(1, NPEER):
            total += recv_ref[peer, here, :].astype(f32)
        agg = total.astype(bf16)
        v = jnp.dot(agg, weight, preferred_element_type=f32) + bias_ref[...]
        s = jnp.tanh(gelu_coef * (v + cube_coef * v * v * v))
        hidden_ref[here, :] = (0.5 * v * (1.0 + s)).astype(bf16)
        slope = 0.5 * (1.0 + s) + 0.5 * v * (1.0 - s * s) * gelu_coef * (
            1.0 + 3.0 * cube_coef * v * v
        )
        grad = (cot_ref[here, :].astype(f32) * slope).astype(bf16)
        wsum = lax.dot_general(agg, grad, (((0,), (0,)), ((), ())), preferred_element_type=f32)
        bsum = jnp.dot(jnp.ones((16, 2 * TILE), bf16), grad, preferred_element_type=f32)[:8]
        back = lax.dot_general(weight, grad, (((1,), (1,)), ((), ())), preferred_element_type=f32)
        back = back.astype(bf16)
        for sub in range(2):
            rows = pl.ds((part * 2 + sub) * FEAT, FEAT)
            one[rows, :] = back[:, sub * TILE : (sub + 1) * TILE]
        rows = pl.ds(part * 2 * FEAT, 2 * FEAT)
        for peer in range(NPEER):
            copies.append(
                pltpu.make_async_copy(
                    one.at[rows], grad_ref.at[peer, rows], sems.at[part * NPEER + peer]
                )
            )
            copies[-1].start()
        if part == 0:
            wsum_ref[pl.ds(0, FEAT), :] = wsum
            wsum_ref[pl.ds(FEAT, 8), :] = bsum
        else:
            wsum_ref[pl.ds(0, FEAT), :] += wsum
            wsum_ref[pl.ds(FEAT, 8), :] += bsum
    for copy in copies:
        copy.wait()


def dense(recv, weight, bias, cotangent):
    return pl.pallas_call(
        dense_kernel,
        out_shape=(
            jax.ShapeDtypeStruct((4 * TILE, FEAT), bf16),
            pltpu.HBM((NPEER, 4 * FEAT, TILE), bf16),
            jax.ShapeDtypeStruct((FEAT + 8, FEAT), f32),
        ),
        in_specs=[vmem()] * 4,
        out_specs=(vmem(), hbm(), vmem()),
        scratch_shapes=[
            pltpu.VMEM((4 * FEAT, TILE), bf16),
            pltpu.SemaphoreType.DMA((2 * NPEER,)),
        ],
        compiler_params=params(),
        cost_estimate=pl.CostEstimate(
            flops=6 * 1024 * FEAT * FEAT, bytes_accessed=5 * 2**20, transcendentals=1024 * FEAT
        ),
        name="dense_layer",
    )(recv, weight, bias, cotangent)


def last_kernel(recv_ref, grad_ref):
    for sub in range(4):
        rows = pl.ds(sub * FEAT, FEAT)
        total = recv_ref[0, rows, :].astype(f32)
        for peer in range(1, NPEER):
            total += recv_ref[peer, rows, :].astype(f32)
        grad_ref[pl.ds(sub * TILE, TILE), :] = total.T.astype(bf16)


def last(recv):
    return pl.pallas_call(
        last_kernel,
        out_shape=jax.ShapeDtypeStruct((4 * TILE, FEAT), bf16),
        in_specs=[vmem()],
        out_specs=vmem(),
        compiler_params=params(),
        cost_estimate=pl.CostEstimate(flops=2**20, bytes_accessed=3 * 2**20, transcendentals=0),
        name="last_sum",
    )(recv)


SAME_CORE = [[2 * j + core for j in range(NPEER)] for core in range(2)]
OTHER_CORE = [(r, r ^ 1) for r in range(16)]


def to_other_core(value):
    return lax.ppermute(value, "row", OTHER_CORE)


def row_exchange(value):
    return lax.all_to_all(value, "row", 0, 0, axis_index_groups=SAME_CORE)


def col_exchange(value):
    return lax.all_to_all(value, "col", 0, 0)


def partner(value, axis, size, bit):
    return lax.ppermute(value, axis, [(i, i ^ bit) for i in range(size)])


def local(features, weight, layer_bias, cotangent, tile_out, tile_in, tile_vals, tile_count):
    values = tile_vals[0, 0]
    where = (lax.axis_index("row") & 1).astype(jnp.int32).reshape(1)
    lists = prep(where, tile_out[0, 0], tile_in[0, 0], tile_count[0])
    bias = layer_bias.reshape(1, FEAT)
    order = lax.optimization_barrier

    sources = col_exchange(copies_of(features))
    other = forward(1, lists, values, sources)
    other, lists = order((other, lists))
    mine = forward(0, lists, values, sources)
    recv = row_exchange(pair_sum(mine, to_other_core(other)))
    hidden, grad, total = dense(recv, weight, bias, cotangent)

    grads = row_exchange(grad)
    for bit in (2, 4):
        total = total + partner(total, "col", 8, bit)
    total = total + partner(total, "row", 16, 1)
    total = total + partner(total, "col", 8, 1)
    grads, total = order((grads, total))
    other = to_other_core(grads)
    second = partner(total, "row", 16, 2)
    back = backward(2, lists, values, grads)
    back = backward(3, lists, values, other, back)
    back, second = order((back, second))
    total = total + second
    back = col_exchange(back)
    for bit in (4, 8):
        total = total + partner(total, "row", 16, bit)
    scale = 1.0 / math.sqrt(4 * TILE * 128)
    weight_grad = total[:FEAT] * scale
    bias_grad = total[FEAT] * scale
    back, weight_grad, bias_grad = order((back, weight_grad, bias_grad))
    feature_grad = last(back)
    return (hidden, feature_grad, weight_grad, bias_grad)


def solution(mesh):
    in_specs = (
        P(("row", "col"), None),
        P(),
        P(),
        P(("col", "row"), None),
        P("row", "col", None),
        P("row", "col", None),
        P("row", "col", None, None, None),
        P("row", "col"),
    )
    out_specs = (P(("col", "row"), None), P(("row", "col"), None), P(), P())
    return jax.shard_map(local, mesh=mesh, in_specs=in_specs, out_specs=out_specs, check_vma=False)
```

```python
import functools
import math

import jax
import jax.numpy as jnp
from jax import lax
from jax.experimental import pallas as pl
from jax.experimental.pallas import tpu as pltpu
from jax.sharding import PartitionSpec as P

gelu_coef = 0.7978845608
cube_coef = 0.044715
TILE = 256
FEAT = 128
SLOTS = 128
NPEER = 8
LIST = 160
UNROLL = 8
DEPTH = 32
FWD_DUMMY = 32
BWD_DUMMY = 32
f32, bf16 = jnp.float32, jnp.bfloat16
VMEM_LIMIT = 28 * 2**20


def params():
    return pltpu.CompilerParams(vmem_limit_bytes=VMEM_LIMIT)


def vmem():
    return pl.BlockSpec(memory_space=pltpu.VMEM)


def smem():
    return pl.BlockSpec(memory_space=pltpu.SMEM)


def hbm():
    return pl.BlockSpec(memory_space=pl.ANY)


def prep_kernel(where_ref, out_ref, in_ref, count_ref, lists_ref):
    core = where_ref[0]

    def clear(i, carry):
        lists_ref[i] = FWD_DUMMY << 16
        lists_ref[LIST + i] = FWD_DUMMY << 16
        lists_ref[2 * LIST + i] = BWD_DUMMY << 16
        lists_ref[3 * LIST + i] = BWD_DUMMY << 16
        return carry

    lax.fori_loop(0, LIST, clear, 0)

    def place(k, carry):
        f0, f1 = carry
        t = out_ref[k]
        s = in_ref[k]
        rel = jnp.bitwise_xor((t >> 2) & 1, core)
        to_t = ((t >> 3) << 2) | (t & 3)
        at_f = jnp.where(rel == 0, f0, LIST + f1)
        lists_ref[at_f] = k | (s << 8) | (to_t << 16)
        lists_ref[2 * LIST + at_f] = k | (to_t << 8) | (s << 16)
        return (f0 + 1 - rel, f1 + rel)

    zero = jnp.int32(0)
    sizes = lax.fori_loop(0, count_ref[0], place, (zero, zero))
    lists_ref[4 * LIST] = sizes[0]
    lists_ref[4 * LIST + 1] = sizes[1]


def prep(where, out_index, in_index, count):
    return pl.pallas_call(
        prep_kernel,
        out_shape=jax.ShapeDtypeStruct((1024,), jnp.int32),
        in_specs=[smem()] * 4,
        out_specs=smem(),
        compiler_params=params(),
        name="slot_lists",
    )(where, out_index, in_index, count)


def copies_kernel(value_ref, out_ref, held, in_sem, sems):
    fetch = pltpu.make_async_copy(value_ref, held, in_sem)
    fetch.start()
    fetch.wait()
    copies = [pltpu.make_async_copy(held, out_ref.at[peer], sems.at[peer]) for peer in range(NPEER)]
    for copy in copies:
        copy.start()
    for copy in copies:
        copy.wait()


def copies_of(value):
    return pl.pallas_call(
        copies_kernel,
        out_shape=pltpu.HBM((NPEER, *value.shape), value.dtype),
        in_specs=[hbm()],
        out_specs=hbm(),
        scratch_shapes=[
            pltpu.VMEM(value.shape, value.dtype),
            pltpu.SemaphoreType.DMA,
            pltpu.SemaphoreType.DMA((NPEER,)),
        ],
        compiler_params=params(),
        name="copies",
    )(in_hbm(value))


def tile_loop(which, lists_ref, vals, buf, sems, acc, ready, product):
    base = which * LIST
    groups = (lists_ref[4 * LIST + (which & 1)] + (UNROLL - 1)) // UNROLL
    ahead = DEPTH // UNROLL

    def copy(g, u):
        slot = lists_ref[base + g * UNROLL + u] & 255
        at = lax.rem(g, ahead) * UNROLL + u
        return pltpu.make_async_copy(vals.at[slot], buf.at[at], sems.at[at])

    for g in range(ahead):

        @pl.when(g < groups)
        def _():
            for u in range(UNROLL):
                copy(g, u).start()

    ready()

    def body(g, carry):
        for u in range(UNROLL):
            copy(g, u).wait()
        todo = []
        for u in range(UNROLL):
            entry = lists_ref[base + g * UNROLL + u]
            at = lax.rem(g, ahead) * UNROLL + u
            todo.append((entry >> 16, product(buf[at], (entry >> 8) & 255)))
        for to, value in todo:
            acc[to] += value

        @pl.when(g + ahead < groups)
        def _():
            for u in range(UNROLL):
                copy(g + ahead, u).start()

        return carry

    lax.fori_loop(0, groups, body, 0)


def in_hbm(array):
    return pltpu.with_memory_space_constraint(array, pltpu.HBM)


TILES_COST = pl.CostEstimate(
    flops=2 * 64 * TILE * TILE * FEAT, bytes_accessed=16 * 2**20, transcendentals=0
)


def forward_kernel(which, lists_ref, vals, x, out_ref, buf, acc, sems):
    def ready():
        def clear(i, carry):
            acc[i] = jnp.zeros((TILE, FEAT), f32)
            return carry

        lax.fori_loop(0, FWD_DUMMY, clear, 0)

    def product(tile, source):
        rows = pl.ds(pl.multiple_of((source & 3) * TILE, TILE), TILE)
        return jnp.dot(tile, x[source >> 2, rows, :], preferred_element_type=f32)

    tile_loop(which, lists_ref, vals, buf, sems, acc, ready, product)

    for i in range(4 * NPEER):
        out_ref[i // 4, pl.ds((i % 4) * TILE, TILE), :] = acc[i].astype(bf16)


def forward(which, lists, values, sources):
    return pl.pallas_call(
        functools.partial(forward_kernel, which),
        out_shape=jax.ShapeDtypeStruct((NPEER, 4 * TILE, FEAT), bf16),
        in_specs=[smem(), hbm(), vmem()],
        out_specs=vmem(),
        scratch_shapes=[
            pltpu.VMEM((DEPTH, TILE, TILE), bf16),
            pltpu.VMEM((FWD_DUMMY + 1, TILE, FEAT), f32),
            pltpu.SemaphoreType.DMA((DEPTH,)),
        ],
        compiler_params=params(),
        cost_estimate=TILES_COST,
        name="forward_tiles",
    )(in_hbm(lists), in_hbm(values), sources)


def pair_sum_kernel(mine_ref, other_ref, out_ref):
    for k in range(NPEER):
        out_ref[k] = (mine_ref[k].astype(f32) + other_ref[k].astype(f32)).astype(bf16)


def pair_sum(mine, other):
    return pl.pallas_call(
        pair_sum_kernel,
        out_shape=jax.ShapeDtypeStruct(mine.shape, bf16),
        in_specs=[vmem()] * 2,
        out_specs=vmem(),
        compiler_params=params(),
        cost_estimate=pl.CostEstimate(flops=2**21, bytes_accessed=6 * 2**20, transcendentals=0),
        name="pair_sum",
    )(mine, other)


def backward_kernel(which, lists_ref, vals, g, *rest):
    if which == 2:
        out, buf, acc, sems = rest
    else:
        before, out_ref, buf, acc, sems, out, out_sems = rest

    def ready():
        def clear(i, carry):
            acc[i] = jnp.zeros((FEAT, TILE), f32)
            return carry

        lax.fori_loop(0, BWD_DUMMY, clear, 0)

    def product(tile, source):
        rows = pl.ds(pl.multiple_of((source & 3) * FEAT, FEAT), FEAT)
        return jnp.dot(g[source >> 2, rows, :], tile, preferred_element_type=f32)

    tile_loop(which, lists_ref, vals, buf, sems, acc, ready, product)

    copies = []
    for i in range(4 * NPEER):
        peer, rows = i // 4, pl.ds((i % 4) * FEAT, FEAT)
        if which == 2:
            out[peer, rows, :] = acc[i].astype(bf16)
        else:
            out[peer, rows, :] = (acc[i] + before[peer, rows, :].astype(f32)).astype(bf16)
            if i % 4 == 3:
                copies.append(
                    pltpu.make_async_copy(out.at[peer], out_ref.at[peer], out_sems.at[peer])
                )
                copies[-1].start()
    for copy in copies:
        copy.wait()


def backward(which, lists, values, *blocks):
    shape = (NPEER, 4 * FEAT, TILE)
    scratch = [
        pltpu.VMEM((DEPTH, TILE, TILE), bf16),
        pltpu.VMEM((BWD_DUMMY + 1, FEAT, TILE), f32),
        pltpu.SemaphoreType.DMA((DEPTH,)),
    ]
    if which == 3:
        scratch += [pltpu.VMEM(shape, bf16), pltpu.SemaphoreType.DMA((NPEER,))]
    return pl.pallas_call(
        functools.partial(backward_kernel, which),
        out_shape=jax.ShapeDtypeStruct(shape, bf16) if which == 2 else pltpu.HBM(shape, bf16),
        in_specs=[smem(), hbm()] + [vmem()] * len(blocks),
        out_specs=vmem() if which == 2 else hbm(),
        scratch_shapes=scratch,
        compiler_params=params(),
        cost_estimate=TILES_COST,
        name="backward_tiles",
    )(in_hbm(lists), in_hbm(values), *blocks)


def dense_kernel(
    recv_ref, weight_ref, bias_ref, cot_ref, hidden_ref, grad_ref, wsum_ref, one, sems
):
    copies = []
    weight = weight_ref[...]
    for part in range(4):
        here = pl.ds(part * TILE, TILE)
        total = recv_ref[0, here, :].astype(f32)
        for peer in range(1, NPEER):
            total += recv_ref[peer, here, :].astype(f32)
        agg = total.astype(bf16)
        v = jnp.dot(agg, weight, preferred_element_type=f32) + bias_ref[...]
        s = jnp.tanh(gelu_coef * (v + cube_coef * v * v * v))
        hidden_ref[here, :] = (0.5 * v * (1.0 + s)).astype(bf16)
        slope = 0.5 * (1.0 + s) + 0.5 * v * (1.0 - s * s) * gelu_coef * (
            1.0 + 3.0 * cube_coef * v * v
        )
        grad = (cot_ref[here, :].astype(f32) * slope).astype(bf16)
        wsum = lax.dot_general(agg, grad, (((0,), (0,)), ((), ())), preferred_element_type=f32)
        bsum = jnp.dot(jnp.ones((16, TILE), bf16), grad, preferred_element_type=f32)[:8]
        back = lax.dot_general(weight, grad, (((1,), (1,)), ((), ())), preferred_element_type=f32)
        back = back.astype(bf16)
        rows = pl.ds(part * FEAT, FEAT)
        one[rows, :] = back
        for peer in range(NPEER):
            copies.append(
                pltpu.make_async_copy(
                    one.at[rows], grad_ref.at[peer, rows], sems.at[part * NPEER + peer]
                )
            )
            copies[-1].start()
        if part == 0:
            wsum_ref[pl.ds(0, FEAT), :] = wsum
            wsum_ref[pl.ds(FEAT, 8), :] = bsum
        else:
            wsum_ref[pl.ds(0, FEAT), :] += wsum
            wsum_ref[pl.ds(FEAT, 8), :] += bsum
    for copy in copies:
        copy.wait()


def dense(recv, weight, bias, cotangent):
    return pl.pallas_call(
        dense_kernel,
        out_shape=(
            jax.ShapeDtypeStruct((4 * TILE, FEAT), bf16),
            pltpu.HBM((NPEER, 4 * FEAT, TILE), bf16),
            jax.ShapeDtypeStruct((FEAT + 8, FEAT), f32),
        ),
        in_specs=[vmem()] * 4,
        out_specs=(vmem(), hbm(), vmem()),
        scratch_shapes=[
            pltpu.VMEM((4 * FEAT, TILE), bf16),
            pltpu.SemaphoreType.DMA((4 * NPEER,)),
        ],
        compiler_params=params(),
        cost_estimate=pl.CostEstimate(
            flops=6 * 1024 * FEAT * FEAT, bytes_accessed=5 * 2**20, transcendentals=1024 * FEAT
        ),
        name="dense_layer",
    )(recv, weight, bias, cotangent)


def last_kernel(recv_ref, grad_ref):
    for sub in range(4):
        rows = pl.ds(sub * FEAT, FEAT)
        total = recv_ref[0, rows, :].astype(f32)
        for peer in range(1, NPEER):
            total += recv_ref[peer, rows, :].astype(f32)
        grad_ref[pl.ds(sub * TILE, TILE), :] = total.T.astype(bf16)


def last(recv):
    return pl.pallas_call(
        last_kernel,
        out_shape=jax.ShapeDtypeStruct((4 * TILE, FEAT), bf16),
        in_specs=[vmem()],
        out_specs=vmem(),
        compiler_params=params(),
        cost_estimate=pl.CostEstimate(flops=2**20, bytes_accessed=3 * 2**20, transcendentals=0),
        name="last_sum",
    )(recv)


SAME_CORE = [[2 * j + core for j in range(NPEER)] for core in range(2)]
OTHER_CORE = [(r, r ^ 1) for r in range(16)]


def to_other_core(value):
    return lax.ppermute(value, "row", OTHER_CORE)


def row_exchange(value):
    return lax.all_to_all(value, "row", 0, 0, axis_index_groups=SAME_CORE)


def col_exchange(value):
    return lax.all_to_all(value, "col", 0, 0)


def partner(value, axis, size, bit):
    return lax.ppermute(value, axis, [(i, i ^ bit) for i in range(size)])


def local(features, weight, layer_bias, cotangent, tile_out, tile_in, tile_vals, tile_count):
    values = tile_vals[0, 0]
    where = (lax.axis_index("row") & 1).astype(jnp.int32).reshape(1)
    lists = prep(where, tile_out[0, 0], tile_in[0, 0], tile_count[0])
    bias = layer_bias.reshape(1, FEAT)
    order = lax.optimization_barrier

    sources = col_exchange(copies_of(features))
    other = forward(1, lists, values, sources)
    other, lists = order((other, lists))
    mine = forward(0, lists, values, sources)
    recv = row_exchange(pair_sum(mine, to_other_core(other)))
    hidden, grad, total = dense(recv, weight, bias, cotangent)

    grads = row_exchange(grad)
    for bit in (2, 4):
        total = total + partner(total, "col", 8, bit)
    total = total + partner(total, "row", 16, 1)
    total = total + partner(total, "col", 8, 1)
    grads, total = order((grads, total))
    other = to_other_core(grads)
    second = partner(total, "row", 16, 2)
    back = backward(2, lists, values, grads)
    back = backward(3, lists, values, other, back)
    back, second = order((back, second))
    total = total + second
    back = col_exchange(back)
    for bit in (4, 8):
        total = total + partner(total, "row", 16, bit)
    scale = 1.0 / math.sqrt(4 * TILE * 128)
    weight_grad = total[:FEAT] * scale
    bias_grad = total[FEAT] * scale
    back, weight_grad, bias_grad = order((back, weight_grad, bias_grad))
    feature_grad = last(back)
    return (hidden, feature_grad, weight_grad, bias_grad)


def solution(mesh):
    in_specs = (
        P(("row", "col"), None),
        P(),
        P(),
        P(("col", "row"), None),
        P("row", "col", None),
        P("row", "col", None),
        P("row", "col", None, None, None),
        P("row", "col"),
    )
    out_specs = (P(("col", "row"), None), P(("row", "col"), None), P(), P())
    return jax.shard_map(local, mesh=mesh, in_specs=in_specs, out_specs=out_specs, check_vma=False)
```

```python
import functools
import math

import jax
import jax.numpy as jnp
from jax import lax
from jax.experimental import pallas as pl
from jax.experimental.pallas import tpu as pltpu
from jax.sharding import PartitionSpec as P

gelu_coef = 0.7978845608
cube_coef = 0.044715
TILE = 256
FEAT = 128
SLOTS = 128
NPEER = 8
LIST = 160
UNROLL = 8
DEPTH = 32
FWD_DUMMY = 32
BWD_DUMMY = 32
f32, bf16 = jnp.float32, jnp.bfloat16
VMEM_LIMIT = 28 * 2**20


def params():
    return pltpu.CompilerParams(vmem_limit_bytes=VMEM_LIMIT)


def vmem():
    return pl.BlockSpec(memory_space=pltpu.VMEM)


def smem():
    return pl.BlockSpec(memory_space=pltpu.SMEM)


def hbm():
    return pl.BlockSpec(memory_space=pl.ANY)


def prep_kernel(where_ref, out_ref, in_ref, count_ref, lists_ref):
    core = where_ref[0]

    def clear(i, carry):
        lists_ref[i] = FWD_DUMMY << 16
        lists_ref[LIST + i] = FWD_DUMMY << 16
        lists_ref[2 * LIST + i] = BWD_DUMMY << 16
        lists_ref[3 * LIST + i] = BWD_DUMMY << 16
        return carry

    lax.fori_loop(0, LIST, clear, 0)

    def place(k, carry):
        f0, f1 = carry
        t = out_ref[k]
        s = in_ref[k]
        rel = jnp.bitwise_xor((t >> 2) & 1, core)
        to_t = ((t >> 3) << 2) | (t & 3)
        at_f = jnp.where(rel == 0, f0, LIST + f1)
        lists_ref[at_f] = k | (s << 8) | (to_t << 16)
        lists_ref[2 * LIST + at_f] = k | (to_t << 8) | (s << 16)
        return (f0 + 1 - rel, f1 + rel)

    zero = jnp.int32(0)
    sizes = lax.fori_loop(0, count_ref[0], place, (zero, zero))
    lists_ref[4 * LIST] = sizes[0]
    lists_ref[4 * LIST + 1] = sizes[1]


def prep(where, out_index, in_index, count):
    return pl.pallas_call(
        prep_kernel,
        out_shape=pltpu.SMEM((1024,), jnp.int32),
        in_specs=[smem()] * 4,
        out_specs=smem(),
        compiler_params=params(),
        name="slot_lists",
    )(where, out_index, in_index, count)


def copies_kernel(value_ref, out_ref, held, in_sem, sems):
    fetch = pltpu.make_async_copy(value_ref, held, in_sem)
    fetch.start()
    fetch.wait()
    copies = [pltpu.make_async_copy(held, out_ref.at[peer], sems.at[peer]) for peer in range(NPEER)]
    for copy in copies:
        copy.start()
    for copy in copies:
        copy.wait()


def copies_of(value):
    return pl.pallas_call(
        copies_kernel,
        out_shape=pltpu.HBM((NPEER, *value.shape), value.dtype),
        in_specs=[hbm()],
        out_specs=hbm(),
        scratch_shapes=[
            pltpu.VMEM(value.shape, value.dtype),
            pltpu.SemaphoreType.DMA,
            pltpu.SemaphoreType.DMA((NPEER,)),
        ],
        compiler_params=params(),
        name="copies",
    )(in_hbm(value))


def tile_loop(which, lists_ref, vals, buf, sems, acc, ready, product):
    base = which * LIST
    groups = (lists_ref[4 * LIST + (which & 1)] + (UNROLL - 1)) // UNROLL
    ahead = DEPTH // UNROLL

    def copy(g, u):
        slot = lists_ref[base + g * UNROLL + u] & 255
        at = lax.rem(g, ahead) * UNROLL + u
        return pltpu.make_async_copy(vals.at[slot], buf.at[at], sems.at[at])

    for g in range(ahead):

        @pl.when(g < groups)
        def _():
            for u in range(UNROLL):
                copy(g, u).start()

    ready()

    def body(g, carry):
        for u in range(UNROLL):
            copy(g, u).wait()
        todo = []
        for u in range(UNROLL):
            entry = lists_ref[base + g * UNROLL + u]
            at = lax.rem(g, ahead) * UNROLL + u
            todo.append((entry >> 16, product(buf[at], (entry >> 8) & 255)))
        for to, value in todo:
            acc[to] += value

        @pl.when(g + ahead < groups)
        def _():
            for u in range(UNROLL):
                copy(g + ahead, u).start()

        return carry

    lax.fori_loop(0, groups, body, 0)


def in_smem(array):
    return pltpu.with_memory_space_constraint(array, pltpu.SMEM)


def in_hbm(array):
    return pltpu.with_memory_space_constraint(array, pltpu.HBM)


TILES_COST = pl.CostEstimate(
    flops=2 * 64 * TILE * TILE * FEAT, bytes_accessed=16 * 2**20, transcendentals=0
)


def forward_kernel(which, lists_ref, vals, x, out_ref, buf, acc, sems):
    def ready():
        def clear(i, carry):
            acc[i] = jnp.zeros((TILE, FEAT), f32)
            return carry

        lax.fori_loop(0, FWD_DUMMY, clear, 0)

    def product(tile, source):
        rows = pl.ds(pl.multiple_of((source & 3) * TILE, TILE), TILE)
        return jnp.dot(tile, x[source >> 2, rows, :], preferred_element_type=f32)

    tile_loop(which, lists_ref, vals, buf, sems, acc, ready, product)

    for i in range(4 * NPEER):
        out_ref[i // 4, pl.ds((i % 4) * TILE, TILE), :] = acc[i].astype(bf16)


def forward(which, lists, values, sources):
    return pl.pallas_call(
        functools.partial(forward_kernel, which),
        out_shape=jax.ShapeDtypeStruct((NPEER, 4 * TILE, FEAT), bf16),
        in_specs=[smem(), hbm(), vmem()],
        out_specs=vmem(),
        scratch_shapes=[
            pltpu.VMEM((DEPTH, TILE, TILE), bf16),
            pltpu.VMEM((FWD_DUMMY + 1, TILE, FEAT), f32),
            pltpu.SemaphoreType.DMA((DEPTH,)),
        ],
        compiler_params=params(),
        cost_estimate=TILES_COST,
        name="forward_tiles",
    )(in_smem(lists), in_hbm(values), sources)


def pair_sum_kernel(mine_ref, other_ref, out_ref):
    for k in range(NPEER):
        out_ref[k] = (mine_ref[k].astype(f32) + other_ref[k].astype(f32)).astype(bf16)


def pair_sum(mine, other):
    return pl.pallas_call(
        pair_sum_kernel,
        out_shape=jax.ShapeDtypeStruct(mine.shape, bf16),
        in_specs=[vmem()] * 2,
        out_specs=vmem(),
        compiler_params=params(),
        cost_estimate=pl.CostEstimate(flops=2**21, bytes_accessed=6 * 2**20, transcendentals=0),
        name="pair_sum",
    )(mine, other)


def backward_kernel(which, lists_ref, vals, g, *rest):
    if which == 2:
        out, buf, acc, sems = rest
    else:
        before, out_ref, buf, acc, sems, out, out_sems = rest

    def ready():
        def clear(i, carry):
            acc[i] = jnp.zeros((FEAT, TILE), f32)
            return carry

        lax.fori_loop(0, BWD_DUMMY, clear, 0)

    def product(tile, source):
        rows = pl.ds(pl.multiple_of((source & 3) * FEAT, FEAT), FEAT)
        return jnp.dot(g[source >> 2, rows, :], tile, preferred_element_type=f32)

    tile_loop(which, lists_ref, vals, buf, sems, acc, ready, product)

    copies = []
    for i in range(4 * NPEER):
        peer, rows = i // 4, pl.ds((i % 4) * FEAT, FEAT)
        if which == 2:
            out[peer, rows, :] = acc[i].astype(bf16)
        else:
            out[peer, rows, :] = (acc[i] + before[peer, rows, :].astype(f32)).astype(bf16)
            if i % 4 == 3:
                copies.append(
                    pltpu.make_async_copy(out.at[peer], out_ref.at[peer], out_sems.at[peer])
                )
                copies[-1].start()
    for copy in copies:
        copy.wait()


def backward(which, lists, values, *blocks):
    shape = (NPEER, 4 * FEAT, TILE)
    scratch = [
        pltpu.VMEM((DEPTH, TILE, TILE), bf16),
        pltpu.VMEM((BWD_DUMMY + 1, FEAT, TILE), f32),
        pltpu.SemaphoreType.DMA((DEPTH,)),
    ]
    if which == 3:
        scratch += [pltpu.VMEM(shape, bf16), pltpu.SemaphoreType.DMA((NPEER,))]
    return pl.pallas_call(
        functools.partial(backward_kernel, which),
        out_shape=jax.ShapeDtypeStruct(shape, bf16) if which == 2 else pltpu.HBM(shape, bf16),
        in_specs=[smem(), hbm()] + [vmem()] * len(blocks),
        out_specs=vmem() if which == 2 else hbm(),
        scratch_shapes=scratch,
        compiler_params=params(),
        cost_estimate=TILES_COST,
        name="backward_tiles",
    )(in_smem(lists), in_hbm(values), *blocks)


def dense_kernel(
    recv_ref, weight_ref, bias_ref, cot_ref, hidden_ref, grad_ref, wsum_ref, one, sems
):
    copies = []
    weight = weight_ref[...]
    for part in range(4):
        here = pl.ds(part * TILE, TILE)
        total = recv_ref[0, here, :].astype(f32)
        for peer in range(1, NPEER):
            total += recv_ref[peer, here, :].astype(f32)
        agg = total.astype(bf16)
        v = jnp.dot(agg, weight, preferred_element_type=f32) + bias_ref[...]
        s = jnp.tanh(gelu_coef * (v + cube_coef * v * v * v))
        hidden_ref[here, :] = (0.5 * v * (1.0 + s)).astype(bf16)
        slope = 0.5 * (1.0 + s) + 0.5 * v * (1.0 - s * s) * gelu_coef * (
            1.0 + 3.0 * cube_coef * v * v
        )
        grad = (cot_ref[here, :].astype(f32) * slope).astype(bf16)
        wsum = lax.dot_general(agg, grad, (((0,), (0,)), ((), ())), preferred_element_type=f32)
        bsum = jnp.dot(jnp.ones((16, TILE), bf16), grad, preferred_element_type=f32)[:8]
        back = lax.dot_general(weight, grad, (((1,), (1,)), ((), ())), preferred_element_type=f32)
        back = back.astype(bf16)
        rows = pl.ds(part * FEAT, FEAT)
        one[rows, :] = back
        for peer in range(NPEER):
            copies.append(
                pltpu.make_async_copy(
                    one.at[rows], grad_ref.at[peer, rows], sems.at[part * NPEER + peer]
                )
            )
            copies[-1].start()
        if part == 0:
            wsum_ref[pl.ds(0, FEAT), :] = wsum
            wsum_ref[pl.ds(FEAT, 8), :] = bsum
        else:
            wsum_ref[pl.ds(0, FEAT), :] += wsum
            wsum_ref[pl.ds(FEAT, 8), :] += bsum
    for copy in copies:
        copy.wait()


def dense(recv, weight, bias, cotangent):
    return pl.pallas_call(
        dense_kernel,
        out_shape=(
            jax.ShapeDtypeStruct((4 * TILE, FEAT), bf16),
            pltpu.HBM((NPEER, 4 * FEAT, TILE), bf16),
            jax.ShapeDtypeStruct((FEAT + 8, FEAT), f32),
        ),
        in_specs=[vmem()] * 4,
        out_specs=(vmem(), hbm(), vmem()),
        scratch_shapes=[
            pltpu.VMEM((4 * FEAT, TILE), bf16),
            pltpu.SemaphoreType.DMA((4 * NPEER,)),
        ],
        compiler_params=params(),
        cost_estimate=pl.CostEstimate(
            flops=6 * 1024 * FEAT * FEAT, bytes_accessed=5 * 2**20, transcendentals=1024 * FEAT
        ),
        name="dense_layer",
    )(recv, weight, bias, cotangent)


def last_kernel(recv_ref, grad_ref):
    for sub in range(4):
        rows = pl.ds(sub * FEAT, FEAT)
        total = recv_ref[0, rows, :].astype(f32)
        for peer in range(1, NPEER):
            total += recv_ref[peer, rows, :].astype(f32)
        grad_ref[pl.ds(sub * TILE, TILE), :] = total.T.astype(bf16)


def last(recv):
    return pl.pallas_call(
        last_kernel,
        out_shape=jax.ShapeDtypeStruct((4 * TILE, FEAT), bf16),
        in_specs=[vmem()],
        out_specs=vmem(),
        compiler_params=params(),
        cost_estimate=pl.CostEstimate(flops=2**20, bytes_accessed=3 * 2**20, transcendentals=0),
        name="last_sum",
    )(recv)


SAME_CORE = [[2 * j + core for j in range(NPEER)] for core in range(2)]
OTHER_CORE = [(r, r ^ 1) for r in range(16)]


def to_other_core(value):
    return lax.ppermute(value, "row", OTHER_CORE)


def row_exchange(value):
    return lax.all_to_all(value, "row", 0, 0, axis_index_groups=SAME_CORE)


def col_exchange(value):
    return lax.all_to_all(value, "col", 0, 0)


def partner(value, axis, size, bit):
    return lax.ppermute(value, axis, [(i, i ^ bit) for i in range(size)])


def local(features, weight, layer_bias, cotangent, tile_out, tile_in, tile_vals, tile_count):
    values = tile_vals[0, 0]
    where = (lax.axis_index("row") & 1).astype(jnp.int32).reshape(1)
    lists = prep(where, tile_out[0, 0], tile_in[0, 0], tile_count[0])
    bias = layer_bias.reshape(1, FEAT)
    order = lax.optimization_barrier

    sources = col_exchange(copies_of(features))
    other = forward(1, lists, values, sources)
    other, lists = order((other, lists))
    mine = forward(0, lists, values, sources)
    recv = row_exchange(pair_sum(mine, to_other_core(other)))
    hidden, grad, total = dense(recv, weight, bias, cotangent)

    grads = row_exchange(grad)
    for bit in (2, 4):
        total = total + partner(total, "col", 8, bit)
    total = total + partner(total, "row", 16, 1)
    total = total + partner(total, "col", 8, 1)
    grads, total = order((grads, total))
    other = to_other_core(grads)
    second = partner(total, "row", 16, 2)
    back = backward(2, lists, values, grads)
    back = backward(3, lists, values, other, back)
    back, second = order((back, second))
    total = total + second
    back = col_exchange(back)
    for bit in (4, 8):
        total = total + partner(total, "row", 16, bit)
    scale = 1.0 / math.sqrt(4 * TILE * 128)
    weight_grad = total[:FEAT] * scale
    bias_grad = total[FEAT] * scale
    back, weight_grad, bias_grad = order((back, weight_grad, bias_grad))
    feature_grad = last(back)
    return (hidden, feature_grad, weight_grad, bias_grad)


def solution(mesh):
    in_specs = (
        P(("row", "col"), None),
        P(),
        P(),
        P(("col", "row"), None),
        P("row", "col", None),
        P("row", "col", None),
        P("row", "col", None, None, None),
        P("row", "col"),
    )
    out_specs = (P(("col", "row"), None), P(("row", "col"), None), P(), P())
    return jax.shard_map(local, mesh=mesh, in_specs=in_specs, out_specs=out_specs, check_vma=False)
```

```python
import functools
import math

import jax
import jax.numpy as jnp
from jax import lax
from jax.experimental import pallas as pl
from jax.experimental.pallas import tpu as pltpu
from jax.sharding import PartitionSpec as P

gelu_coef = 0.7978845608
cube_coef = 0.044715
TILE = 256
FEAT = 128
SLOTS = 128
NPEER = 8
LIST = 160
UNROLL = 8
DEPTH = 32
FWD_DUMMY = 32
BWD_DUMMY = 32
f32, bf16 = jnp.float32, jnp.bfloat16
VMEM_LIMIT = 28 * 2**20


def params():
    return pltpu.CompilerParams(vmem_limit_bytes=VMEM_LIMIT)


def vmem():
    return pl.BlockSpec(memory_space=pltpu.VMEM)


def smem():
    return pl.BlockSpec(memory_space=pltpu.SMEM)


def hbm():
    return pl.BlockSpec(memory_space=pl.ANY)


def prep_kernel(where_ref, out_ref, in_ref, count_ref, lists_ref):
    core = where_ref[0]

    def clear(i, carry):
        lists_ref[i] = FWD_DUMMY << 16
        lists_ref[LIST + i] = FWD_DUMMY << 16
        lists_ref[2 * LIST + i] = BWD_DUMMY << 16
        lists_ref[3 * LIST + i] = BWD_DUMMY << 16
        return carry

    lax.fori_loop(0, LIST, clear, 0)

    def place(k, carry):
        f0, f1 = carry
        t = out_ref[k]
        s = in_ref[k]
        rel = jnp.bitwise_xor((t >> 2) & 1, core)
        to_t = ((t >> 3) << 2) | (t & 3)
        at_f = jnp.where(rel == 0, f0, LIST + f1)
        lists_ref[at_f] = k | (s << 8) | (to_t << 16)
        lists_ref[2 * LIST + at_f] = k | (to_t << 8) | (s << 16)
        return (f0 + 1 - rel, f1 + rel)

    zero = jnp.int32(0)
    sizes = lax.fori_loop(0, count_ref[0], place, (zero, zero))
    lists_ref[4 * LIST] = sizes[0]
    lists_ref[4 * LIST + 1] = sizes[1]


def prep(where, out_index, in_index, count):
    return pl.pallas_call(
        prep_kernel,
        out_shape=pltpu.SMEM((1024,), jnp.int32),
        in_specs=[smem()] * 4,
        out_specs=smem(),
        compiler_params=params(),
        name="slot_lists",
    )(where, out_index, in_index, count)


def copies_kernel(value_ref, out_ref, held, in_sem, sems):
    fetch = pltpu.make_async_copy(value_ref, held, in_sem)
    fetch.start()
    fetch.wait()
    copies = [pltpu.make_async_copy(held, out_ref.at[peer], sems.at[peer]) for peer in range(NPEER)]
    for copy in copies:
        copy.start()
    for copy in copies:
        copy.wait()


def copies_of(value):
    return pl.pallas_call(
        copies_kernel,
        out_shape=pltpu.HBM((NPEER, *value.shape), value.dtype),
        in_specs=[hbm()],
        out_specs=hbm(),
        scratch_shapes=[
            pltpu.VMEM(value.shape, value.dtype),
            pltpu.SemaphoreType.DMA,
            pltpu.SemaphoreType.DMA((NPEER,)),
        ],
        compiler_params=params(),
        name="copies",
    )(in_hbm(value))


def tile_loop(which, lists_ref, vals, buf, sems, acc, ready, product):
    base = which * LIST
    groups = (lists_ref[4 * LIST + (which & 1)] + (UNROLL - 1)) // UNROLL
    ahead = DEPTH // UNROLL

    def copy(g, u):
        slot = lists_ref[base + g * UNROLL + u] & 255
        at = lax.rem(g, ahead) * UNROLL + u
        return pltpu.make_async_copy(vals.at[slot], buf.at[at], sems.at[at])

    for g in range(ahead):

        @pl.when(g < groups)
        def _():
            for u in range(UNROLL):
                copy(g, u).start()

    ready()

    def body(g, carry):
        for u in range(UNROLL):
            copy(g, u).wait()
        todo = []
        for u in range(UNROLL):
            entry = lists_ref[base + g * UNROLL + u]
            at = lax.rem(g, ahead) * UNROLL + u
            todo.append((entry >> 16, product(buf[at], (entry >> 8) & 255)))
        for to, value in todo:
            acc[to] += value

        @pl.when(g + ahead < groups)
        def _():
            for u in range(UNROLL):
                copy(g + ahead, u).start()

        return carry

    lax.fori_loop(0, groups, body, 0)


def in_smem(array):
    return pltpu.with_memory_space_constraint(array, pltpu.SMEM)


def in_hbm(array):
    return pltpu.with_memory_space_constraint(array, pltpu.HBM)


TILES_COST = pl.CostEstimate(
    flops=2 * 64 * TILE * TILE * FEAT, bytes_accessed=16 * 2**20, transcendentals=0
)


def forward_kernel(which, lists_ref, vals, x, out_ref, buf, acc, sems):
    def ready():
        def clear(i, carry):
            acc[i] = jnp.zeros((TILE, FEAT), f32)
            return carry

        lax.fori_loop(0, FWD_DUMMY, clear, 0)

    def product(tile, source):
        rows = pl.ds(pl.multiple_of((source & 3) * TILE, TILE), TILE)
        return jnp.dot(tile, x[source >> 2, rows, :], preferred_element_type=f32)

    tile_loop(which, lists_ref, vals, buf, sems, acc, ready, product)

    for i in range(4 * NPEER):
        out_ref[i // 4, pl.ds((i % 4) * TILE, TILE), :] = acc[i].astype(bf16)


def forward(which, lists, values, sources):
    return pl.pallas_call(
        functools.partial(forward_kernel, which),
        out_shape=jax.ShapeDtypeStruct((NPEER, 4 * TILE, FEAT), bf16),
        in_specs=[smem(), hbm(), vmem()],
        out_specs=vmem(),
        scratch_shapes=[
            pltpu.VMEM((DEPTH, TILE, TILE), bf16),
            pltpu.VMEM((FWD_DUMMY + 1, TILE, FEAT), f32),
            pltpu.SemaphoreType.DMA((DEPTH,)),
        ],
        compiler_params=params(),
        cost_estimate=TILES_COST,
        name="forward_tiles",
    )(in_smem(lists), in_hbm(values), sources)


def pair_sum_kernel(mine_ref, other_ref, out_ref):
    for k in range(NPEER):
        out_ref[k] = (mine_ref[k].astype(f32) + other_ref[k].astype(f32)).astype(bf16)


def pair_sum(mine, other):
    return pl.pallas_call(
        pair_sum_kernel,
        out_shape=jax.ShapeDtypeStruct(mine.shape, bf16),
        in_specs=[vmem()] * 2,
        out_specs=vmem(),
        compiler_params=params(),
        cost_estimate=pl.CostEstimate(flops=2**21, bytes_accessed=6 * 2**20, transcendentals=0),
        name="pair_sum",
    )(mine, other)


def backward_kernel(which, lists_ref, vals, g, *rest):
    if which == 2:
        out, buf, acc, sems = rest
    else:
        before, out_ref, buf, acc, sems, out, out_sems = rest

    def ready():
        def clear(i, carry):
            acc[i] = jnp.zeros((FEAT, TILE), f32)
            return carry

        lax.fori_loop(0, BWD_DUMMY, clear, 0)

    def product(tile, source):
        rows = pl.ds(pl.multiple_of((source & 3) * FEAT, FEAT), FEAT)
        return jnp.dot(g[source >> 2, rows, :], tile, preferred_element_type=f32)

    tile_loop(which, lists_ref, vals, buf, sems, acc, ready, product)

    copies = []
    for i in range(4 * NPEER):
        peer, rows = i // 4, pl.ds((i % 4) * FEAT, FEAT)
        if which == 2:
            out[peer, rows, :] = acc[i].astype(bf16)
        else:
            out[peer, rows, :] = (acc[i] + before[peer, rows, :].astype(f32)).astype(bf16)
            if i % 4 == 3:
                copies.append(
                    pltpu.make_async_copy(out.at[peer], out_ref.at[peer], out_sems.at[peer])
                )
                copies[-1].start()
    for copy in copies:
        copy.wait()


def backward(which, lists, values, *blocks):
    shape = (NPEER, 4 * FEAT, TILE)
    scratch = [
        pltpu.VMEM((DEPTH, TILE, TILE), bf16),
        pltpu.VMEM((BWD_DUMMY + 1, FEAT, TILE), f32),
        pltpu.SemaphoreType.DMA((DEPTH,)),
    ]
    if which == 3:
        scratch += [pltpu.VMEM(shape, bf16), pltpu.SemaphoreType.DMA((NPEER,))]
    return pl.pallas_call(
        functools.partial(backward_kernel, which),
        out_shape=jax.ShapeDtypeStruct(shape, bf16) if which == 2 else pltpu.HBM(shape, bf16),
        in_specs=[smem(), hbm()] + [vmem()] * len(blocks),
        out_specs=vmem() if which == 2 else hbm(),
        scratch_shapes=scratch,
        compiler_params=params(),
        cost_estimate=TILES_COST,
        name="backward_tiles",
    )(in_smem(lists), in_hbm(values), *blocks)


def dense_kernel(
    recv_ref, weight_ref, bias_ref, cot_ref, hidden_ref, grad_ref, wsum_ref, one, sems
):
    copies = []
    weight = weight_ref[...]
    for part in range(4):
        here = pl.ds(part * TILE, TILE)
        total = recv_ref[0, here, :].astype(f32)
        for peer in range(1, NPEER):
            total += recv_ref[peer, here, :].astype(f32)
        agg = total.astype(bf16)
        v = jnp.dot(agg, weight, preferred_element_type=f32) + bias_ref[...]
        s = jnp.tanh(gelu_coef * (v + cube_coef * v * v * v))
        hidden_ref[here, :] = (0.5 * v * (1.0 + s)).astype(bf16)
        slope = 0.5 * (1.0 + s) + 0.5 * v * (1.0 - s * s) * gelu_coef * (
            1.0 + 3.0 * cube_coef * v * v
        )
        grad = (cot_ref[here, :].astype(f32) * slope).astype(bf16)
        wsum = lax.dot_general(agg, grad, (((0,), (0,)), ((), ())), preferred_element_type=f32)
        bsum = jnp.dot(jnp.ones((16, TILE), bf16), grad, preferred_element_type=f32)[:8]
        back = lax.dot_general(weight, grad, (((1,), (1,)), ((), ())), preferred_element_type=f32)
        back = back.astype(bf16)
        rows = pl.ds(part * FEAT, FEAT)
        one[rows, :] = back
        for peer in range(NPEER):
            copies.append(
                pltpu.make_async_copy(
                    one.at[rows], grad_ref.at[peer, rows], sems.at[part * NPEER + peer]
                )
            )
            copies[-1].start()
        if part == 0:
            wsum_ref[pl.ds(0, FEAT), :] = wsum
            wsum_ref[pl.ds(FEAT, 8), :] = bsum
        else:
            wsum_ref[pl.ds(0, FEAT), :] += wsum
            wsum_ref[pl.ds(FEAT, 8), :] += bsum
    for copy in copies:
        copy.wait()


def dense(recv, weight, bias, cotangent):
    return pl.pallas_call(
        dense_kernel,
        out_shape=(
            jax.ShapeDtypeStruct((4 * TILE, FEAT), bf16),
            pltpu.HBM((NPEER, 4 * FEAT, TILE), bf16),
            jax.ShapeDtypeStruct((FEAT + 8, FEAT), f32),
        ),
        in_specs=[vmem()] * 4,
        out_specs=(vmem(), hbm(), vmem()),
        scratch_shapes=[
            pltpu.VMEM((4 * FEAT, TILE), bf16),
            pltpu.SemaphoreType.DMA((4 * NPEER,)),
        ],
        compiler_params=params(),
        cost_estimate=pl.CostEstimate(
            flops=6 * 1024 * FEAT * FEAT, bytes_accessed=5 * 2**20, transcendentals=1024 * FEAT
        ),
        name="dense_layer",
    )(recv, weight, bias, cotangent)


def last_kernel(recv_ref, grad_ref):
    for sub in range(4):
        rows = pl.ds(sub * FEAT, FEAT)
        total = recv_ref[0, rows, :].astype(f32)
        for peer in range(1, NPEER):
            total += recv_ref[peer, rows, :].astype(f32)
        grad_ref[pl.ds(sub * TILE, TILE), :] = total.T.astype(bf16)


def last(recv):
    return pl.pallas_call(
        last_kernel,
        out_shape=jax.ShapeDtypeStruct((4 * TILE, FEAT), bf16),
        in_specs=[vmem()],
        out_specs=vmem(),
        compiler_params=params(),
        cost_estimate=pl.CostEstimate(flops=2**20, bytes_accessed=3 * 2**20, transcendentals=0),
        name="last_sum",
    )(recv)


SAME_CORE = [[2 * j + core for j in range(NPEER)] for core in range(2)]
OTHER_CORE = [(r, r ^ 1) for r in range(16)]


def to_other_core(value):
    return lax.ppermute(value, "row", OTHER_CORE)


def row_exchange(value):
    return lax.all_to_all(value, "row", 0, 0, axis_index_groups=SAME_CORE)


def col_exchange(value):
    return lax.all_to_all(value, "col", 0, 0)


def partner(value, axis, size, bit):
    return lax.ppermute(value, axis, [(i, i ^ bit) for i in range(size)])


def local(features, weight, layer_bias, cotangent, tile_out, tile_in, tile_vals, tile_count):
    values = tile_vals[0, 0]
    where = (lax.axis_index("row") & 1).astype(jnp.int32).reshape(1)
    lists = prep(where, tile_out[0, 0], tile_in[0, 0], tile_count[0])
    bias = layer_bias.reshape(1, FEAT)
    order = lax.optimization_barrier

    sources = col_exchange(copies_of(features))
    other = forward(1, lists, values, sources)
    other, lists = order((other, lists))
    mine = forward(0, lists, values, sources)
    recv = row_exchange(pair_sum(mine, to_other_core(other)))
    hidden, grad, total = dense(recv, weight, bias, cotangent)

    grads = row_exchange(grad)
    for bit in (2, 4):
        total = total + partner(total, "col", 8, bit)
    total = total + partner(total, "row", 16, 1)
    both = [(r * 8 + c, (r ^ 2) * 8 + (c ^ 1)) for r in range(16) for c in range(8)]
    near, far = partner(total, "col", 8, 1), partner(total, "row", 16, 2)
    total = (total + near) + (far + lax.ppermute(total, ("row", "col"), both))
    grads, total = order((grads, total))
    other = to_other_core(grads)
    back = backward(2, lists, values, grads)
    back = backward(3, lists, values, other, back)
    back = col_exchange(back)
    for bit in (4, 8):
        total = total + partner(total, "row", 16, bit)
    scale = 1.0 / math.sqrt(4 * TILE * 128)
    weight_grad = total[:FEAT] * scale
    bias_grad = total[FEAT] * scale
    back, weight_grad, bias_grad = order((back, weight_grad, bias_grad))
    feature_grad = last(back)
    return (hidden, feature_grad, weight_grad, bias_grad)


def solution(mesh):
    in_specs = (
        P(("row", "col"), None),
        P(),
        P(),
        P(("col", "row"), None),
        P("row", "col", None),
        P("row", "col", None),
        P("row", "col", None, None, None),
        P("row", "col"),
    )
    out_specs = (P(("col", "row"), None), P(("row", "col"), None), P(), P())
    return jax.shard_map(local, mesh=mesh, in_specs=in_specs, out_specs=out_specs, check_vma=False)
```

```python
import functools
import math

import jax
import jax.numpy as jnp
from jax import lax
from jax.experimental import pallas as pl
from jax.experimental.pallas import tpu as pltpu
from jax.sharding import PartitionSpec as P

gelu_coef = 0.7978845608
cube_coef = 0.044715
TILE = 256
FEAT = 128
SLOTS = 128
NPEER = 8
LIST = 160
UNROLL = 8
DEPTH = 32
FWD_DUMMY = 32
BWD_DUMMY = 32
f32, bf16 = jnp.float32, jnp.bfloat16
VMEM_LIMIT = 28 * 2**20


def params():
    return pltpu.CompilerParams(vmem_limit_bytes=VMEM_LIMIT)


def vmem():
    return pl.BlockSpec(memory_space=pltpu.VMEM)


def smem():
    return pl.BlockSpec(memory_space=pltpu.SMEM)


def hbm():
    return pl.BlockSpec(memory_space=pl.ANY)


def prep_kernel(where_ref, out_ref, in_ref, count_ref, lists_ref):
    core = where_ref[0]

    def clear(i, carry):
        lists_ref[i] = FWD_DUMMY << 16
        lists_ref[LIST + i] = FWD_DUMMY << 16
        lists_ref[2 * LIST + i] = BWD_DUMMY << 16
        lists_ref[3 * LIST + i] = BWD_DUMMY << 16
        return carry

    lax.fori_loop(0, LIST, clear, 0)

    def place(k, carry):
        f0, f1 = carry
        t = out_ref[k]
        s = in_ref[k]
        rel = jnp.bitwise_xor((t >> 2) & 1, core)
        to_t = ((t >> 3) << 2) | (t & 3)
        at_f = jnp.where(rel == 0, f0, LIST + f1)
        lists_ref[at_f] = k | (s << 8) | (to_t << 16)
        lists_ref[2 * LIST + at_f] = k | (to_t << 8) | (s << 16)
        return (f0 + 1 - rel, f1 + rel)

    zero = jnp.int32(0)
    sizes = lax.fori_loop(0, count_ref[0], place, (zero, zero))
    lists_ref[4 * LIST] = sizes[0]
    lists_ref[4 * LIST + 1] = sizes[1]


def prep(where, out_index, in_index, count):
    return pl.pallas_call(
        prep_kernel,
        out_shape=pltpu.SMEM((1024,), jnp.int32),
        in_specs=[smem()] * 4,
        out_specs=smem(),
        compiler_params=params(),
        name="slot_lists",
    )(where, out_index, in_index, count)


def copies_kernel(value_ref, out_ref, held, in_sem, sems):
    fetch = pltpu.make_async_copy(value_ref, held, in_sem)
    fetch.start()
    fetch.wait()
    copies = [pltpu.make_async_copy(held, out_ref.at[peer], sems.at[peer]) for peer in range(NPEER)]
    for copy in copies:
        copy.start()
    for copy in copies:
        copy.wait()


def copies_of(value):
    return pl.pallas_call(
        copies_kernel,
        out_shape=pltpu.HBM((NPEER, *value.shape), value.dtype),
        in_specs=[hbm()],
        out_specs=hbm(),
        scratch_shapes=[
            pltpu.VMEM(value.shape, value.dtype),
            pltpu.SemaphoreType.DMA,
            pltpu.SemaphoreType.DMA((NPEER,)),
        ],
        compiler_params=params(),
        name="copies",
    )(in_hbm(value))


def tile_loop(which, lists_ref, vals, buf, sems, acc, ready, product):
    base = which * LIST
    groups = (lists_ref[4 * LIST + (which & 1)] + (UNROLL - 1)) // UNROLL
    ahead = DEPTH // UNROLL

    def copy(g, u):
        slot = lists_ref[base + g * UNROLL + u] & 255
        at = lax.rem(g, ahead) * UNROLL + u
        return pltpu.make_async_copy(vals.at[slot], buf.at[at], sems.at[at])

    for g in range(ahead):

        @pl.when(g < groups)
        def _():
            for u in range(UNROLL):
                copy(g, u).start()

    ready()

    def body(g, carry):
        for u in range(UNROLL):
            copy(g, u).wait()
        todo = []
        for u in range(UNROLL):
            entry = lists_ref[base + g * UNROLL + u]
            at = lax.rem(g, ahead) * UNROLL + u
            todo.append((entry >> 16, product(buf[at], (entry >> 8) & 255)))
        for to, value in todo:
            acc[to] += value

        @pl.when(g + ahead < groups)
        def _():
            for u in range(UNROLL):
                copy(g + ahead, u).start()

        return carry

    lax.fori_loop(0, groups, body, 0)


def in_smem(array):
    return pltpu.with_memory_space_constraint(array, pltpu.SMEM)


def in_hbm(array):
    return pltpu.with_memory_space_constraint(array, pltpu.HBM)


TILES_COST = pl.CostEstimate(
    flops=2 * 64 * TILE * TILE * FEAT, bytes_accessed=16 * 2**20, transcendentals=0
)


def forward_kernel(which, lists_ref, vals, x, out_ref, buf, acc, sems):
    def ready():
        def clear(i, carry):
            acc[i] = jnp.zeros((TILE, FEAT), f32)
            return carry

        lax.fori_loop(0, FWD_DUMMY, clear, 0)

    def product(tile, source):
        rows = pl.ds(pl.multiple_of((source & 3) * TILE, TILE), TILE)
        return jnp.dot(tile, x[source >> 2, rows, :], preferred_element_type=f32)

    tile_loop(which, lists_ref, vals, buf, sems, acc, ready, product)

    for i in range(4 * NPEER):
        out_ref[i // 4, pl.ds((i % 4) * TILE, TILE), :] = acc[i].astype(bf16)


def forward(which, lists, values, sources):
    return pl.pallas_call(
        functools.partial(forward_kernel, which),
        out_shape=jax.ShapeDtypeStruct((NPEER, 4 * TILE, FEAT), bf16),
        in_specs=[smem(), hbm(), vmem()],
        out_specs=vmem(),
        scratch_shapes=[
            pltpu.VMEM((DEPTH, TILE, TILE), bf16),
            pltpu.VMEM((FWD_DUMMY + 1, TILE, FEAT), f32),
            pltpu.SemaphoreType.DMA((DEPTH,)),
        ],
        compiler_params=params(),
        cost_estimate=TILES_COST,
        name="forward_tiles",
    )(in_smem(lists), in_hbm(values), sources)


def pair_sum_kernel(mine_ref, other_ref, out_ref):
    for k in range(NPEER):
        out_ref[k] = (mine_ref[k].astype(f32) + other_ref[k].astype(f32)).astype(bf16)


def pair_sum(mine, other):
    return pl.pallas_call(
        pair_sum_kernel,
        out_shape=jax.ShapeDtypeStruct(mine.shape, bf16),
        in_specs=[vmem()] * 2,
        out_specs=vmem(),
        compiler_params=params(),
        cost_estimate=pl.CostEstimate(flops=2**21, bytes_accessed=6 * 2**20, transcendentals=0),
        name="pair_sum",
    )(mine, other)


def backward_kernel(which, lists_ref, vals, g, *rest):
    if which == 2:
        out, buf, acc, sems = rest
    else:
        before, out_ref, buf, acc, sems, out, out_sems = rest

    def ready():
        def clear(i, carry):
            acc[i] = jnp.zeros((FEAT, TILE), f32)
            return carry

        lax.fori_loop(0, BWD_DUMMY, clear, 0)

    def product(tile, source):
        rows = pl.ds(pl.multiple_of((source & 3) * FEAT, FEAT), FEAT)
        return jnp.dot(g[source >> 2, rows, :], tile, preferred_element_type=f32)

    tile_loop(which, lists_ref, vals, buf, sems, acc, ready, product)

    copies = []
    for i in range(4 * NPEER):
        peer, rows = i // 4, pl.ds((i % 4) * FEAT, FEAT)
        if which == 2:
            out[peer, rows, :] = acc[i].astype(bf16)
        else:
            out[peer, rows, :] = (acc[i] + before[peer, rows, :].astype(f32)).astype(bf16)
            if i % 4 == 3:
                copies.append(
                    pltpu.make_async_copy(out.at[peer], out_ref.at[peer], out_sems.at[peer])
                )
                copies[-1].start()
    for copy in copies:
        copy.wait()


def backward(which, lists, values, *blocks):
    shape = (NPEER, 4 * FEAT, TILE)
    scratch = [
        pltpu.VMEM((DEPTH, TILE, TILE), bf16),
        pltpu.VMEM((BWD_DUMMY + 1, FEAT, TILE), f32),
        pltpu.SemaphoreType.DMA((DEPTH,)),
    ]
    if which == 3:
        scratch += [pltpu.VMEM(shape, bf16), pltpu.SemaphoreType.DMA((NPEER,))]
    return pl.pallas_call(
        functools.partial(backward_kernel, which),
        out_shape=jax.ShapeDtypeStruct(shape, bf16) if which == 2 else pltpu.HBM(shape, bf16),
        in_specs=[smem(), hbm()] + [vmem()] * len(blocks),
        out_specs=vmem() if which == 2 else hbm(),
        scratch_shapes=scratch,
        compiler_params=params(),
        cost_estimate=TILES_COST,
        name="backward_tiles",
    )(in_smem(lists), in_hbm(values), *blocks)


def dense_kernel(
    recv_ref, weight_ref, bias_ref, cot_ref, hidden_ref, grad_ref, wsum_ref, one, sems
):
    copies = []
    weight = weight_ref[...]
    for part in range(4):
        here = pl.ds(part * TILE, TILE)
        total = recv_ref[0, here, :].astype(f32)
        for peer in range(1, NPEER):
            total += recv_ref[peer, here, :].astype(f32)
        agg = total.astype(bf16)
        v = jnp.dot(agg, weight, preferred_element_type=f32) + bias_ref[...]
        s = jnp.tanh(gelu_coef * (v + cube_coef * v * v * v))
        hidden_ref[here, :] = (0.5 * v * (1.0 + s)).astype(bf16)
        slope = 0.5 * (1.0 + s) + 0.5 * v * (1.0 - s * s) * gelu_coef * (
            1.0 + 3.0 * cube_coef * v * v
        )
        grad = (cot_ref[here, :].astype(f32) * slope).astype(bf16)
        wsum = lax.dot_general(agg, grad, (((0,), (0,)), ((), ())), preferred_element_type=f32)
        bsum = jnp.dot(jnp.ones((16, TILE), bf16), grad, preferred_element_type=f32)[:8]
        back = lax.dot_general(weight, grad, (((1,), (1,)), ((), ())), preferred_element_type=f32)
        back = back.astype(bf16)
        rows = pl.ds(part * FEAT, FEAT)
        one[rows, :] = back
        for peer in range(NPEER):
            copies.append(
                pltpu.make_async_copy(
                    one.at[rows], grad_ref.at[peer, rows], sems.at[part * NPEER + peer]
                )
            )
            copies[-1].start()
        if part == 0:
            wsum_ref[pl.ds(0, FEAT), :] = wsum
            wsum_ref[pl.ds(FEAT, 8), :] = bsum
        else:
            wsum_ref[pl.ds(0, FEAT), :] += wsum
            wsum_ref[pl.ds(FEAT, 8), :] += bsum
    for copy in copies:
        copy.wait()


def dense(recv, weight, bias, cotangent):
    return pl.pallas_call(
        dense_kernel,
        out_shape=(
            jax.ShapeDtypeStruct((4 * TILE, FEAT), bf16),
            pltpu.HBM((NPEER, 4 * FEAT, TILE), bf16),
            jax.ShapeDtypeStruct((FEAT + 8, FEAT), f32),
        ),
        in_specs=[vmem()] * 4,
        out_specs=(vmem(), hbm(), vmem()),
        scratch_shapes=[
            pltpu.VMEM((4 * FEAT, TILE), bf16),
            pltpu.SemaphoreType.DMA((4 * NPEER,)),
        ],
        compiler_params=params(),
        cost_estimate=pl.CostEstimate(
            flops=6 * 1024 * FEAT * FEAT, bytes_accessed=5 * 2**20, transcendentals=1024 * FEAT
        ),
        name="dense_layer",
    )(recv, weight, bias, cotangent)


def last_kernel(recv_ref, grad_ref):
    for sub in range(4):
        rows = pl.ds(sub * FEAT, FEAT)
        total = recv_ref[0, rows, :].astype(f32)
        for peer in range(1, NPEER):
            total += recv_ref[peer, rows, :].astype(f32)
        grad_ref[pl.ds(sub * TILE, TILE), :] = total.T.astype(bf16)


def last(recv):
    return pl.pallas_call(
        last_kernel,
        out_shape=jax.ShapeDtypeStruct((4 * TILE, FEAT), bf16),
        in_specs=[vmem()],
        out_specs=vmem(),
        compiler_params=params(),
        cost_estimate=pl.CostEstimate(flops=2**20, bytes_accessed=3 * 2**20, transcendentals=0),
        name="last_sum",
    )(recv)


SAME_CORE = [[2 * j + core for j in range(NPEER)] for core in range(2)]
OTHER_CORE = [(r, r ^ 1) for r in range(16)]


def to_other_core(value):
    return lax.ppermute(value, "row", OTHER_CORE)


def row_exchange(value):
    return lax.all_to_all(value, "row", 0, 0, axis_index_groups=SAME_CORE)


def col_exchange(value):
    return lax.all_to_all(value, "col", 0, 0)


def partner(value, axis, size, bit):
    return lax.ppermute(value, axis, [(i, i ^ bit) for i in range(size)])


def local(features, weight, layer_bias, cotangent, tile_out, tile_in, tile_vals, tile_count):
    values = tile_vals[0, 0]
    where = (lax.axis_index("row") & 1).astype(jnp.int32).reshape(1)
    lists = prep(where, tile_out[0, 0], tile_in[0, 0], tile_count[0])
    bias = layer_bias.reshape(1, FEAT)
    order = lax.optimization_barrier

    sources = col_exchange(copies_of(features))
    other = forward(1, lists, values, sources)
    other, lists = order((other, lists))
    mine = forward(0, lists, values, sources)
    recv = row_exchange(pair_sum(mine, to_other_core(other)))
    hidden, grad, total = dense(recv, weight, bias, cotangent)

    grads = row_exchange(grad)
    one, two, three = (partner(total, "col", 8, bit) for bit in (2, 4, 6))
    total = (total + one) + (two + three)
    total = total + partner(total, "row", 16, 1)
    both = [(r * 8 + c, (r ^ 2) * 8 + (c ^ 1)) for r in range(16) for c in range(8)]
    near, far = partner(total, "col", 8, 1), partner(total, "row", 16, 2)
    total = (total + near) + (far + lax.ppermute(total, ("row", "col"), both))
    grads, total = order((grads, total))
    other = to_other_core(grads)
    back = backward(2, lists, values, grads)
    back = backward(3, lists, values, other, back)
    back = col_exchange(back)
    for bit in (4, 8):
        total = total + partner(total, "row", 16, bit)
    scale = 1.0 / math.sqrt(4 * TILE * 128)
    weight_grad = total[:FEAT] * scale
    bias_grad = total[FEAT] * scale
    back, weight_grad, bias_grad = order((back, weight_grad, bias_grad))
    feature_grad = last(back)
    return (hidden, feature_grad, weight_grad, bias_grad)


def solution(mesh):
    in_specs = (
        P(("row", "col"), None),
        P(),
        P(),
        P(("col", "row"), None),
        P("row", "col", None),
        P("row", "col", None),
        P("row", "col", None, None, None),
        P("row", "col"),
    )
    out_specs = (P(("col", "row"), None), P(("row", "col"), None), P(), P())
    return jax.shard_map(local, mesh=mesh, in_specs=in_specs, out_specs=out_specs, check_vma=False)
```

```python
import functools
import math

import jax
import jax.numpy as jnp
from jax import lax
from jax.experimental import pallas as pl
from jax.experimental.pallas import tpu as pltpu
from jax.sharding import PartitionSpec as P

gelu_coef = 0.7978845608
cube_coef = 0.044715
TILE = 256
FEAT = 128
SLOTS = 128
NPEER = 8
LIST = 160
UNROLL = 8
DEPTH = 32
FWD_DUMMY = 32
BWD_DUMMY = 32
f32, bf16 = jnp.float32, jnp.bfloat16
VMEM_LIMIT = 28 * 2**20


def params():
    return pltpu.CompilerParams(vmem_limit_bytes=VMEM_LIMIT)


def vmem():
    return pl.BlockSpec(memory_space=pltpu.VMEM)


def smem():
    return pl.BlockSpec(memory_space=pltpu.SMEM)


def hbm():
    return pl.BlockSpec(memory_space=pl.ANY)


def prep_kernel(where_ref, out_ref, in_ref, count_ref, lists_ref):
    core = where_ref[0]

    def clear(i, carry):
        lists_ref[i] = FWD_DUMMY << 16
        lists_ref[LIST + i] = FWD_DUMMY << 16
        lists_ref[2 * LIST + i] = BWD_DUMMY << 16
        lists_ref[3 * LIST + i] = BWD_DUMMY << 16
        return carry

    lax.fori_loop(0, LIST, clear, 0)

    def place(k, carry):
        f0, f1 = carry
        t = out_ref[k]
        s = in_ref[k]
        rel = jnp.bitwise_xor((t >> 2) & 1, core)
        to_t = ((t >> 3) << 2) | (t & 3)
        at_f = jnp.where(rel == 0, f0, LIST + f1)
        lists_ref[at_f] = k | (s << 8) | (to_t << 16)
        lists_ref[2 * LIST + at_f] = k | (to_t << 8) | (s << 16)
        return (f0 + 1 - rel, f1 + rel)

    zero = jnp.int32(0)
    sizes = lax.fori_loop(0, count_ref[0], place, (zero, zero))
    lists_ref[4 * LIST] = sizes[0]
    lists_ref[4 * LIST + 1] = sizes[1]


def prep(where, out_index, in_index, count):
    return pl.pallas_call(
        prep_kernel,
        out_shape=pltpu.SMEM((1024,), jnp.int32),
        in_specs=[smem()] * 4,
        out_specs=smem(),
        compiler_params=params(),
        name="slot_lists",
    )(where, out_index, in_index, count)


def copies_kernel(value_ref, out_ref, held, in_sem, sems):
    fetch = pltpu.make_async_copy(value_ref, held, in_sem)
    fetch.start()
    fetch.wait()
    copies = [pltpu.make_async_copy(held, out_ref.at[peer], sems.at[peer]) for peer in range(NPEER)]
    for copy in copies:
        copy.start()
    for copy in copies:
        copy.wait()


def copies_of(value):
    return pl.pallas_call(
        copies_kernel,
        out_shape=pltpu.HBM((NPEER, *value.shape), value.dtype),
        in_specs=[hbm()],
        out_specs=hbm(),
        scratch_shapes=[
            pltpu.VMEM(value.shape, value.dtype),
            pltpu.SemaphoreType.DMA,
            pltpu.SemaphoreType.DMA((NPEER,)),
        ],
        compiler_params=params(),
        name="copies",
    )(in_hbm(value))


def tile_loop(which, lists_ref, vals, buf, sems, acc, ready, product):
    base = which * LIST
    groups = (lists_ref[4 * LIST + (which & 1)] + (UNROLL - 1)) // UNROLL
    ahead = DEPTH // UNROLL

    def copy(g, u):
        slot = lists_ref[base + g * UNROLL + u] & 255
        at = lax.rem(g, ahead) * UNROLL + u
        return pltpu.make_async_copy(vals.at[slot], buf.at[at], sems.at[at])

    for g in range(ahead):

        @pl.when(g < groups)
        def _():
            for u in range(UNROLL):
                copy(g, u).start()

    ready()

    def body(g, carry):
        for u in range(UNROLL):
            copy(g, u).wait()
        todo = []
        for u in range(UNROLL):
            entry = lists_ref[base + g * UNROLL + u]
            at = lax.rem(g, ahead) * UNROLL + u
            todo.append((entry >> 16, product(buf[at], (entry >> 8) & 255)))
        for to, value in todo:
            acc[to] += value

        @pl.when(g + ahead < groups)
        def _():
            for u in range(UNROLL):
                copy(g + ahead, u).start()

        return carry

    lax.fori_loop(0, groups, body, 0)


def in_smem(array):
    return pltpu.with_memory_space_constraint(array, pltpu.SMEM)


def in_hbm(array):
    return pltpu.with_memory_space_constraint(array, pltpu.HBM)


TILES_COST = pl.CostEstimate(
    flops=2 * 64 * TILE * TILE * FEAT, bytes_accessed=16 * 2**20, transcendentals=0
)


def forward_kernel(which, lists_ref, vals, x, out_ref, buf, acc, sems):
    def ready():
        def clear(i, carry):
            acc[i] = jnp.zeros((TILE, FEAT), f32)
            return carry

        lax.fori_loop(0, FWD_DUMMY, clear, 0)

    def product(tile, source):
        rows = pl.ds(pl.multiple_of((source & 3) * TILE, TILE), TILE)
        return jnp.dot(tile, x[source >> 2, rows, :], preferred_element_type=f32)

    tile_loop(which, lists_ref, vals, buf, sems, acc, ready, product)

    for i in range(4 * NPEER):
        out_ref[i // 4, pl.ds((i % 4) * TILE, TILE), :] = acc[i].astype(bf16)


def forward(which, lists, values, sources):
    return pl.pallas_call(
        functools.partial(forward_kernel, which),
        out_shape=jax.ShapeDtypeStruct((NPEER, 4 * TILE, FEAT), bf16),
        in_specs=[smem(), hbm(), vmem()],
        out_specs=vmem(),
        scratch_shapes=[
            pltpu.VMEM((DEPTH, TILE, TILE), bf16),
            pltpu.VMEM((FWD_DUMMY + 1, TILE, FEAT), f32),
            pltpu.SemaphoreType.DMA((DEPTH,)),
        ],
        compiler_params=params(),
        cost_estimate=TILES_COST,
        name="forward_tiles",
    )(in_smem(lists), in_hbm(values), sources)


def pair_sum_kernel(mine_ref, other_ref, out_ref):
    for k in range(NPEER):
        out_ref[k] = (mine_ref[k].astype(f32) + other_ref[k].astype(f32)).astype(bf16)


def pair_sum(mine, other):
    return pl.pallas_call(
        pair_sum_kernel,
        out_shape=jax.ShapeDtypeStruct(mine.shape, bf16),
        in_specs=[vmem()] * 2,
        out_specs=vmem(),
        compiler_params=params(),
        cost_estimate=pl.CostEstimate(flops=2**21, bytes_accessed=6 * 2**20, transcendentals=0),
        name="pair_sum",
    )(mine, other)


def backward_kernel(which, lists_ref, vals, g, *rest):
    if which == 2:
        out, buf, acc, sems = rest
    else:
        before, out_ref, buf, acc, sems, out, out_sems = rest

    def ready():
        def clear(i, carry):
            acc[i] = jnp.zeros((FEAT, TILE), f32)
            return carry

        lax.fori_loop(0, BWD_DUMMY, clear, 0)

    def product(tile, source):
        rows = pl.ds(pl.multiple_of((source & 3) * FEAT, FEAT), FEAT)
        return jnp.dot(g[source >> 2, rows, :], tile, preferred_element_type=f32)

    tile_loop(which, lists_ref, vals, buf, sems, acc, ready, product)

    copies = []
    for i in range(4 * NPEER):
        peer, rows = i // 4, pl.ds((i % 4) * FEAT, FEAT)
        if which == 2:
            out[peer, rows, :] = acc[i].astype(bf16)
        else:
            out[peer, rows, :] = (acc[i] + before[peer, rows, :].astype(f32)).astype(bf16)
            if i % 4 == 3:
                copies.append(
                    pltpu.make_async_copy(out.at[peer], out_ref.at[peer], out_sems.at[peer])
                )
                copies[-1].start()
    for copy in copies:
        copy.wait()


def backward(which, lists, values, *blocks):
    shape = (NPEER, 4 * FEAT, TILE)
    scratch = [
        pltpu.VMEM((DEPTH, TILE, TILE), bf16),
        pltpu.VMEM((BWD_DUMMY + 1, FEAT, TILE), f32),
        pltpu.SemaphoreType.DMA((DEPTH,)),
    ]
    if which == 3:
        scratch += [pltpu.VMEM(shape, bf16), pltpu.SemaphoreType.DMA((NPEER,))]
    return pl.pallas_call(
        functools.partial(backward_kernel, which),
        out_shape=jax.ShapeDtypeStruct(shape, bf16) if which == 2 else pltpu.HBM(shape, bf16),
        in_specs=[smem(), hbm()] + [vmem()] * len(blocks),
        out_specs=vmem() if which == 2 else hbm(),
        scratch_shapes=scratch,
        compiler_params=params(),
        cost_estimate=TILES_COST,
        name="backward_tiles",
    )(in_smem(lists), in_hbm(values), *blocks)


def dense_kernel(
    recv_ref, weight_ref, bias_ref, cot_ref, hidden_ref, grad_ref, wsum_ref, one, sems
):
    copies = []
    weight = weight_ref[...]
    for part in range(4):
        here = pl.ds(part * TILE, TILE)
        total = recv_ref[0, here, :].astype(f32)
        for peer in range(1, NPEER):
            total += recv_ref[peer, here, :].astype(f32)
        agg = total.astype(bf16)
        v = jnp.dot(agg, weight, preferred_element_type=f32) + bias_ref[...]
        s = jnp.tanh(gelu_coef * (v + cube_coef * v * v * v))
        hidden_ref[here, :] = (0.5 * v * (1.0 + s)).astype(bf16)
        slope = 0.5 * (1.0 + s) + 0.5 * v * (1.0 - s * s) * gelu_coef * (
            1.0 + 3.0 * cube_coef * v * v
        )
        grad = (cot_ref[here, :].astype(f32) * slope).astype(bf16)
        wsum = lax.dot_general(agg, grad, (((0,), (0,)), ((), ())), preferred_element_type=f32)
        bsum = jnp.dot(jnp.ones((16, TILE), bf16), grad, preferred_element_type=f32)[:8]
        back = lax.dot_general(weight, grad, (((1,), (1,)), ((), ())), preferred_element_type=f32)
        back = back.astype(bf16)
        rows = pl.ds(part * FEAT, FEAT)
        one[rows, :] = back
        for peer in range(NPEER):
            copies.append(
                pltpu.make_async_copy(
                    one.at[rows], grad_ref.at[peer, rows], sems.at[part * NPEER + peer]
                )
            )
            copies[-1].start()
        if part == 0:
            wsum_ref[pl.ds(0, FEAT), :] = wsum
            wsum_ref[pl.ds(FEAT, 8), :] = bsum
        else:
            wsum_ref[pl.ds(0, FEAT), :] += wsum
            wsum_ref[pl.ds(FEAT, 8), :] += bsum
    for copy in copies:
        copy.wait()


def dense(recv, weight, bias, cotangent):
    return pl.pallas_call(
        dense_kernel,
        out_shape=(
            jax.ShapeDtypeStruct((4 * TILE, FEAT), bf16),
            pltpu.HBM((NPEER, 4 * FEAT, TILE), bf16),
            jax.ShapeDtypeStruct((FEAT + 8, FEAT), f32),
        ),
        in_specs=[vmem()] * 4,
        out_specs=(vmem(), hbm(), vmem()),
        scratch_shapes=[
            pltpu.VMEM((4 * FEAT, TILE), bf16),
            pltpu.SemaphoreType.DMA((4 * NPEER,)),
        ],
        compiler_params=params(),
        cost_estimate=pl.CostEstimate(
            flops=6 * 1024 * FEAT * FEAT, bytes_accessed=5 * 2**20, transcendentals=1024 * FEAT
        ),
        name="dense_layer",
    )(recv, weight, bias, cotangent)


def last_kernel(recv_ref, grad_ref):
    for sub in range(4):
        rows = pl.ds(sub * FEAT, FEAT)
        total = recv_ref[0, rows, :].astype(f32)
        for peer in range(1, NPEER):
            total += recv_ref[peer, rows, :].astype(f32)
        grad_ref[pl.ds(sub * TILE, TILE), :] = total.T.astype(bf16)


def last(recv):
    return pl.pallas_call(
        last_kernel,
        out_shape=jax.ShapeDtypeStruct((4 * TILE, FEAT), bf16),
        in_specs=[vmem()],
        out_specs=vmem(),
        compiler_params=params(),
        cost_estimate=pl.CostEstimate(flops=2**20, bytes_accessed=3 * 2**20, transcendentals=0),
        name="last_sum",
    )(recv)


SAME_CORE = [[2 * j + core for j in range(NPEER)] for core in range(2)]
OTHER_CORE = [(r, r ^ 1) for r in range(16)]


def to_other_core(value):
    return lax.ppermute(value, "row", OTHER_CORE)


def row_exchange(value):
    return lax.all_to_all(value, "row", 0, 0, axis_index_groups=SAME_CORE)


def col_exchange(value):
    return lax.all_to_all(value, "col", 0, 0)


def partner(value, axis, size, bit):
    return lax.ppermute(value, axis, [(i, i ^ bit) for i in range(size)])


def local(features, weight, layer_bias, cotangent, tile_out, tile_in, tile_vals, tile_count):
    values = tile_vals[0, 0]
    where = (lax.axis_index("row") & 1).astype(jnp.int32).reshape(1)
    lists = prep(where, tile_out[0, 0], tile_in[0, 0], tile_count[0])
    bias = layer_bias.reshape(1, FEAT)
    order = lax.optimization_barrier

    sources = col_exchange(copies_of(features))
    other = forward(1, lists, values, sources)
    other, lists = order((other, lists))
    mine = forward(0, lists, values, sources)
    recv = row_exchange(pair_sum(mine, to_other_core(other)))
    hidden, grad, total = dense(recv, weight, bias, cotangent)

    grads = row_exchange(grad)
    one, two, three = (partner(total, "col", 8, bit) for bit in (2, 4, 6))
    total = (total + one) + (two + three)
    total = total + partner(total, "row", 16, 1)
    both = [(r * 8 + c, (r ^ 2) * 8 + (c ^ 1)) for r in range(16) for c in range(8)]
    near, far = partner(total, "col", 8, 1), partner(total, "row", 16, 2)
    total = (total + near) + (far + lax.ppermute(total, ("row", "col"), both))
    other = to_other_core(grads)
    back = backward(2, lists, values, grads)
    back = backward(3, lists, values, other, back)
    back = col_exchange(back)
    for bit in (4, 8):
        total = total + partner(total, "row", 16, bit)
    scale = 1.0 / math.sqrt(4 * TILE * 128)
    weight_grad = total[:FEAT] * scale
    bias_grad = total[FEAT] * scale
    back, weight_grad, bias_grad = order((back, weight_grad, bias_grad))
    feature_grad = last(back)
    return (hidden, feature_grad, weight_grad, bias_grad)


def solution(mesh):
    in_specs = (
        P(("row", "col"), None),
        P(),
        P(),
        P(("col", "row"), None),
        P("row", "col", None),
        P("row", "col", None),
        P("row", "col", None, None, None),
        P("row", "col"),
    )
    out_specs = (P(("col", "row"), None), P(("row", "col"), None), P(), P())
    return jax.shard_map(local, mesh=mesh, in_specs=in_specs, out_specs=out_specs, check_vma=False)
```
